32 devices in a mesh: grp: 2 (over y), wide: 16 (over z, x, core).
Axes of the slice: x: 2, y: 2, z: 4, core: 2. Of those that a mesh axis runs over, the one named last changes fastest.
Arguments:
- source_points: bfloat16 [64, 12288], P(None, ('grp', 'wide')), parts along dimension 1, may hold values from -25 to 25
- target_points: bfloat16 [64, 4096], P(None, ('grp', 'wide')), parts along dimension 1, may hold values from -25 to 25
- source_logw: bfloat16 [12288], P(('grp', 'wide')), parts along dimension 0, may hold values from -1 to 1
- target_logw: bfloat16 [4096], P(('grp', 'wide')), parts along dimension 0, may hold values from -1 to 1
- inverse_eps: float32 [1], replicated, may hold values from 0.08 to 0.12
Outputs:
- mapped: float32 [64, 12288], P(None, ('grp', 'wide')), parts along dimension 1
- target_potential: float32 [4096], P(('grp', 'wide')), parts along dimension 0
The draws below stay inside these ranges and needn't reach their ends.
There are 2 independent parts, one for each index of `grp`. The reference program is written for one: setup_inputs(seed, part) draws one part's arguments, and reference() takes and returns one part's arrays. A program takes and returns all parts, laid end to end along the dimension named above; an argument that names none is the same for every part. Nothing has to cross between parts.
All inputs are finite; a program needn't handle non-finite values.
Results may differ from the reference program's by a relative error of at most 0.0024.
Values may be sent and summed in bfloat16 or wider, within the bound.
No kernel may reach another device: no remote copies, remote signals or barrier semaphores. Data moves between devices by JAX's collectives and lax.ppermute only.
A program may use at most 64 MiB of HBM per device.

```python
import math
import jax
import jax.numpy as jnp
from jax import lax

FEAT = 64
ITERS = 2
SRC = 6144
TGT = 2048


def draw_source_points(key, part):
    key = jax.random.fold_in(key, 11)
    sample = jnp.clip(jax.random.normal(key, (FEAT, SRC), jnp.float32), -6.0, 6.0)
    return sample.astype(jnp.bfloat16)


def draw_target_points(key, part):
    key = jax.random.fold_in(key, 12)
    sample = jnp.clip(jax.random.normal(key, (FEAT, TGT), jnp.float32), -6.0, 6.0)
    return sample.astype(jnp.bfloat16)


def block_scale(rng, shape, shards, smallest, high):
    loudness, own = 1.0, jax.random.fold_in(rng, 6)
    for dim, shards_of in shards:
        draws = jnp.exp(jax.random.uniform(jax.random.fold_in(own, dim), (shards_of,), jnp.float32, smallest / len(shards), high / len(shards)))
        loudness = loudness * jnp.repeat(draws, shape[dim] // shards_of).reshape([-1 if axis == dim else 1 for axis in range(len(shape))])
    return loudness


def setup_inputs(seed: int = 0, part: int = 0) -> dict:
    key_of = jax.random.split(jax.random.key(seed), 6)
    part_splits = jax.random.split(jax.random.fold_in(key_of[5], part), 6)
    source_points = draw_source_points(jax.random.fold_in(jax.random.fold_in(key_of[5], part), 71), part)
    target_points = draw_target_points(jax.random.fold_in(jax.random.fold_in(key_of[5], part), 71), part)
    source_logw = jnp.clip(jax.random.uniform(part_splits[2], (SRC,), jnp.float32, -1.0, 1.0) * block_scale(part_splits[2], (SRC,), ((0, 16),), -0.4, 0.0), -1.0, 1.0).astype(jnp.bfloat16)
    target_logw = jnp.clip(jax.random.uniform(part_splits[3], (TGT,), jnp.float32, -1.0, 1.0) * block_scale(part_splits[3], (TGT,), ((0, 16),), -0.4, 0.0), -1.0, 1.0).astype(jnp.bfloat16)
    inverse_eps = jnp.clip(jax.random.uniform(key_of[4], (1,), jnp.float32, 0.08, 0.12), 0.08, 0.12)
    return {"source_points": source_points, "target_points": target_points, "source_logw": source_logw, "target_logw": target_logw, "inverse_eps": inverse_eps}


def cost_scores(left, right, term, inverse):
    cross = lax.dot_general(left, right, (((0,), (0,)), ((), ())), preferred_element_type=jnp.float32)
    sq_left = jnp.sum(jnp.square(left.astype(jnp.float32)), axis=0)
    sq_right = jnp.sum(jnp.square(right.astype(jnp.float32)), axis=0)
    return term[None, :] - inverse * (sq_left[:, None] + sq_right[None, :] - 2.0 * cross)


def stable_lse(scores):
    peak = jnp.max(scores, axis=1)
    return peak + jnp.log(jnp.sum(jnp.exp(scores - peak[:, None]), axis=1))


def split_blocks(points):
    total = points.shape[1]
    width = math.gcd(total, 512)
    return points.reshape(points.shape[0], total // width, width).transpose(1, 0, 2)


def row_lse(left, right, term, inverse):
    return lax.map(lambda piece: stable_lse(cost_scores(piece, right, term, inverse)), split_blocks(left)).reshape(-1)


def mapped_points(left, right, term, inverse):
    def one_block(piece):
        scores = cost_scores(piece, right, term, inverse)
        weights = jnp.exp(scores - stable_lse(scores)[:, None]).astype(jnp.bfloat16)
        return lax.dot_general(weights, right, (((1,), (1,)), ((), ())), preferred_element_type=jnp.float32)

    moved = lax.map(one_block, split_blocks(left))
    return moved.reshape(-1, right.shape[0]).T


def reference(source_points, target_points, source_logw, target_logw, inverse_eps):
    inverse = inverse_eps[0]
    weight_a = source_logw.astype(jnp.float32)
    weight_b = target_logw.astype(jnp.float32)
    target_pot = jnp.zeros((target_points.shape[1],), jnp.float32)
    for iteration in range(ITERS):
        source_pot = -row_lse(source_points, target_points, target_pot + weight_b, inverse)
        target_pot = -row_lse(target_points, source_points, source_pot + weight_a, inverse)
    mapped = mapped_points(source_points, target_points, target_pot + weight_b, inverse)
    return mapped, target_pot
```

```python
import jax
import jax.numpy as jnp
from jax import lax
from jax.sharding import PartitionSpec as P

ITERS = 2
AXIS = "wide"


def sq_norms(points):
    return jnp.sum(jnp.square(points.astype(jnp.float32)), axis=0)


def digit_groups(count, widest):
    bits = count.bit_length() - 1
    groups, low = [], 0
    while low < bits:
        width = min(widest, bits - low)
        groups.append((low, width))
        low += width
    return groups


def lse_across(partial, count, widest):
    for low, width in digit_groups(count, widest):
        held = [partial]
        for digit in range(1, 1 << width):
            pairs = [(source, source ^ (digit << low)) for source in range(count)]
            held.append(lax.ppermute(partial, AXIS, pairs))
        stacked = jnp.stack(held)
        peak = jnp.max(stacked, axis=0)
        partial = peak + jnp.log(jnp.sum(jnp.exp(stacked - peak[None]), axis=0))
    return partial


def gather_targets(points, logw, count):
    feat, own = points.shape
    pad = -(feat + 1) % 16
    packed = jnp.concatenate(
        [points, logw[None, :], jnp.zeros((pad, own), points.dtype)], axis=0
    )
    spread = jnp.broadcast_to(packed[None], (count,) + packed.shape)
    every = lax.all_to_all(spread, AXIS, 0, 0, tiled=True)
    joined = every.transpose(1, 0, 2).reshape(packed.shape[0], count * own)
    return joined[:feat], joined[feat]


def on_device(source_points, target_points, source_logw, target_logw, inverse_eps, count):
    inverse = inverse_eps[0]
    own = target_points.shape[1]
    targets, logb = gather_targets(target_points, target_logw, count)
    weight_a = source_logw.astype(jnp.float32)
    weight_b = logb.astype(jnp.float32)
    cross = lax.dot_general(
        source_points, targets, (((0,), (0,)), ((), ())), preferred_element_type=jnp.float32
    )
    cost = inverse * (
        sq_norms(source_points)[:, None] + sq_norms(targets)[None, :] - 2.0 * cross
    )

    def row_lse(term):
        scores = term[None, :] - cost
        peak = jnp.max(scores, axis=1)
        return scores, peak + jnp.log(jnp.sum(jnp.exp(scores - peak[:, None]), axis=1))

    target_pot = jnp.zeros((targets.shape[1],), jnp.float32)
    for iteration in range(ITERS):
        source_pot = -row_lse(target_pot + weight_b)[1]
        scores = (source_pot + weight_a)[:, None] - cost
        peak = jnp.max(scores, axis=0)
        partial = peak + jnp.log(jnp.sum(jnp.exp(scores - peak[None, :]), axis=0))
        target_pot = -lse_across(partial, count, 4 if iteration == 0 else 1)
    scores, final_lse = row_lse(target_pot + weight_b)
    plan = jnp.exp(scores - final_lse[:, None]).astype(jnp.bfloat16)
    mapped = lax.dot_general(
        targets, plan, (((1,), (1,)), ((), ())), preferred_element_type=jnp.float32
    )
    own_pot = lax.dynamic_slice_in_dim(target_pot, lax.axis_index(AXIS) * own, own)
    return (mapped, own_pot)


def solution(mesh):
    count = mesh.shape[AXIS]
    placed = (
        P(None, ("grp", "wide")),
        P(None, ("grp", "wide")),
        P(("grp", "wide")),
        P(("grp", "wide")),
        P(),
    )

    def body(*blocks):
        return on_device(*blocks, count)

    return jax.shard_map(
        body,
        mesh=mesh,
        in_specs=placed,
        out_specs=(P(None, ("grp", "wide")), P(("grp", "wide"))),
        check_vma=False,
    )
```

```python
import jax
import jax.numpy as jnp
from jax import lax
from jax.sharding import PartitionSpec as P

ITERS = 2
AXIS = "wide"


def sq_norms(points):
    return jnp.sum(jnp.square(points.astype(jnp.float32)), axis=0)


def digit_stages(count):
    bits = count.bit_length() - 1
    stages, low = [], 0
    while low < bits:
        width = min(1 if low < 2 else 2, bits - low)
        stages.append((low, width))
        low += width
    return stages


def line_groups(count, low, width):
    span, mask = 1 << width, ((1 << width) - 1) << low
    bases = [index for index in range(count) if index & mask == 0]
    return [[base | (digit << low) for digit in range(span)] for base in bases]


def lse_staged(partial, count):
    for low, width in reversed(digit_stages(count)):
        stacked = lax.all_gather(
            partial, AXIS, axis_index_groups=line_groups(count, low, width)
        )
        peak = jnp.max(stacked, axis=0)
        partial = peak + jnp.log(jnp.sum(jnp.exp(stacked - peak[None]), axis=0))
    return partial


def lse_reduced(peak, total):
    highest = lax.pmax(peak, AXIS)
    return highest + jnp.log(lax.psum(total * jnp.exp(peak - highest), AXIS))


def gather_targets(points, logw, count):
    feat, own = points.shape
    pad = -(feat + 1) % 16
    packed = jnp.concatenate(
        [points, logw[None, :], jnp.zeros((pad, own), points.dtype)], axis=0
    )
    every = packed[None]
    for low, width in digit_stages(count):
        every = lax.all_gather(
            every, AXIS, axis_index_groups=line_groups(count, low, width), tiled=True
        )
    joined = every.transpose(1, 0, 2).reshape(packed.shape[0], count * own)
    return joined[:feat], joined[feat]


def on_device(source_points, target_points, source_logw, target_logw, inverse_eps, count):
    inverse = inverse_eps[0]
    own = target_points.shape[1]
    targets, logb = gather_targets(target_points, target_logw, count)
    weight_a = source_logw.astype(jnp.float32)
    weight_b = logb.astype(jnp.float32)
    cross = lax.dot_general(
        source_points, targets, (((0,), (0,)), ((), ())), preferred_element_type=jnp.float32
    )
    cost = inverse * (
        sq_norms(source_points)[:, None] + sq_norms(targets)[None, :] - 2.0 * cross
    )

    def row_lse(term):
        scores = term[None, :] - cost
        peak = jnp.max(scores, axis=1)
        return scores, peak + jnp.log(jnp.sum(jnp.exp(scores - peak[:, None]), axis=1))

    target_pot = jnp.zeros((targets.shape[1],), jnp.float32)
    for iteration in range(ITERS):
        source_pot = -row_lse(target_pot + weight_b)[1]
        scores = (source_pot + weight_a)[:, None] - cost
        peak = jnp.max(scores, axis=0)
        total = jnp.sum(jnp.exp(scores - peak[None, :]), axis=0)
        if iteration == 0:
            target_pot = -lse_staged(peak + jnp.log(total), count)
        else:
            target_pot = -lse_reduced(peak, total)
    scores, final_lse = row_lse(target_pot + weight_b)
    plan = jnp.exp(scores - final_lse[:, None]).astype(jnp.bfloat16)
    mapped = lax.dot_general(
        targets, plan, (((1,), (1,)), ((), ())), preferred_element_type=jnp.float32
    )
    own_pot = lax.dynamic_slice_in_dim(target_pot, lax.axis_index(AXIS) * own, own)
    return (mapped, own_pot)


def solution(mesh):
    count = mesh.shape[AXIS]
    placed = (
        P(None, ("grp", "wide")),
        P(None, ("grp", "wide")),
        P(("grp", "wide")),
        P(("grp", "wide")),
        P(),
    )

    def body(*blocks):
        return on_device(*blocks, count)

    return jax.shard_map(
        body,
        mesh=mesh,
        in_specs=placed,
        out_specs=(P(None, ("grp", "wide")), P(("grp", "wide"))),
        check_vma=False,
    )
```

```python
import jax
import jax.numpy as jnp
from jax import lax
from jax.sharding import PartitionSpec as P

ITERS = 2
AXIS = "wide"


def sq_norms(points):
    return jnp.sum(jnp.square(points.astype(jnp.float32)), axis=0)


def same_core(count):
    return [list(range(core, count, 2)) for core in range(2)]


def swap(value, count, step):
    return lax.ppermute(value, AXIS, [(source, source ^ step) for source in range(count)])


def join_lse(held):
    stacked = jnp.stack(held) if isinstance(held, list) else held
    peak = jnp.max(stacked, axis=0)
    return peak + jnp.log(jnp.sum(jnp.exp(stacked - peak[None]), axis=0))


def lse_spread(partial, count):
    partial = join_lse([partial, swap(partial, count, 1)])
    chips = count // 2
    spread = jnp.broadcast_to(partial[None], (chips,) + partial.shape)
    every = lax.all_to_all(
        spread, AXIS, 0, 0, axis_index_groups=same_core(count), tiled=True
    )
    return join_lse(every)


def lse_swapped(partial, count):
    bits = count.bit_length() - 1
    for low in range(min(2, bits)):
        partial = join_lse([partial, swap(partial, count, 1 << low)])
    low = 2
    while low < bits:
        width = min(2, bits - low)
        digits = range((1 << width) - 1, 0, -1)
        partial = join_lse([partial] + [swap(partial, count, digit << low) for digit in digits])
        low += width
    return partial


def gather_targets(points, logw, count):
    feat, own = points.shape
    pad = -(feat + 1) % 16
    packed = jnp.concatenate(
        [points, logw[None, :], jnp.zeros((pad, own), points.dtype)], axis=0
    )
    chips = count // 2
    spread = jnp.broadcast_to(packed[None], (chips,) + packed.shape)
    every = lax.all_to_all(
        spread, AXIS, 0, 0, axis_index_groups=same_core(count), tiled=True
    )
    other = swap(every, count, 1)
    first = lax.axis_index(AXIS) % 2 == 0
    pair = jnp.stack([jnp.where(first, every, other), jnp.where(first, other, every)], axis=1)
    joined = pair.reshape((count,) + packed.shape).transpose(1, 0, 2)
    joined = joined.reshape(packed.shape[0], count * own)
    return joined[:feat], joined[feat]


def on_device(source_points, target_points, source_logw, target_logw, inverse_eps, count):
    inverse = inverse_eps[0]
    own = target_points.shape[1]
    targets, logb = gather_targets(target_points, target_logw, count)
    weight_a = source_logw.astype(jnp.float32)
    weight_b = logb.astype(jnp.float32)
    cross = lax.dot_general(
        source_points, targets, (((0,), (0,)), ((), ())), preferred_element_type=jnp.float32
    )
    cost = inverse * (
        sq_norms(source_points)[:, None] + sq_norms(targets)[None, :] - 2.0 * cross
    )

    def row_lse(term):
        scores = term[None, :] - cost
        peak = jnp.max(scores, axis=1)
        return scores, peak + jnp.log(jnp.sum(jnp.exp(scores - peak[:, None]), axis=1))

    target_pot = jnp.zeros((targets.shape[1],), jnp.float32)
    for iteration in range(ITERS):
        source_pot = -row_lse(target_pot + weight_b)[1]
        scores = (source_pot + weight_a)[:, None] - cost
        peak = jnp.max(scores, axis=0)
        partial = peak + jnp.log(jnp.sum(jnp.exp(scores - peak[None, :]), axis=0))
        combine = lse_spread if iteration == 0 else lse_swapped
        target_pot = -combine(partial, count)
    scores, final_lse = row_lse(target_pot + weight_b)
    plan = jnp.exp(scores - final_lse[:, None]).astype(jnp.bfloat16)
    mapped = lax.dot_general(
        targets, plan, (((1,), (1,)), ((), ())), preferred_element_type=jnp.float32
    )
    own_pot = lax.dynamic_slice_in_dim(target_pot, lax.axis_index(AXIS) * own, own)
    return (mapped, own_pot)


def solution(mesh):
    count = mesh.shape[AXIS]
    placed = (
        P(None, ("grp", "wide")),
        P(None, ("grp", "wide")),
        P(("grp", "wide")),
        P(("grp", "wide")),
        P(),
    )

    def body(*blocks):
        return on_device(*blocks, count)

    return jax.shard_map(
        body,
        mesh=mesh,
        in_specs=placed,
        out_specs=(P(None, ("grp", "wide")), P(("grp", "wide"))),
        check_vma=False,
    )
```

```python
import functools
import math

import jax
import jax.numpy as jnp
from jax import lax
from jax.experimental import pallas as pl
from jax.experimental.pallas import tpu as pltpu
from jax.sharding import PartitionSpec as P

ITERS = 2
AXIS = "wide"
LOG2E = math.log2(math.e)
LANES = 128
ROWS = 128
DEPTH = 256
SMALL_ROW = 2.0**-64
SMALL_COL = 2.0**-32
LARGE_COL = 2.0**100
FLOOR = -1e30

EXTRA = 64


def three_terms(value):
    high = value.astype(jnp.bfloat16)
    rest = value - high.astype(jnp.float32)
    middle = rest.astype(jnp.bfloat16)
    low = (rest - middle.astype(jnp.float32)).astype(jnp.bfloat16)
    return high, middle, low


def pick_rows(shape, rows, rest):
    index = lax.broadcasted_iota(jnp.int32, shape, 0)
    out = jnp.full(shape, rest, jnp.float32)
    for place, row in enumerate(rows):
        out = jnp.where(index == place, row, out)
    return out


def stage_source(points, logw, scale):
    feat, count = points.shape
    wide = points.astype(jnp.float32)
    shift = scale * jnp.sum(wide * wide, axis=0, keepdims=True)
    shift = shift.astype(jnp.bfloat16).astype(jnp.float32)
    extras = pick_rows((LANES - feat, count), [1.0, 1.0, 1.0, -shift, logw], 0.0)
    turned = jnp.concatenate([wide, extras], axis=0).T
    lane = lax.broadcasted_iota(jnp.int32, turned.shape, 1)
    high, middle, low = three_terms(jnp.where(lane < feat, 2.0 * scale, 1.0) * turned)
    low = pltpu.roll(low.astype(jnp.float32), feat, 1)
    tail = jnp.where(lane < feat, middle.astype(jnp.float32), low).astype(jnp.bfloat16)
    return high, tail


def stage_targets(parts, previous, scale, taug, g_ref, q_ref, feat):
    place = 0
    for part in parts:
        for block in range(part.shape[0]):
            at = pl.ds(place * LANES, LANES)
            coords = part[block, :feat, :]
            wide = coords.astype(jnp.float32)
            q_ref[:, at] = scale * jnp.sum(wide * wide, axis=0, keepdims=True)
            logw = part[block, feat : feat + 16, :].astype(jnp.float32)[0:1]
            g_ref[:, at] = logw * LOG2E
            taug[0:feat, at] = coords
            taug[2 * feat : 3 * feat, at] = coords
            taug[3 * feat : 4 * feat, at] = coords
            place += 1
    total = place * LANES
    potential = None
    if previous is not None:
        own, other, g_old = (ref[...] for ref in previous)
        other = jnp.concatenate([other[:, total // 2 :], other[:, : total // 2]], axis=1)
        peak = jnp.maximum(own, other)
        potential = g_old - (peak + jnp.log2(jnp.exp2(own - peak) + jnp.exp2(other - peak)))
        g_ref[...] = g_ref[...] + potential
    g = g_ref[...]
    high, middle, low = three_terms(g - jnp.max(g) - q_ref[...])
    extras = pick_rows(
        (EXTRA, total),
        [high.astype(jnp.float32), middle.astype(jnp.float32), low.astype(jnp.float32), 1.0],
        0.0,
    )
    taug[EXTRA : 2 * EXTRA, :] = extras.astype(jnp.bfloat16)
    return potential


def exponents(left, taug, begin, width):
    return jnp.dot(left, taug[:, begin : begin + width], preferred_element_type=jnp.float32)


def row_logw(left):
    return left[:, EXTRA + 4 : EXTRA + 5].astype(jnp.float32) * LOG2E


def fast_tile(left, taug, p_ref, col_ref):
    total = taug.shape[1]
    width = min(total, 256)
    sums = jnp.zeros((ROWS, LANES), jnp.float32)
    for begin in range(0, total, width):
        p = jnp.exp2(exponents(left, taug, begin, width))
        p_ref[:, begin : begin + width] = p
        for lane in range(0, width, LANES):
            sums = sums + p[:, lane : lane + LANES]
    s = jnp.sum(sums, axis=1, keepdims=True)
    weight = jnp.exp2(row_logw(left)) / s
    for begin in range(0, total, width):
        p = p_ref[:, begin : begin + width] * weight
        col_ref[:, begin : begin + width] += jnp.sum(p.reshape(ROWS // 8, 8, width), axis=0)
    return jnp.min(s.reshape(ROWS // 8, 8, 1), axis=0)


def column_sums(xaug, taug, p_ref, col_ref, top_ref, out_ref):
    total = taug.shape[1]
    tiles = xaug.shape[0] // ROWS
    side = p_ref.shape[0]
    col_ref[...] = jnp.zeros_like(col_ref)

    def advance(step, least):
        for slot in range(side):
            left = xaug[pl.ds(pl.multiple_of((step * side + slot) * ROWS, ROWS), ROWS), :]
            least = jnp.minimum(least, fast_tile(left, taug, p_ref.at[slot], col_ref))
        return least

    least = lax.fori_loop(0, tiles // side, advance, jnp.full((8, 1), 1e30, jnp.float32))
    cols = jnp.sum(col_ref[...], axis=0, keepdims=True)
    out_ref[...] = jnp.log2(cols)
    fine = jnp.logical_and(
        jnp.min(least) >= SMALL_ROW,
        jnp.logical_and(jnp.min(cols) >= SMALL_COL, jnp.max(cols) <= LARGE_COL),
    )

    @pl.when(jnp.logical_not(fine))
    def _():
        col_ref[...] = jnp.zeros_like(col_ref)
        top_ref[...] = jnp.full_like(top_ref, FLOOR)

        def careful(step, carry):
            left = xaug[pl.ds(pl.multiple_of(step * ROWS, ROWS), ROWS), :]
            e = exponents(left, taug, 0, total)
            peak = jnp.max(e, axis=1, keepdims=True)
            s = jnp.sum(jnp.exp2(e - peak), axis=1, keepdims=True)
            term = e + (row_logw(left) - peak - jnp.log2(s))
            old = top_ref[...]
            top = jnp.maximum(old, jnp.max(term, axis=0, keepdims=True))
            added = jnp.sum(jnp.exp2(term - top), axis=0, keepdims=True)
            col_ref[0:1, :] = col_ref[0:1, :] * jnp.exp2(old - top) + added
            top_ref[...] = top
            return carry

        lax.fori_loop(0, tiles, careful, 0)
        out_ref[...] = top_ref[...] + jnp.log2(col_ref[0:1, :])


def first_kernel(n_x, n_t, feat, inverse, *refs):
    xs, ts, logws = refs[:n_x], refs[n_x : n_x + n_t], refs[n_x + n_t]
    xaug, out_ref, g_ref, taug, q_ref, p_ref, col_ref, top_ref = refs[n_x + n_t + 1 :]
    scale = inverse[0] * LOG2E
    count = xs[0].shape[2]
    place = 0
    for part in xs:
        for block in range(part.shape[0]):
            high, tail = stage_source(part[block], logws[place : place + 1, :], scale)
            rows = pl.ds(place * count, count)
            xaug[rows, 0:LANES] = high
            xaug[rows, LANES:DEPTH] = tail
            place += 1
    stage_targets(ts, None, scale, taug, g_ref, q_ref, feat)
    column_sums(xaug, taug, p_ref, col_ref, top_ref, out_ref)


def next_kernel(n_t, feat, inverse, xaug, own, other, g_old, *refs):
    ts = refs[:n_t]
    out_ref, g_ref, taug, q_ref, p_ref, col_ref, top_ref = refs[n_t:]
    scale = inverse[0] * LOG2E
    stage_targets(ts, (own, other, g_old), scale, taug, g_ref, q_ref, feat)
    column_sums(xaug, taug, p_ref, col_ref, top_ref, out_ref)


def map_kernel(n_t, feat, inverse, xaug, own, other, g_old, *refs):
    ts = refs[:n_t]
    mapped_ref, pot_ref, g_ref, taug, q_ref, p_ref, plan_ref = refs[n_t:]
    scale = inverse[0] * LOG2E
    potential = stage_targets(ts, (own, other, g_old), scale, taug, g_ref, q_ref, feat)
    pot_ref[...] = potential[:, :LANES] * (1.0 / LOG2E)
    total = taug.shape[1]
    width = min(total, 256)

    for begin_row in range(0, xaug.shape[0], ROWS):
        rows = slice(begin_row, begin_row + ROWS)
        left = xaug[rows, :]
        sums = jnp.zeros((ROWS, LANES), jnp.float32)
        for begin in range(0, total, width):
            p = jnp.exp2(exponents(left, taug, begin, width))
            p_ref[:, begin : begin + width] = p
            for lane in range(0, width, LANES):
                sums = sums + p[:, lane : lane + LANES]
        s = jnp.sum(sums, axis=1, keepdims=True)
        inv_s = 1.0 / s
        for begin in range(0, total, width):
            piece = slice(begin, begin + width)
            plan_ref[rows, piece] = (p_ref[:, piece] * inv_s).astype(jnp.bfloat16)

        @pl.when(jnp.logical_not(jnp.min(s) >= SMALL_ROW))
        def _():
            e = exponents(left, taug, 0, total)
            e = e - jnp.max(e, axis=1, keepdims=True)
            e = e - jnp.log2(jnp.sum(jnp.exp2(e), axis=1, keepdims=True))
            plan_ref[rows, :] = jnp.exp2(e).astype(jnp.bfloat16)

    mapped_ref[...] = lax.dot_general(
        taug[0:feat, :],
        plan_ref[...],
        (((1,), (1,)), ((), ())),
        preferred_element_type=jnp.float32,
    )


def swap(value, count, step):
    return lax.ppermute(value, AXIS, [(source, source ^ step) for source in range(count)])


def chip_stages(count):
    high, stages = count.bit_length() - 1, []
    while high > 1:
        width = min(2, high - 1)
        stages.append((high - width, width))
        high -= width
    return stages


def gather_chips(block, count):
    parts = [block[None]]
    for low, width in chip_stages(count):
        held = parts[0] if len(parts) == 1 else jnp.concatenate(parts, axis=0)
        digits = range((1 << width) - 1, 0, -1)
        parts = [held] + [swap(held, count, digit << low) for digit in digits]
    return parts


def on_device(source_points, target_points, source_logw, target_logw, inverse_eps, count):
    feat, own_sources = source_points.shape
    own_targets = target_points.shape[1]
    extra_rows = own_sources // LANES
    pad = -(1 + extra_rows) % 16
    packed = jnp.concatenate(
        [
            target_points,
            target_logw[None, :],
            source_logw.reshape(extra_rows, LANES),
            jnp.zeros((pad, own_targets), target_points.dtype),
        ],
        axis=0,
    )
    mine = gather_chips(packed, count)
    theirs = [swap(part, count, 1) for part in mine]
    ts = mine + theirs
    xs = gather_chips(source_points, count)
    chips = count // 2
    logws = jnp.concatenate(
        [part[:, feat + 1 : feat + 1 + extra_rows] for part in mine], axis=0
    ).reshape(chips, own_sources).astype(jnp.float32)

    total, rows = count * own_targets, chips * own_sources
    side = 3 if total <= 4096 else 1
    f32, bf16 = jnp.float32, jnp.bfloat16
    vmem = pl.BlockSpec(memory_space=pltpu.VMEM)
    smem = pl.BlockSpec(memory_space=pltpu.SMEM)
    params = pltpu.CompilerParams(vmem_limit_bytes=(24 if total <= 4096 else 56) << 20)
    line = jax.ShapeDtypeStruct((1, total), f32)
    sums_scratch = [
        pltpu.VMEM((DEPTH, total), bf16),
        pltpu.VMEM((1, total), f32),
        pltpu.VMEM((side, ROWS, total), f32),
        pltpu.VMEM((8, total), f32),
        pltpu.VMEM((1, total), f32),
    ]

    xaug, sums, g = pl.pallas_call(
        functools.partial(first_kernel, len(xs), len(ts), feat),
        out_shape=[jax.ShapeDtypeStruct((rows, DEPTH), bf16), line, line],
        in_specs=[smem] + [vmem] * (len(xs) + len(ts) + 1),
        out_specs=[vmem] * 3,
        scratch_shapes=sums_scratch,
        compiler_params=params,
    )(inverse_eps, *xs, *ts, logws)
    for _ in range(ITERS - 1):
        sums, g = pl.pallas_call(
            functools.partial(next_kernel, len(ts), feat),
            out_shape=[line, line],
            in_specs=[smem] + [vmem] * (4 + len(ts)),
            out_specs=[vmem] * 2,
            scratch_shapes=sums_scratch,
            compiler_params=params,
        )(inverse_eps, xaug, sums, swap(sums, count, 1), g, *ts)
    mapped, potential = pl.pallas_call(
        functools.partial(map_kernel, len(ts), feat),
        out_shape=[
            jax.ShapeDtypeStruct((feat, own_sources), f32),
            jax.ShapeDtypeStruct((1, own_targets), f32),
        ],
        in_specs=[smem] + [vmem] * (4 + len(ts)),
        out_specs=[vmem] * 2,
        scratch_shapes=[
            pltpu.VMEM((1, total), f32),
            pltpu.VMEM((DEPTH, total), bf16),
            pltpu.VMEM((1, total), f32),
            pltpu.VMEM((ROWS, total), f32),
            pltpu.VMEM((own_sources, total), bf16),
        ],
        compiler_params=params,
    )(inverse_eps, xaug[:own_sources], sums, swap(sums, count, 1), g, *ts)
    return (mapped, potential.reshape(own_targets))


def solution(mesh):
    count = mesh.shape[AXIS]
    placed = (
        P(None, ("grp", "wide")),
        P(None, ("grp", "wide")),
        P(("grp", "wide")),
        P(("grp", "wide")),
        P(),
    )

    def body(*blocks):
        return on_device(*blocks, count)

    return jax.shard_map(
        body,
        mesh=mesh,
        in_specs=placed,
        out_specs=(P(None, ("grp", "wide")), P(("grp", "wide"))),
        check_vma=False,
    )
```

```python
import functools
import math

import jax
import jax.numpy as jnp
from jax import lax
from jax.experimental import pallas as pl
from jax.experimental.pallas import tpu as pltpu
from jax.sharding import PartitionSpec as P

ITERS = 2
AXIS = "wide"
LOG2E = math.log2(math.e)
LANES = 128
DEPTH = 256
SMALL_ROW = 2.0**-64
SMALL_COL = 2.0**-32
LARGE_COL = 2.0**100
FLOOR = -1e30


def three_terms(value):
    high = value.astype(jnp.bfloat16)
    rest = value - high.astype(jnp.float32)
    middle = rest.astype(jnp.bfloat16)
    low = (rest - middle.astype(jnp.float32)).astype(jnp.bfloat16)
    return high, middle, low


def pick_rows(shape, rows):
    index = lax.broadcasted_iota(jnp.int32, shape, 0)
    out = jnp.zeros(shape, jnp.float32)
    for place, row in enumerate(rows):
        out = jnp.where(index == place, row, out)
    return out


def stage_source(points, scale, xaug, at):
    feat, count = points.shape
    wide = points.astype(jnp.float32)
    shift = scale * jnp.sum(wide * wide, axis=0, keepdims=True)
    shift = shift.astype(jnp.bfloat16).astype(jnp.float32)
    xaug[0:feat, at] = pick_rows((feat, count), [1.0, 1.0, 1.0, -shift]).astype(jnp.bfloat16)
    for place, term in enumerate(three_terms(2.0 * scale * wide)):
        xaug[(place + 1) * feat : (place + 2) * feat, at] = term


def stage_targets(parts, previous, scale, taug, g_ref, q_ref, feat):
    blocks = [(part, block) for part in parts for block in range(part.shape[0])]
    total = len(blocks) * LANES
    for place, (part, block) in enumerate(blocks):
        at = slice(place * LANES, (place + 1) * LANES)
        wide = part[block, :feat, :].astype(jnp.float32)
        q_ref[:, at] = scale * jnp.sum(wide * wide, axis=0, keepdims=True)
        logw = part[block, feat : feat + 16, :].astype(jnp.float32)[0:1]
        g_ref[:, at] = logw * LOG2E
    potential = None
    if previous is not None:
        own, other, g_old = (ref[...] for ref in previous)
        other = jnp.concatenate([other[:, total // 2 :], other[:, : total // 2]], axis=1)
        peak = jnp.maximum(own, other)
        potential = g_old - (peak + jnp.log2(jnp.exp2(own - peak) + jnp.exp2(other - peak)))
        g_ref[...] = g_ref[...] + potential
    g = g_ref[...]
    terms = [term.astype(jnp.float32) for term in three_terms(g - jnp.max(g) - q_ref[...])]
    for place, (part, block) in enumerate(blocks):
        at = slice(place * LANES, (place + 1) * LANES)
        extras = pick_rows((feat, LANES), [term[:, at] for term in terms] + [1.0])
        wide = part[block, :feat, :].astype(jnp.float32)
        turned = jnp.concatenate([extras, wide], axis=0).T
        lane = lax.broadcasted_iota(jnp.int32, turned.shape, 1)
        twice = jnp.where(lane < feat, pltpu.roll(turned, feat, 1), turned)
        taug[at, 0:LANES] = turned.astype(jnp.bfloat16)
        taug[at, LANES:DEPTH] = twice.astype(jnp.bfloat16)
    return potential


def exponents(left, right):
    return jnp.dot(left, right, preferred_element_type=jnp.float32)


def spread_rows(taug, right, p_ref, beside):
    total, width = taug.shape[0], right.shape[1]
    reach = min(total, 2048)
    sums = jnp.zeros((8, width), jnp.float32)
    for begin in range(0, total, reach):
        e = exponents(taug[begin : begin + reach, :], right)
        for inner in range(0, reach, LANES):
            p = jnp.exp2(e[inner : inner + LANES])
            p_ref[begin + inner : begin + inner + LANES, :] = p
            sums = sums + jnp.sum(p.reshape(LANES // 8, 8, width), axis=0)
            beside(slice(begin + inner, begin + inner + LANES))
    return jnp.sum(sums, axis=0, keepdims=True)


def add_columns(p_ref, weight, col_ref, rows):
    width = weight.shape[1]
    added = p_ref[rows, 0:LANES] * weight[:, 0:LANES]
    for lane in range(LANES, width, LANES):
        added = added + p_ref[rows, lane : lane + LANES] * weight[:, lane : lane + LANES]
    col_ref[rows, :] += added


def column_sums(xaug, logws, taug, p_refs, col_ref, top_ref, out_ref):
    total = taug.shape[0]
    width = p_refs[0].shape[1]
    tiles = xaug.shape[1] // width
    col_ref[...] = jnp.zeros_like(col_ref)

    def columns(tile):
        if isinstance(tile, int):
            return pl.ds(tile * width, width)
        return pl.ds(pl.multiple_of(tile * width, width), width)

    def step(tile, slot, held):
        def beside(rows):
            if held is not None:
                add_columns(p_refs[1 - slot], held, col_ref, rows)

        at = columns(tile)
        s = spread_rows(taug, xaug[:, at], p_refs[slot], beside)
        return s, jnp.exp2(logws[:, at] * LOG2E) / s

    def two_steps(pair, carry):
        least, weight = carry
        s1, weight1 = step(2 * pair + 1, 1, weight)
        s0, weight0 = step(2 * pair + 2, 0, weight1)
        return jnp.minimum(least, jnp.minimum(s0, s1)), weight0

    s, weight = step(0, 0, None)
    least, weight = lax.fori_loop(0, tiles // 2 - 1, two_steps, (s, weight))
    s, weight = step(tiles - 1, 1, weight)
    least = jnp.minimum(least, s)
    for begin in range(0, total, LANES):
        rows = slice(begin, begin + LANES)
        add_columns(p_refs[1], weight, col_ref, rows)
        out_ref[:, rows] = jnp.sum(col_ref[rows, :].T, axis=0, keepdims=True)
    cols = out_ref[...]
    out_ref[...] = jnp.log2(cols)
    fine = jnp.logical_and(
        jnp.min(least) >= SMALL_ROW,
        jnp.logical_and(jnp.min(cols) >= SMALL_COL, jnp.max(cols) <= LARGE_COL),
    )

    @pl.when(jnp.logical_not(fine))
    def _():
        col_ref[...] = jnp.zeros_like(col_ref)
        top_ref[...] = jnp.full_like(top_ref, FLOOR)
        blocks = total // LANES

        def block_rows(block):
            return pl.ds(pl.multiple_of(block * LANES, LANES), LANES)

        def careful(tile, carry):
            at = columns(tile)
            right = xaug[:, at]

            def highest(block, peak):
                e = exponents(taug[block_rows(block), :], right)
                return jnp.maximum(peak, jnp.max(e, axis=0, keepdims=True))

            peak = lax.fori_loop(0, blocks, highest, jnp.full((1, width), FLOOR, jnp.float32))

            def summed(block, s):
                e = exponents(taug[block_rows(block), :], right)
                return s + jnp.sum(jnp.exp2(e - peak), axis=0, keepdims=True)

            s = lax.fori_loop(0, blocks, summed, jnp.zeros((1, width), jnp.float32))
            shift = logws[:, at] * LOG2E - peak - jnp.log2(s)

            def collected(block, carry):
                rows = block_rows(block)
                term = exponents(taug[rows, :], right) + shift
                for lane in range(0, width, LANES):
                    piece = term[:, lane : lane + LANES]
                    old = top_ref[rows, :]
                    top = jnp.maximum(old, piece)
                    col_ref[rows, :] = col_ref[rows, :] * jnp.exp2(old - top) + jnp.exp2(
                        piece - top
                    )
                    top_ref[rows, :] = top
                return carry

            return lax.fori_loop(0, blocks, collected, carry)

        lax.fori_loop(0, tiles, careful, 0)
        for begin in range(0, total, LANES):
            rows = slice(begin, begin + LANES)
            tops = top_ref[rows, :].T
            top = jnp.max(tops, axis=0, keepdims=True)
            added = jnp.sum(col_ref[rows, :].T * jnp.exp2(tops - top), axis=0, keepdims=True)
            out_ref[:, rows] = top + jnp.log2(added)


def first_kernel(n_x, n_t, feat, inverse, logws, *refs):
    xs, ts = refs[:n_x], refs[n_x : n_x + n_t]
    xaug, out_ref, g_ref, taug, q_ref, p0, p1, col_ref, top_ref = refs[n_x + n_t :]
    scale = inverse[0] * LOG2E
    count = xs[0].shape[2]
    place = 0
    for part in xs:
        for block in range(part.shape[0]):
            stage_source(part[block], scale, xaug, slice(place * count, (place + 1) * count))
            place += 1
    stage_targets(ts, None, scale, taug, g_ref, q_ref, feat)
    column_sums(xaug, logws, taug, (p0, p1), col_ref, top_ref, out_ref)


def next_kernel(n_t, feat, inverse, logws, xaug, own, other, g_old, *refs):
    ts = refs[:n_t]
    out_ref, g_ref, taug, q_ref, p0, p1, col_ref, top_ref = refs[n_t:]
    scale = inverse[0] * LOG2E
    stage_targets(ts, (own, other, g_old), scale, taug, g_ref, q_ref, feat)
    column_sums(xaug, logws, taug, (p0, p1), col_ref, top_ref, out_ref)


def map_kernel(n_t, feat, inverse, xaug, own, other, g_old, *refs):
    ts = refs[:n_t]
    mapped_ref, pot_ref, g_ref, taug, q_ref, p_ref, plan_ref, coords = refs[n_t:]
    scale = inverse[0] * LOG2E
    potential = stage_targets(ts, (own, other, g_old), scale, taug, g_ref, q_ref, feat)
    pot_ref[...] = potential[:, :LANES] * (1.0 / LOG2E)
    place = 0
    for part in ts:
        for block in range(part.shape[0]):
            coords[:, place * LANES : (place + 1) * LANES] = part[block, :feat, :]
            place += 1
    total = taug.shape[0]
    right = xaug[...]
    s = spread_rows(taug, right, p_ref, lambda rows: None)
    weight = 1.0 / s
    for begin in range(0, total, LANES):
        rows = slice(begin, begin + LANES)
        plan_ref[rows, :] = (p_ref[rows, :] * weight).astype(jnp.bfloat16)

    @pl.when(jnp.logical_not(jnp.min(s) >= SMALL_ROW))
    def _():
        reach = min(total, 2048)
        peak = jnp.full(s.shape, FLOOR, jnp.float32)
        for begin in range(0, total, reach):
            rows = slice(begin, begin + reach)
            p_ref[rows, :] = exponents(taug[rows, :], right)
            peak = jnp.maximum(peak, jnp.max(p_ref[rows, :], axis=0, keepdims=True))
        sums = jnp.zeros(s.shape, jnp.float32)
        for begin in range(0, total, reach):
            rows = slice(begin, begin + reach)
            sums += jnp.sum(jnp.exp2(p_ref[rows, :] - peak), axis=0, keepdims=True)
        shift = peak + jnp.log2(sums)
        for begin in range(0, total, reach):
            rows = slice(begin, begin + reach)
            plan_ref[rows, :] = jnp.exp2(p_ref[rows, :] - shift).astype(jnp.bfloat16)

    mapped_ref[...] = jnp.dot(coords[...], plan_ref[...], preferred_element_type=jnp.float32)


def swap(value, count, step):
    return lax.ppermute(value, AXIS, [(source, source ^ step) for source in range(count)])


def chip_stages(count):
    high, stages = count.bit_length() - 1, []
    while high > 1:
        width = min(2, high - 1)
        stages.append((high - width, width))
        high -= width
    return stages


def gather_chips(block, count):
    parts = [block[None]]
    for low, width in chip_stages(count):
        held = parts[0] if len(parts) == 1 else jnp.concatenate(parts, axis=0)
        digits = range((1 << width) - 1, 0, -1)
        parts = [held] + [swap(held, count, digit << low) for digit in digits]
    return parts


def on_device(source_points, target_points, source_logw, target_logw, inverse_eps, count):
    feat, own_sources = source_points.shape
    own_targets = target_points.shape[1]
    extra_rows = own_sources // LANES
    pad = -(1 + extra_rows) % 16
    packed = jnp.concatenate(
        [
            target_points,
            target_logw[None, :],
            source_logw.reshape(extra_rows, LANES),
            jnp.zeros((pad, own_targets), target_points.dtype),
        ],
        axis=0,
    )
    mine = gather_chips(packed, count)
    theirs = [swap(part, count, 1) for part in mine]
    ts = mine + theirs
    xs = gather_chips(source_points, count)
    chips = count // 2
    logws = jnp.concatenate(
        [part[:, feat + 1 : feat + 1 + extra_rows] for part in mine], axis=0
    ).reshape(1, chips * own_sources).astype(jnp.float32)

    total, rows = count * own_targets, chips * own_sources
    small = total <= 4096
    width = 2 * LANES if small else LANES
    f32, bf16 = jnp.float32, jnp.bfloat16
    vmem = pl.BlockSpec(memory_space=pltpu.VMEM)
    smem = pl.BlockSpec(memory_space=pltpu.SMEM)
    params = pltpu.CompilerParams(vmem_limit_bytes=(24 if small else 60) << 20)
    line = jax.ShapeDtypeStruct((1, total), f32)
    sums_scratch = [
        pltpu.VMEM((total, DEPTH), bf16),
        pltpu.VMEM((1, total), f32),
        pltpu.VMEM((total, width), f32),
        pltpu.VMEM((total, width), f32),
        pltpu.VMEM((total, LANES), f32),
        pltpu.VMEM((total, LANES), f32),
    ]

    xaug, sums, g = pl.pallas_call(
        functools.partial(first_kernel, len(xs), len(ts), feat),
        out_shape=[jax.ShapeDtypeStruct((DEPTH, rows), bf16), line, line],
        in_specs=[smem] + [vmem] * (len(xs) + len(ts) + 1),
        out_specs=[vmem] * 3,
        scratch_shapes=sums_scratch,
        compiler_params=params,
    )(inverse_eps, logws, *xs, *ts)
    for _ in range(ITERS - 1):
        sums, g = pl.pallas_call(
            functools.partial(next_kernel, len(ts), feat),
            out_shape=[line, line],
            in_specs=[smem] + [vmem] * (5 + len(ts)),
            out_specs=[vmem] * 2,
            scratch_shapes=sums_scratch,
            compiler_params=params,
        )(inverse_eps, logws, xaug, sums, swap(sums, count, 1), g, *ts)
    mapped, potential = pl.pallas_call(
        functools.partial(map_kernel, len(ts), feat),
        out_shape=[
            jax.ShapeDtypeStruct((feat, own_sources), f32),
            jax.ShapeDtypeStruct((1, own_targets), f32),
        ],
        in_specs=[smem] + [vmem] * (4 + len(ts)),
        out_specs=[vmem] * 2,
        scratch_shapes=[
            pltpu.VMEM((1, total), f32),
            pltpu.VMEM((total, DEPTH), bf16),
            pltpu.VMEM((1, total), f32),
            pltpu.VMEM((total, own_sources), f32),
            pltpu.VMEM((total, own_sources), bf16),
            pltpu.VMEM((feat, total), bf16),
        ],
        compiler_params=params,
    )(inverse_eps, xaug[:, :own_sources], sums, swap(sums, count, 1), g, *ts)
    return (mapped, potential.reshape(own_targets))


def solution(mesh):
    count = mesh.shape[AXIS]
    placed = (
        P(None, ("grp", "wide")),
        P(None, ("grp", "wide")),
        P(("grp", "wide")),
        P(("grp", "wide")),
        P(),
    )

    def body(*blocks):
        return on_device(*blocks, count)

    return jax.shard_map(
        body,
        mesh=mesh,
        in_specs=placed,
        out_specs=(P(None, ("grp", "wide")), P(("grp", "wide"))),
        check_vma=False,
    )
```

```python
import functools
import math

import jax
import jax.numpy as jnp
from jax import lax
from jax.experimental import pallas as pl
from jax.experimental.pallas import tpu as pltpu
from jax.sharding import PartitionSpec as P

ITERS = 2
AXIS = "wide"
LOG2E = math.log2(math.e)
LANES = 128
DEPTH = 256
SMALL_ROW = 2.0**-64
SMALL_COL = 2.0**-32
LARGE_COL = 2.0**100
FLOOR = -1e30


def three_terms(value):
    high = value.astype(jnp.bfloat16)
    rest = value - high.astype(jnp.float32)
    middle = rest.astype(jnp.bfloat16)
    low = (rest - middle.astype(jnp.float32)).astype(jnp.bfloat16)
    return high, middle, low


def pick_rows(shape, rows):
    index = lax.broadcasted_iota(jnp.int32, shape, 0)
    out = jnp.zeros(shape, jnp.float32)
    for place, row in enumerate(rows):
        out = jnp.where(index == place, row, out)
    return out


def stage_source(points, scale, xaug, at):
    feat, count = points.shape
    wide = points.astype(jnp.float32)
    shift = scale * jnp.sum(wide * wide, axis=0, keepdims=True)
    shift = shift.astype(jnp.bfloat16).astype(jnp.float32)
    xaug[0:feat, at] = pick_rows((feat, count), [1.0, 1.0, 1.0, -shift]).astype(jnp.bfloat16)
    for place, term in enumerate(three_terms(2.0 * scale * wide)):
        xaug[(place + 1) * feat : (place + 2) * feat, at] = term


def stage_sources(parts, scale, xaug):
    place = 0
    for part in parts:
        count = part.shape[2]
        for block in range(part.shape[0]):
            stage_source(part[block], scale, xaug, slice(place * count, (place + 1) * count))
            place += 1


def target_lines(part, block, scale, feat):
    wide = part[block, :feat, :].astype(jnp.float32)
    logw = part[block, feat : feat + 16, :].astype(jnp.float32)[0:1]
    return scale * jnp.sum(wide * wide, axis=0, keepdims=True), logw * LOG2E


def stage_targets(parts, scale, taug, begin, feat):
    for part in parts:
        for block in range(part.shape[0]):
            q, logw = target_lines(part, block, scale, feat)
            terms = [term.astype(jnp.float32) for term in three_terms(logw - q)]
            extras = pick_rows((feat, LANES), terms + [1.0])
            wide = part[block, :feat, :].astype(jnp.float32)
            turned = jnp.concatenate([extras, wide], axis=0).T
            lane = lax.broadcasted_iota(jnp.int32, turned.shape, 1)
            twice = jnp.where(lane < feat, pltpu.roll(turned, feat, 1), turned)
            taug[begin : begin + LANES, 0:LANES] = turned.astype(jnp.bfloat16)
            taug[begin : begin + LANES, LANES:DEPTH] = twice.astype(jnp.bfloat16)
            begin += LANES


def renew_targets(own, other, g, q, logw, taug):
    total = own.shape[1]
    other = jnp.concatenate([other[:, total // 2 :], other[:, : total // 2]], axis=1)
    peak = jnp.maximum(own, other)
    potential = g - (peak + jnp.log2(jnp.exp2(own - peak) + jnp.exp2(other - peak)))
    g = potential + logw
    terms = [term.astype(jnp.float32) for term in three_terms(g - jnp.max(g) - q)]
    for begin in range(0, total, LANES):
        rows = slice(begin, begin + LANES)
        extras = pick_rows((8, LANES), [term[:, rows] for term in terms] + [1.0])
        taug[rows, 0:8] = extras.T.astype(jnp.bfloat16)
    return potential, g


def exponents(left, right):
    return jnp.dot(left, right, preferred_element_type=jnp.float32)


def spread_rows(taug, right, p_ref, beside):
    total, width = taug.shape[0], right.shape[1]
    reach = min(total, 2048)
    sums = jnp.zeros((8, width), jnp.float32)
    for begin in range(0, total, reach):
        e = exponents(taug[begin : begin + reach, :], right)
        for inner in range(0, reach, LANES):
            rows = slice(begin + inner, begin + inner + LANES)
            beside(rows)
            p = jnp.exp2(e[inner : inner + LANES])
            p_ref[rows, :] = p
            sums = sums + jnp.sum(p.reshape(LANES // 8, 8, width), axis=0)
    return jnp.sum(sums, axis=0, keepdims=True)


def add_columns(p_ref, weight, col_ref, rows):
    width = weight.shape[1]
    added = p_ref[rows, 0:LANES] * weight[:, 0:LANES]
    for lane in range(LANES, width, LANES):
        added = added + p_ref[rows, lane : lane + LANES] * weight[:, lane : lane + LANES]
    col_ref[rows, :] += added


def tile_columns(tile, width):
    if isinstance(tile, int):
        return pl.ds(tile * width, width)
    return pl.ds(pl.multiple_of(tile * width, width), width)


def add_sources(xaug, logws, taug, p_refs, col_ref):
    total = taug.shape[0]
    width = p_refs[0].shape[1]
    tiles = xaug.shape[1] // width
    if p_refs[1].shape != p_refs[0].shape:
        p_refs = (p_refs[0], p_refs[0])

    def step(tile, slot, held):
        def beside(rows):
            if held is not None:
                add_columns(p_refs[1 - slot], held, col_ref, rows)

        at = tile_columns(tile, width)
        s = spread_rows(taug, xaug[:, at], p_refs[slot], beside)
        return s, jnp.exp2(logws[:, at] * LOG2E) / s

    def two_steps(pair, carry):
        least, weight = carry
        s1, weight1 = step(2 * pair + 1, 1, weight)
        s0, weight0 = step(2 * pair + 2, 0, weight1)
        return jnp.minimum(least, jnp.minimum(s0, s1)), weight0

    s, weight = step(0, 0, None)
    least, weight = lax.fori_loop(0, tiles // 2 - 1, two_steps, (s, weight))
    s, weight = step(tiles - 1, 1, weight)
    for begin in range(0, total, LANES):
        add_columns(p_refs[1], weight, col_ref, slice(begin, begin + LANES))
    return jnp.minimum(least, s)


def lane_totals(col_ref, out_ref):
    total = col_ref.shape[0]
    reach = min(total, 2048)
    ones = jnp.ones((16, 2 * LANES), jnp.bfloat16)
    for begin in range(0, total, reach):
        high, middle, _ = three_terms(col_ref[begin : begin + reach, :])
        both = jnp.concatenate([high, middle], axis=1)
        added = lax.dot_general(
            ones, both, (((1,), (1,)), ((), ())), preferred_element_type=jnp.float32
        )
        out_ref[:, begin : begin + reach] = added[0:1]


def finish_sums(pieces, taug, least, p_ref, col_ref, out_ref):
    total = taug.shape[0]
    lane_totals(col_ref, out_ref)
    cols = out_ref[...]
    out_ref[...] = jnp.log2(cols)
    fine = jnp.logical_and(
        jnp.min(least) >= SMALL_ROW,
        jnp.logical_and(jnp.min(cols) >= SMALL_COL, jnp.max(cols) <= LARGE_COL),
    )

    top_ref = p_ref.at[:, 0:LANES]

    @pl.when(jnp.logical_not(fine))
    def _():
        col_ref[...] = jnp.zeros_like(col_ref)
        top_ref[...] = jnp.full_like(top_ref, FLOOR)
        blocks = total // LANES

        def block_rows(block):
            return pl.ds(pl.multiple_of(block * LANES, LANES), LANES)

        def careful(xaug, logws, tile, carry):
            at = tile_columns(tile, LANES)
            right = xaug[:, at]

            def highest(block, peak):
                e = exponents(taug[block_rows(block), :], right)
                return jnp.maximum(peak, jnp.max(e, axis=0, keepdims=True))

            peak = lax.fori_loop(0, blocks, highest, jnp.full((1, LANES), FLOOR, jnp.float32))

            def summed(block, s):
                e = exponents(taug[block_rows(block), :], right)
                return s + jnp.sum(jnp.exp2(e - peak), axis=0, keepdims=True)

            s = lax.fori_loop(0, blocks, summed, jnp.zeros((1, LANES), jnp.float32))
            shift = logws[:, at] * LOG2E - peak - jnp.log2(s)

            def collected(block, carry):
                rows = block_rows(block)
                term = exponents(taug[rows, :], right) + shift
                old = top_ref[rows, :]
                top = jnp.maximum(old, term)
                col_ref[rows, :] = col_ref[rows, :] * jnp.exp2(old - top) + jnp.exp2(term - top)
                top_ref[rows, :] = top
                return carry

            return lax.fori_loop(0, blocks, collected, carry)

        for xaug, logws in pieces:
            tiles = xaug.shape[1] // LANES
            lax.fori_loop(0, tiles, functools.partial(careful, xaug, logws), 0)

        def turned(block, carry):
            rows = block_rows(block)
            tops = top_ref[rows, :].T
            top = jnp.max(tops, axis=0, keepdims=True)
            added = jnp.sum(col_ref[rows, :].T * jnp.exp2(tops - top), axis=0, keepdims=True)
            out_ref[:, rows] = top + jnp.log2(added)
            return carry

        lax.fori_loop(0, blocks, turned, 0)


def part_kernel(n_t, feat, inverse, points, *refs):
    ts, (taug, copy_ref) = refs[:n_t], refs[n_t:]
    copy_ref[0] = points[...]
    stage_targets(ts, inverse[0] * LOG2E, taug, 0, feat)


def more_kernel(n_t, feat, inverse, *refs):
    ts, (taug,) = refs[:n_t], refs[n_t:]
    stage_targets(ts, inverse[0] * LOG2E, taug, 0, feat)


def near_kernel(n_x, n_staged, n_t, n_late, feat, inverse, logws, *refs):
    xs, refs = refs[:n_x], refs[n_x:]
    staged, refs = refs[:n_staged], refs[n_staged:]
    ts, refs = refs[:n_t], refs[n_t:]
    late = ts[n_t - n_late :]
    xaug, taug, col_ref, least_ref, g_ref, q_ref, p0, p1 = refs
    scale = inverse[0] * LOG2E
    stage_sources(xs, scale, xaug)
    place = 0
    for part in ts:
        for block in range(part.shape[0]):
            at = slice(place * LANES, (place + 1) * LANES)
            q_ref[:, at], g_ref[:, at] = target_lines(part, block, scale, feat)
            place += 1
    begin = 0
    for part in staged:
        taug[begin : begin + part.shape[0], :] = part[...]
        begin += part.shape[0]
    stage_targets(late, scale, taug, begin, feat)
    col_ref[...] = jnp.zeros_like(col_ref)
    least_ref[...] = add_sources(xaug, logws, taug, (p0, p1), col_ref)


def far_kernel(n_x, inverse, near_logws, logws, near_xaug, taug, near_col, near_least, *refs):
    xs, refs = refs[:n_x], refs[n_x:]
    xaug, out_ref, p0, p1, col_ref = refs
    stage_sources(xs, inverse[0] * LOG2E, xaug)
    col_ref[...] = near_col[...]
    least = add_sources(xaug, logws, taug, (p0, p1), col_ref)
    least = jnp.minimum(least, near_least[...])
    pieces = [(near_xaug, near_logws), (xaug, logws)]
    finish_sums(pieces, taug, least, p0, col_ref, out_ref)


def next_kernel(near_logws, far_logws, near_xaug, far_xaug, old, own, other, g, q, logw, *refs):
    out_ref, g_ref, taug, p0, p1, col_ref = refs
    taug[...] = old[...]
    g_ref[...] = renew_targets(own[...], other[...], g[...], q[...], logw[...], taug)[1]
    col_ref[...] = jnp.zeros_like(col_ref)
    pieces = [(near_xaug, near_logws), (far_xaug, far_logws)]
    least = [add_sources(xaug, logws, taug, (p0, p1), col_ref) for xaug, logws in pieces]
    least = jnp.minimum(least[0], least[1])
    finish_sums(pieces, taug, least, p0, col_ref, out_ref)


def map_kernel(n_t, feat, xaug, old, own, other, g, q, logw, *refs):
    ts = refs[:n_t]
    mapped_ref, pot_ref, taug, p_ref, plan_ref, coords = refs[n_t:]
    taug[...] = old[...]
    potential = renew_targets(own[...], other[...], g[...], q[...], logw[...], taug)[0]
    pot_ref[...] = potential[:, :LANES] * (1.0 / LOG2E)
    place = 0
    for part in ts:
        for block in range(part.shape[0]):
            coords[:, place * LANES : (place + 1) * LANES] = part[block, :feat, :]
            place += 1
    total = taug.shape[0]
    right = xaug[:, : p_ref.shape[1]]
    s = spread_rows(taug, right, p_ref, lambda rows: None)
    weight = 1.0 / s
    for begin in range(0, total, LANES):
        rows = slice(begin, begin + LANES)
        plan_ref[rows, :] = (p_ref[rows, :] * weight).astype(jnp.bfloat16)

    @pl.when(jnp.logical_not(jnp.min(s) >= SMALL_ROW))
    def _():
        reach = min(total, 2048)
        peak = jnp.full(s.shape, FLOOR, jnp.float32)
        for begin in range(0, total, reach):
            rows = slice(begin, begin + reach)
            p_ref[rows, :] = exponents(taug[rows, :], right)
            peak = jnp.maximum(peak, jnp.max(p_ref[rows, :], axis=0, keepdims=True))
        sums = jnp.zeros(s.shape, jnp.float32)
        for begin in range(0, total, reach):
            rows = slice(begin, begin + reach)
            sums += jnp.sum(jnp.exp2(p_ref[rows, :] - peak), axis=0, keepdims=True)
        shift = peak + jnp.log2(sums)
        for begin in range(0, total, reach):
            rows = slice(begin, begin + reach)
            plan_ref[rows, :] = jnp.exp2(p_ref[rows, :] - shift).astype(jnp.bfloat16)

    mapped_ref[...] = jnp.dot(coords[...], plan_ref[...], preferred_element_type=jnp.float32)


def swap(value, count, step):
    return lax.ppermute(value, AXIS, [(source, source ^ step) for source in range(count)])


def chip_stages(count):
    high, stages = count.bit_length() - 1, []
    while high > 1:
        width = min(2, high - 1)
        stages.append((high - width, width))
        high -= width
    return stages


def gather_chips(block, count):
    parts = [block[None]]
    for low, width in chip_stages(count):
        held = parts[0] if len(parts) == 1 else jnp.concatenate(parts, axis=0)
        digits = range((1 << width) - 1, 0, -1)
        parts = [held] + [swap(held, count, digit << low) for digit in digits]
    return parts


def on_device(source_points, target_points, source_logw, target_logw, inverse_eps, count):
    feat, own_sources = source_points.shape
    own_targets = target_points.shape[1]
    extra_rows = own_sources // LANES
    pad = -(1 + extra_rows) % 16
    packed = jnp.concatenate(
        [
            target_points,
            target_logw[None, :],
            source_logw.reshape(extra_rows, LANES),
            jnp.zeros((pad, own_targets), target_points.dtype),
        ],
        axis=0,
    )
    f32, bf16 = jnp.float32, jnp.bfloat16
    total, chips = count * own_targets, count // 2
    small = total <= 4096
    width = 2 * LANES if small else LANES
    vmem = pl.BlockSpec(memory_space=pltpu.VMEM)
    smem = pl.BlockSpec(memory_space=pltpu.SMEM)
    params = pltpu.CompilerParams(vmem_limit_bytes=(24 if small else 63) << 20)
    line = jax.ShapeDtypeStruct((1, total), f32)

    def call(kernel, operands, outs, scratch=(), scalars=1):
        return pl.pallas_call(
            kernel,
            out_shape=outs,
            in_specs=[smem] * scalars + [vmem] * (len(operands) - scalars),
            out_specs=[vmem] * len(outs),
            scratch_shapes=list(scratch),
            compiler_params=params,
        )(*operands)

    def staged_shape(parts):
        rows = sum(part.shape[0] for part in parts) * own_targets
        return jax.ShapeDtypeStruct((rows, DEPTH), bf16)

    def logw_line(parts):
        rows = [part[:, feat + 1 : feat + 1 + extra_rows] for part in parts]
        return jnp.concatenate(rows, axis=0).reshape(1, -1).astype(f32)

    mine = gather_chips(packed, count)
    theirs = [swap(part, count, 1) for part in mine]
    first, second, late = [mine[0]], mine[1:] + theirs[:1], theirs[1:]
    ts = first + second + late
    taug_first, points = call(
        functools.partial(part_kernel, len(first), feat),
        [inverse_eps, source_points] + first,
        [staged_shape(first), jax.ShapeDtypeStruct((1, feat, own_sources), bf16)],
    )
    (taug_second,) = call(
        functools.partial(more_kernel, len(second), feat),
        [inverse_eps] + second,
        [staged_shape(second)],
    )
    xs = gather_chips(points[0], count)
    near, far = xs[:1], xs[1:]
    near_logws, far_logws = logw_line(mine[:1]), logw_line(mine[1:])
    near_rows, far_rows = near_logws.shape[1], far_logws.shape[1]

    p_scratch = pltpu.VMEM((total, width), f32)
    p_pair = [p_scratch, p_scratch if small else pltpu.VMEM((8, LANES), f32)]
    col_scratch = pltpu.VMEM((total, LANES), f32)
    near_xaug, taug, near_col, near_least, logw, q = call(
        functools.partial(near_kernel, len(near), 2, len(ts), len(late), feat),
        [inverse_eps, near_logws] + near + [taug_first, taug_second] + ts,
        [
            jax.ShapeDtypeStruct((DEPTH, near_rows), bf16),
            jax.ShapeDtypeStruct((total, DEPTH), bf16),
            jax.ShapeDtypeStruct((total, LANES), f32),
            jax.ShapeDtypeStruct((1, width), f32),
            line,
            line,
        ],
        p_pair,
    )
    far_xaug, sums = call(
        functools.partial(far_kernel, len(far)),
        [inverse_eps, near_logws, far_logws, near_xaug, taug, near_col, near_least] + far,
        [jax.ShapeDtypeStruct((DEPTH, far_rows), bf16), line],
        p_pair + [col_scratch],
    )
    g = logw
    for _ in range(ITERS - 1):
        lines = [sums, swap(sums, count, 1), g, q, logw]
        sums, g = call(
            next_kernel,
            [near_logws, far_logws, near_xaug, far_xaug, taug] + lines,
            [line, line],
            [pltpu.VMEM((total, DEPTH), bf16)] + p_pair + [col_scratch],
            scalars=0,
        )
    lines = [sums, swap(sums, count, 1), g, q, logw]
    mapped, potential = call(
        functools.partial(map_kernel, len(ts), feat),
        [near_xaug, taug] + lines + ts,
        [
            jax.ShapeDtypeStruct((feat, own_sources), f32),
            jax.ShapeDtypeStruct((1, own_targets), f32),
        ],
        [
            pltpu.VMEM((total, DEPTH), bf16),
            pltpu.VMEM((total, own_sources), f32),
            pltpu.VMEM((total, own_sources), bf16),
            pltpu.VMEM((feat, total), bf16),
        ],
        scalars=0,
    )
    return (mapped, potential.reshape(own_targets))


def solution(mesh):
    count = mesh.shape[AXIS]
    placed = (
        P(None, ("grp", "wide")),
        P(None, ("grp", "wide")),
        P(("grp", "wide")),
        P(("grp", "wide")),
        P(),
    )

    def body(*blocks):
        return on_device(*blocks, count)

    return jax.shard_map(
        body,
        mesh=mesh,
        in_specs=placed,
        out_specs=(P(None, ("grp", "wide")), P(("grp", "wide"))),
        check_vma=False,
    )
```

```python
import functools
import math

import jax
import jax.numpy as jnp
from jax import lax
from jax.experimental import pallas as pl
from jax.experimental.pallas import tpu as pltpu
from jax.sharding import PartitionSpec as P

ITERS = 2
AXIS = "wide"
LOG2E = math.log2(math.e)
LANES = 128
DEPTH = 256
SMALL_ROW = 2.0**-64
SMALL_COL = 2.0**-32
LARGE_COL = 2.0**100
FLOOR = -1e30


def three_terms(value):
    high = value.astype(jnp.bfloat16)
    rest = value - high.astype(jnp.float32)
    middle = rest.astype(jnp.bfloat16)
    low = (rest - middle.astype(jnp.float32)).astype(jnp.bfloat16)
    return high, middle, low


def pick_rows(shape, rows):
    index = lax.broadcasted_iota(jnp.int32, shape, 0)
    out = jnp.zeros(shape, jnp.float32)
    for place, row in enumerate(rows):
        out = jnp.where(index == place, row, out)
    return out


def stage_source(points, scale, xaug, at):
    feat, count = points.shape
    wide = points.astype(jnp.float32)
    shift = scale * jnp.sum(wide * wide, axis=0, keepdims=True)
    shift = shift.astype(jnp.bfloat16).astype(jnp.float32)
    xaug[0:feat, at] = pick_rows((feat, count), [1.0, 1.0, 1.0, -shift]).astype(jnp.bfloat16)
    for place, term in enumerate(three_terms(2.0 * scale * wide)):
        xaug[(place + 1) * feat : (place + 2) * feat, at] = term


def stage_sources(parts, scale, xaug, begin=0):
    for part in parts:
        count = part.shape[2]
        for block in range(part.shape[0]):
            stage_source(part[block], scale, xaug, slice(begin, begin + count))
            begin += count


def target_lines(part, block, scale, feat):
    wide = part[block, :feat, :].astype(jnp.float32)
    logw = part[block, feat : feat + 16, :].astype(jnp.float32)[0:1]
    return scale * jnp.sum(wide * wide, axis=0, keepdims=True), logw * LOG2E


def stage_targets(parts, scale, taug, begin, feat):
    for part in parts:
        for block in range(part.shape[0]):
            q, logw = target_lines(part, block, scale, feat)
            terms = [term.astype(jnp.float32) for term in three_terms(logw - q)]
            extras = pick_rows((feat, LANES), terms + [1.0])
            wide = part[block, :feat, :].astype(jnp.float32)
            turned = jnp.concatenate([extras, wide], axis=0).T
            lane = lax.broadcasted_iota(jnp.int32, turned.shape, 1)
            twice = jnp.where(lane < feat, pltpu.roll(turned, feat, 1), turned)
            taug[begin : begin + LANES, 0:LANES] = turned.astype(jnp.bfloat16)
            taug[begin : begin + LANES, LANES:DEPTH] = twice.astype(jnp.bfloat16)
            begin += LANES


def renew_targets(lines, flips, parts, g, q, logw, taug):
    total = lines[0].shape[1]
    size = total // (2 * parts)
    held = []
    for line, (core, digit) in zip(lines, flips):
        value = line[...]
        places = [(block ^ (core * parts)) ^ digit for block in range(2 * parts)]
        pieces = [value[:, place * size : (place + 1) * size] for place in places]
        held.append(jnp.concatenate(pieces, axis=1))
    peak = functools.reduce(jnp.maximum, held)
    added = functools.reduce(jnp.add, [jnp.exp2(value - peak) for value in held])
    potential = g - (peak + jnp.log2(added))
    g = potential + logw
    terms = [term.astype(jnp.float32) for term in three_terms(g - jnp.max(g) - q)]
    for begin in range(0, total, LANES):
        rows = slice(begin, begin + LANES)
        extras = pick_rows((8, LANES), [term[:, rows] for term in terms] + [1.0])
        taug[rows, 0:8] = extras.T.astype(jnp.bfloat16)
    return potential, g


def exponents(left, right):
    return jnp.dot(left, right, preferred_element_type=jnp.float32)


def spread_rows(taug, right, p_ref, beside):
    total, width = taug.shape[0], right.shape[1]
    reach = min(total, 512)
    sums = jnp.zeros((8, width), jnp.float32)
    for begin in range(0, total, reach):
        e = exponents(taug[begin : begin + reach, :], right)
        for inner in range(0, reach, LANES):
            rows = slice(begin + inner, begin + inner + LANES)
            beside(rows)
            p = jnp.exp2(e[inner : inner + LANES])
            p_ref[rows, :] = p
            sums = sums + jnp.sum(p.reshape(LANES // 8, 8, width), axis=0)
    return jnp.sum(sums, axis=0, keepdims=True)


def add_columns(p_ref, weight, col_ref, rows):
    width = weight.shape[1]
    added = p_ref[rows, 0:LANES] * weight[:, 0:LANES]
    for lane in range(LANES, width, LANES):
        added = added + p_ref[rows, lane : lane + LANES] * weight[:, lane : lane + LANES]
    col_ref[rows, :] += added


def tile_columns(tile, width):
    if isinstance(tile, int):
        return pl.ds(tile * width, width)
    return pl.ds(pl.multiple_of(tile * width, width), width)


def add_sources(xaug, logws, taug, p_refs, col_ref):
    total = taug.shape[0]
    width = p_refs[0].shape[1]
    tiles = xaug.shape[1] // width
    if p_refs[1].shape != p_refs[0].shape:
        p_refs = (p_refs[0], p_refs[0])

    def step(tile, slot, held):
        def beside(rows):
            if held is not None:
                add_columns(p_refs[1 - slot], held, col_ref, rows)

        at = tile_columns(tile, width)
        s = spread_rows(taug, xaug[:, at], p_refs[slot], beside)
        return s, jnp.exp2(logws[:, at] * LOG2E) / s

    def two_steps(pair, carry):
        least, weight = carry
        s1, weight1 = step(2 * pair + 1, 1, weight)
        s0, weight0 = step(2 * pair + 2, 0, weight1)
        return jnp.minimum(least, jnp.minimum(s0, s1)), weight0

    s, weight = step(0, 0, None)
    least, weight = lax.fori_loop(0, tiles // 2 - 1, two_steps, (s, weight))
    s, weight = step(tiles - 1, 1, weight)
    for begin in range(0, total, LANES):
        add_columns(p_refs[1], weight, col_ref, slice(begin, begin + LANES))
    return jnp.minimum(least, s)


def lane_totals(col_ref, out_ref):
    total = col_ref.shape[0]
    reach = min(total, 2048)
    ones = jnp.ones((16, 2 * LANES), jnp.bfloat16)
    for begin in range(0, total, reach):
        high, middle, _ = three_terms(col_ref[begin : begin + reach, :])
        both = jnp.concatenate([high, middle], axis=1)
        added = lax.dot_general(
            ones, both, (((1,), (1,)), ((), ())), preferred_element_type=jnp.float32
        )
        out_ref[:, begin : begin + reach] = added[0:1]


def finish_sums(xaug, logws, taug, least, p_ref, col_ref, out_ref):
    total = taug.shape[0]
    lane_totals(col_ref, out_ref)
    cols = out_ref[...]
    out_ref[...] = jnp.log2(cols)
    fine = jnp.logical_and(
        jnp.min(least) >= SMALL_ROW,
        jnp.logical_and(jnp.min(cols) >= SMALL_COL, jnp.max(cols) <= LARGE_COL),
    )

    top_ref = p_ref.at[:, 0:LANES]

    @pl.when(jnp.logical_not(fine))
    def _():
        col_ref[...] = jnp.zeros_like(col_ref)
        top_ref[...] = jnp.full_like(top_ref, FLOOR)
        blocks = total // LANES

        def block_rows(block):
            return pl.ds(pl.multiple_of(block * LANES, LANES), LANES)

        def careful(tile, carry):
            at = tile_columns(tile, LANES)
            right = xaug[:, at]

            def highest(block, peak):
                e = exponents(taug[block_rows(block), :], right)
                return jnp.maximum(peak, jnp.max(e, axis=0, keepdims=True))

            peak = lax.fori_loop(0, blocks, highest, jnp.full((1, LANES), FLOOR, jnp.float32))

            def summed(block, s):
                e = exponents(taug[block_rows(block), :], right)
                return s + jnp.sum(jnp.exp2(e - peak), axis=0, keepdims=True)

            s = lax.fori_loop(0, blocks, summed, jnp.zeros((1, LANES), jnp.float32))
            shift = logws[:, at] * LOG2E - peak - jnp.log2(s)

            def collected(block, carry):
                rows = block_rows(block)
                term = exponents(taug[rows, :], right) + shift
                old = top_ref[rows, :]
                top = jnp.maximum(old, term)
                col_ref[rows, :] = col_ref[rows, :] * jnp.exp2(old - top) + jnp.exp2(term - top)
                top_ref[rows, :] = top
                return carry

            return lax.fori_loop(0, blocks, collected, carry)

        lax.fori_loop(0, xaug.shape[1] // LANES, careful, 0)

        def turned(block, carry):
            rows = block_rows(block)
            tops = top_ref[rows, :].T
            top = jnp.max(tops, axis=0, keepdims=True)
            added = jnp.sum(col_ref[rows, :].T * jnp.exp2(tops - top), axis=0, keepdims=True)
            out_ref[:, rows] = top + jnp.log2(added)
            return carry

        lax.fori_loop(0, blocks, turned, 0)


def part_kernel(feat, inverse, *refs):
    stage_targets(refs[:-1], inverse[0] * LOG2E, refs[-1], 0, feat)


def part_copy_kernel(feat, inverse, points, *refs):
    ts, (taug, copy_ref) = refs[:-2], refs[-2:]
    copy_ref[...] = points[...]
    stage_targets(ts, inverse[0] * LOG2E, taug, 0, feat)


def near_kernel(parts, feat, inverse, logws, xs, mine, rest, theirs, *refs):
    ts, refs = refs[: 2 * parts], refs[2 * parts :]
    xaug, taug, out_ref, g_ref, q_ref, p0, p1, col_ref = refs
    scale = inverse[0] * LOG2E
    stage_sources([xs], scale, xaug)
    place = 0
    for part in ts:
        for block in range(part.shape[0]):
            at = slice(place * LANES, (place + 1) * LANES)
            q_ref[:, at], g_ref[:, at] = target_lines(part, block, scale, feat)
            place += 1
    begin = 0
    for part in (mine, rest, theirs):
        taug[begin : begin + part.shape[0], :] = part[...]
        begin += part.shape[0]
    stage_targets(ts[parts + 1 :], scale, taug, begin, feat)
    col_ref[...] = jnp.zeros_like(col_ref)
    least = add_sources(xaug, logws, taug, (p0, p1), col_ref)
    finish_sums(xaug, logws, taug, least, p0, col_ref, out_ref)


def far_kernel(inverse, near_xaug, *refs):
    xs, xaug = refs[:-1], refs[-1]
    begin = near_xaug.shape[1]
    xaug[:, 0:begin] = near_xaug[...]
    stage_sources(xs, inverse[0] * LOG2E, xaug, begin)


def next_kernel(flips, parts, logws, xaug, old, g, q, logw, *refs):
    lines, refs = refs[: len(flips)], refs[len(flips) :]
    out_ref, g_ref, taug, p0, p1, col_ref = refs
    taug[...] = old[...]
    g_ref[...] = renew_targets(lines, flips, parts, g[...], q[...], logw[...], taug)[1]
    col_ref[...] = jnp.zeros_like(col_ref)
    least = add_sources(xaug, logws, taug, (p0, p1), col_ref)
    finish_sums(xaug, logws, taug, least, p0, col_ref, out_ref)


def map_kernel(flips, parts, n_t, feat, xaug, old, g, q, logw, *refs):
    lines, refs = refs[: len(flips)], refs[len(flips) :]
    ts = refs[:n_t]
    mapped_ref, pot_ref, taug, p_ref, plan_ref, coords = refs[n_t:]
    taug[...] = old[...]
    potential = renew_targets(lines, flips, parts, g[...], q[...], logw[...], taug)[0]
    pot_ref[...] = potential[:, :LANES] * (1.0 / LOG2E)
    place = 0
    for part in ts:
        for block in range(part.shape[0]):
            coords[:, place * LANES : (place + 1) * LANES] = part[block, :feat, :]
            place += 1
    total = taug.shape[0]
    right = xaug[:, : p_ref.shape[1]]
    s = spread_rows(taug, right, p_ref, lambda rows: None)
    weight = 1.0 / s
    for begin in range(0, total, LANES):
        rows = slice(begin, begin + LANES)
        plan_ref[rows, :] = (p_ref[rows, :] * weight).astype(jnp.bfloat16)

    @pl.when(jnp.logical_not(jnp.min(s) >= SMALL_ROW))
    def _():
        reach = min(total, 2048)
        peak = jnp.full(s.shape, FLOOR, jnp.float32)
        for begin in range(0, total, reach):
            rows = slice(begin, begin + reach)
            p_ref[rows, :] = exponents(taug[rows, :], right)
            peak = jnp.maximum(peak, jnp.max(p_ref[rows, :], axis=0, keepdims=True))
        sums = jnp.zeros(s.shape, jnp.float32)
        for begin in range(0, total, reach):
            rows = slice(begin, begin + reach)
            sums += jnp.sum(jnp.exp2(p_ref[rows, :] - peak), axis=0, keepdims=True)
        shift = peak + jnp.log2(sums)
        for begin in range(0, total, reach):
            rows = slice(begin, begin + reach)
            plan_ref[rows, :] = jnp.exp2(p_ref[rows, :] - shift).astype(jnp.bfloat16)

    mapped_ref[...] = jnp.dot(coords[...], plan_ref[...], preferred_element_type=jnp.float32)


def swap(value, count, step):
    return lax.ppermute(value, AXIS, [(source, source ^ step) for source in range(count)])


def chip_stages(count):
    high, stages = count.bit_length() - 1, []
    while high > 1:
        width = min(2, high - 1)
        stages.append((high - width, width))
        high -= width
    return stages


def gather_chips(block, count):
    parts = [block[None]]
    for low, width in chip_stages(count):
        held = parts[0] if len(parts) == 1 else jnp.concatenate(parts, axis=0)
        parts = [held] + [swap(held, count, digit << low) for digit in range(1, 1 << width)]
    return parts


def on_device(source_points, target_points, source_logw, target_logw, inverse_eps, count):
    feat, own_sources = source_points.shape
    own_targets = target_points.shape[1]
    extra_rows = own_sources // LANES
    pad = -(1 + extra_rows) % 16
    packed = jnp.concatenate(
        [
            target_points,
            target_logw[None, :],
            source_logw.reshape(extra_rows, LANES),
            jnp.zeros((pad, own_targets), target_points.dtype),
        ],
        axis=0,
    )
    f32, bf16 = jnp.float32, jnp.bfloat16
    total, chips = count * own_targets, count // 2
    small = total <= 4096
    width = 2 * LANES if small else LANES
    vmem = pl.BlockSpec(memory_space=pltpu.VMEM)
    smem = pl.BlockSpec(memory_space=pltpu.SMEM)
    params = pltpu.CompilerParams(vmem_limit_bytes=(24 if small else 63) << 20)
    line = jax.ShapeDtypeStruct((1, total), f32)

    def call(kernel, operands, outs, scratch=(), scalars=1):
        return pl.pallas_call(
            kernel,
            out_shape=outs,
            in_specs=[smem] * scalars + [vmem] * (len(operands) - scalars),
            out_specs=[vmem] * len(outs),
            scratch_shapes=list(scratch),
            compiler_params=params,
        )(*operands)

    def staged_shape(parts):
        rows = sum(part.shape[0] for part in parts) * own_targets
        return jax.ShapeDtypeStruct((rows, DEPTH), bf16)

    def logw_line(parts):
        rows = [part[:, feat + 1 : feat + 1 + extra_rows] for part in parts]
        return jnp.concatenate(rows, axis=0).reshape(1, -1).astype(f32)

    mine = gather_chips(packed, count)
    theirs = [swap(part, count, 1) for part in mine]
    parts, low = len(mine), chip_stages(count)[-1][0]
    ts = mine + theirs
    (taug_mine,) = call(
        functools.partial(part_kernel, feat),
        [inverse_eps, mine[0]],
        [staged_shape(mine[:1])],
    )
    taug_theirs, points = call(
        functools.partial(part_copy_kernel, feat),
        [inverse_eps, source_points, theirs[0]],
        [staged_shape(theirs[:1]), jax.ShapeDtypeStruct((feat, own_sources), bf16)],
    )
    (taug_rest,) = call(
        functools.partial(part_kernel, feat),
        [inverse_eps] + mine[1:],
        [staged_shape(mine[1:])],
    )
    xs = gather_chips(points, count)
    logws = logw_line(mine)
    near_rows, rows = xs[0].shape[0] * own_sources, chips * own_sources

    p_scratch = pltpu.VMEM((total, width), f32)
    scratch = [
        p_scratch,
        p_scratch if small else pltpu.VMEM((8, LANES), f32),
        pltpu.VMEM((total, LANES), f32),
    ]
    near_xaug, taug, sums, logw, q = call(
        functools.partial(near_kernel, parts, feat),
        [inverse_eps, logws, xs[0], taug_mine, taug_rest, taug_theirs] + ts,
        [
            jax.ShapeDtypeStruct((DEPTH, near_rows), bf16),
            jax.ShapeDtypeStruct((total, DEPTH), bf16),
            line,
            line,
            line,
        ],
        scratch,
    )
    (xaug,) = call(
        far_kernel,
        [inverse_eps, near_xaug] + xs[1:],
        [jax.ShapeDtypeStruct((DEPTH, rows), bf16)],
    )
    lines = [sums] + [swap(sums, count, digit << low) for digit in range(1, parts)]
    lines = lines + [swap(line_, count, 1) for line_ in lines]
    flips = [(core, digit) for core in range(2) for digit in range(parts)]
    g = logw
    for _ in range(ITERS - 1):
        sums, g = call(
            functools.partial(next_kernel, flips, parts),
            [logws, xaug, taug, g, q, logw] + lines,
            [line, line],
            [pltpu.VMEM((total, DEPTH), bf16)] + scratch,
            scalars=0,
        )
        lines, flips = [sums, swap(sums, count, 1)], [(0, 0), (1, 0)]
    mapped, potential = call(
        functools.partial(map_kernel, flips, parts, len(ts), feat),
        [near_xaug, taug, g, q, logw] + lines + ts,
        [
            jax.ShapeDtypeStruct((feat, own_sources), f32),
            jax.ShapeDtypeStruct((1, own_targets), f32),
        ],
        [
            pltpu.VMEM((total, DEPTH), bf16),
            pltpu.VMEM((total, own_sources), f32),
            pltpu.VMEM((total, own_sources), bf16),
            pltpu.VMEM((feat, total), bf16),
        ],
        scalars=0,
    )
    return (mapped, potential.reshape(own_targets))


def solution(mesh):
    count = mesh.shape[AXIS]
    placed = (
        P(None, ("grp", "wide")),
        P(None, ("grp", "wide")),
        P(("grp", "wide")),
        P(("grp", "wide")),
        P(),
    )

    def body(*blocks):
        return on_device(*blocks, count)

    return jax.shard_map(
        body,
        mesh=mesh,
        in_specs=placed,
        out_specs=(P(None, ("grp", "wide")), P(("grp", "wide"))),
        check_vma=False,
    )
```

```python
import functools
import math

import jax
import jax.numpy as jnp
from jax import lax
from jax.experimental import pallas as pl
from jax.experimental.pallas import tpu as pltpu
from jax.sharding import PartitionSpec as P

ITERS = 2
AXIS = "wide"
LOG2E = math.log2(math.e)
LANES = 128
DEPTH = 256
SMALL_ROW = 2.0**-64
SMALL_COL = 2.0**-32
LARGE_COL = 2.0**100
FLOOR = -1e30


def three_terms(value):
    high = value.astype(jnp.bfloat16)
    rest = value - high.astype(jnp.float32)
    middle = rest.astype(jnp.bfloat16)
    low = (rest - middle.astype(jnp.float32)).astype(jnp.bfloat16)
    return high, middle, low


def pick_rows(shape, rows):
    index = lax.broadcasted_iota(jnp.int32, shape, 0)
    out = jnp.zeros(shape, jnp.float32)
    for place, row in enumerate(rows):
        out = jnp.where(index == place, row, out)
    return out


def stage_source(points, scale, xaug, at):
    feat, count = points.shape
    wide = points.astype(jnp.float32)
    shift = scale * jnp.sum(wide * wide, axis=0, keepdims=True)
    shift = shift.astype(jnp.bfloat16).astype(jnp.float32)
    xaug[0:feat, at] = pick_rows((feat, count), [1.0, 1.0, 1.0, -shift]).astype(jnp.bfloat16)
    for place, term in enumerate(three_terms(2.0 * scale * wide)):
        xaug[(place + 1) * feat : (place + 2) * feat, at] = term


def stage_sources(parts, scale, xaug, begin=0):
    for part in parts:
        count = part.shape[2]
        for block in range(part.shape[0]):
            stage_source(part[block], scale, xaug, slice(begin, begin + count))
            begin += count


def target_lines(part, block, scale, feat):
    wide = part[block, :feat, :].astype(jnp.float32)
    logw = part[block, feat : feat + 16, :].astype(jnp.float32)[0:1]
    return scale * jnp.sum(wide * wide, axis=0, keepdims=True), logw * LOG2E


def stage_targets(parts, scale, taug, begin, feat):
    for part in parts:
        for block in range(part.shape[0]):
            q, logw = target_lines(part, block, scale, feat)
            terms = [term.astype(jnp.float32) for term in three_terms(logw - q)]
            extras = pick_rows((feat, LANES), terms + [1.0])
            wide = part[block, :feat, :].astype(jnp.float32)
            turned = jnp.concatenate([extras, wide], axis=0).T
            lane = lax.broadcasted_iota(jnp.int32, turned.shape, 1)
            twice = jnp.where(lane < feat, pltpu.roll(turned, feat, 1), turned)
            taug[begin : begin + LANES, 0:LANES] = turned.astype(jnp.bfloat16)
            taug[begin : begin + LANES, LANES:DEPTH] = twice.astype(jnp.bfloat16)
            begin += LANES


def renew_targets(lines, flips, parts, g, q, logw, taug):
    total = lines[0].shape[1]
    size = total // (2 * parts)
    held = []
    for line, (core, digit) in zip(lines, flips):
        value = line[...]
        places = [(block ^ (core * parts)) ^ digit for block in range(2 * parts)]
        pieces = [value[:, place * size : (place + 1) * size] for place in places]
        held.append(jnp.concatenate(pieces, axis=1))
    peak = functools.reduce(jnp.maximum, held)
    added = functools.reduce(jnp.add, [jnp.exp2(value - peak) for value in held])
    potential = g - (peak + jnp.log2(added))
    g = potential + logw
    terms = [term.astype(jnp.float32) for term in three_terms(g - jnp.max(g) - q)]
    for begin in range(0, total, LANES):
        rows = slice(begin, begin + LANES)
        extras = pick_rows((8, LANES), [term[:, rows] for term in terms] + [1.0])
        taug[rows, 0:8] = extras.T.astype(jnp.bfloat16)
    return potential, g


def exponents(left, right):
    return jnp.dot(left, right, preferred_element_type=jnp.float32)


def spread_rows(taug, right, p_ref, beside):
    total, width = taug.shape[0], right.shape[1]
    reach = min(total, 512)
    sums = jnp.zeros((8, width), jnp.float32)
    for begin in range(0, total, reach):
        e = exponents(taug[begin : begin + reach, :], right)
        for inner in range(0, reach, LANES):
            rows = slice(begin + inner, begin + inner + LANES)
            beside(rows)
            p = jnp.exp2(e[inner : inner + LANES])
            p_ref[rows, :] = p
            sums = sums + jnp.sum(p.reshape(LANES // 8, 8, width), axis=0)
    return jnp.sum(sums, axis=0, keepdims=True)


def add_columns(p_ref, weight, col_ref, rows):
    width = weight.shape[1]
    added = p_ref[rows, 0:LANES] * weight[:, 0:LANES]
    for lane in range(LANES, width, LANES):
        added = added + p_ref[rows, lane : lane + LANES] * weight[:, lane : lane + LANES]
    col_ref[rows, :] += added


def tile_columns(tile, width):
    if isinstance(tile, int):
        return pl.ds(tile * width, width)
    return pl.ds(pl.multiple_of(tile * width, width), width)


def add_sources(xaug, logws, taug, p_refs, col_ref):
    total = taug.shape[0]
    width = p_refs[0].shape[1]
    tiles = xaug.shape[1] // width
    if p_refs[1].shape != p_refs[0].shape:
        p_refs = (p_refs[0], p_refs[0])

    def step(tile, slot, held):
        def beside(rows):
            if held is not None:
                add_columns(p_refs[1 - slot], held, col_ref, rows)

        at = tile_columns(tile, width)
        s = spread_rows(taug, xaug[:, at], p_refs[slot], beside)
        return s, jnp.exp2(logws[:, at] * LOG2E) / s

    def two_steps(pair, carry):
        least, weight = carry
        s1, weight1 = step(2 * pair + 1, 1, weight)
        s0, weight0 = step(2 * pair + 2, 0, weight1)
        return jnp.minimum(least, jnp.minimum(s0, s1)), weight0

    s, weight = step(0, 0, None)
    least, weight = lax.fori_loop(0, tiles // 2 - 1, two_steps, (s, weight))
    s, weight = step(tiles - 1, 1, weight)
    for begin in range(0, total, LANES):
        add_columns(p_refs[1], weight, col_ref, slice(begin, begin + LANES))
    return jnp.minimum(least, s)


def lane_totals(col_ref, out_ref):
    total = col_ref.shape[0]
    reach = min(total, 2048)
    ones = jnp.ones((16, 2 * LANES), jnp.bfloat16)
    for begin in range(0, total, reach):
        high, middle, _ = three_terms(col_ref[begin : begin + reach, :])
        both = jnp.concatenate([high, middle], axis=1)
        added = lax.dot_general(
            ones, both, (((1,), (1,)), ((), ())), preferred_element_type=jnp.float32
        )
        out_ref[:, begin : begin + reach] = added[0:1]


def finish_sums(xaug, logws, taug, least, p_ref, col_ref, out_ref):
    total = taug.shape[0]
    lane_totals(col_ref, out_ref)
    cols = out_ref[...]
    out_ref[...] = jnp.log2(cols)
    fine = jnp.logical_and(
        jnp.min(least) >= SMALL_ROW,
        jnp.logical_and(jnp.min(cols) >= SMALL_COL, jnp.max(cols) <= LARGE_COL),
    )

    top_ref = p_ref.at[:, 0:LANES]

    @pl.when(jnp.logical_not(fine))
    def _():
        col_ref[...] = jnp.zeros_like(col_ref)
        top_ref[...] = jnp.full_like(top_ref, FLOOR)
        blocks = total // LANES

        def block_rows(block):
            return pl.ds(pl.multiple_of(block * LANES, LANES), LANES)

        def careful(tile, carry):
            at = tile_columns(tile, LANES)
            right = xaug[:, at]

            def highest(block, peak):
                e = exponents(taug[block_rows(block), :], right)
                return jnp.maximum(peak, jnp.max(e, axis=0, keepdims=True))

            peak = lax.fori_loop(0, blocks, highest, jnp.full((1, LANES), FLOOR, jnp.float32))

            def summed(block, s):
                e = exponents(taug[block_rows(block), :], right)
                return s + jnp.sum(jnp.exp2(e - peak), axis=0, keepdims=True)

            s = lax.fori_loop(0, blocks, summed, jnp.zeros((1, LANES), jnp.float32))
            shift = logws[:, at] * LOG2E - peak - jnp.log2(s)

            def collected(block, carry):
                rows = block_rows(block)
                term = exponents(taug[rows, :], right) + shift
                old = top_ref[rows, :]
                top = jnp.maximum(old, term)
                col_ref[rows, :] = col_ref[rows, :] * jnp.exp2(old - top) + jnp.exp2(term - top)
                top_ref[rows, :] = top
                return carry

            return lax.fori_loop(0, blocks, collected, carry)

        lax.fori_loop(0, xaug.shape[1] // LANES, careful, 0)

        def turned(block, carry):
            rows = block_rows(block)
            tops = top_ref[rows, :].T
            top = jnp.max(tops, axis=0, keepdims=True)
            added = jnp.sum(col_ref[rows, :].T * jnp.exp2(tops - top), axis=0, keepdims=True)
            out_ref[:, rows] = top + jnp.log2(added)
            return carry

        lax.fori_loop(0, blocks, turned, 0)


def part_kernel(feat, inverse, *refs):
    stage_targets(refs[:-1], inverse[0] * LOG2E, refs[-1], 0, feat)


def part_copy_kernel(feat, inverse, points, *refs):
    ts, (taug, copy_ref) = refs[:-2], refs[-2:]
    copy_ref[...] = points[...]
    stage_targets(ts, inverse[0] * LOG2E, taug, 0, feat)


def near_kernel(parts, feat, inverse, logws, xs, mine, rest, theirs, *refs):
    ts, refs = refs[: 2 * parts], refs[2 * parts :]
    xaug, taug, out_ref, g_ref, q_ref, p0, p1, col_ref = refs
    scale = inverse[0] * LOG2E
    stage_sources([xs], scale, xaug)
    place = 0
    for part in ts:
        for block in range(part.shape[0]):
            at = slice(place * LANES, (place + 1) * LANES)
            q_ref[:, at], g_ref[:, at] = target_lines(part, block, scale, feat)
            place += 1
    begin = 0
    for part in (mine, rest, theirs):
        taug[begin : begin + part.shape[0], :] = part[...]
        begin += part.shape[0]
    stage_targets(ts[parts + 1 :], scale, taug, begin, feat)
    col_ref[...] = jnp.zeros_like(col_ref)
    least = add_sources(xaug, logws, taug, (p0, p1), col_ref)
    finish_sums(xaug, logws, taug, least, p0, col_ref, out_ref)


def next_kernel(flips, parts, logws, xaug, old, g, q, logw, *refs):
    lines, refs = refs[: len(flips)], refs[len(flips) :]
    out_ref, g_ref, taug, p0, p1, col_ref = refs
    taug[...] = old[...]
    g_ref[...] = renew_targets(lines, flips, parts, g[...], q[...], logw[...], taug)[1]
    col_ref[...] = jnp.zeros_like(col_ref)
    least = add_sources(xaug, logws, taug, (p0, p1), col_ref)
    finish_sums(xaug, logws, taug, least, p0, col_ref, out_ref)


def map_kernel(flips, parts, n_t, feat, xaug, old, g, q, logw, *refs):
    lines, refs = refs[: len(flips)], refs[len(flips) :]
    ts = refs[:n_t]
    mapped_ref, pot_ref, taug, p_ref, plan_ref, coords = refs[n_t:]
    taug[...] = old[...]
    potential = renew_targets(lines, flips, parts, g[...], q[...], logw[...], taug)[0]
    pot_ref[...] = potential[:, :LANES] * (1.0 / LOG2E)
    place = 0
    for part in ts:
        for block in range(part.shape[0]):
            coords[:, place * LANES : (place + 1) * LANES] = part[block, :feat, :]
            place += 1
    total = taug.shape[0]
    right = xaug[:, : p_ref.shape[1]]
    s = spread_rows(taug, right, p_ref, lambda rows: None)
    weight = 1.0 / s
    for begin in range(0, total, LANES):
        rows = slice(begin, begin + LANES)
        plan_ref[rows, :] = (p_ref[rows, :] * weight).astype(jnp.bfloat16)

    @pl.when(jnp.logical_not(jnp.min(s) >= SMALL_ROW))
    def _():
        reach = min(total, 2048)
        peak = jnp.full(s.shape, FLOOR, jnp.float32)
        for begin in range(0, total, reach):
            rows = slice(begin, begin + reach)
            p_ref[rows, :] = exponents(taug[rows, :], right)
            peak = jnp.maximum(peak, jnp.max(p_ref[rows, :], axis=0, keepdims=True))
        sums = jnp.zeros(s.shape, jnp.float32)
        for begin in range(0, total, reach):
            rows = slice(begin, begin + reach)
            sums += jnp.sum(jnp.exp2(p_ref[rows, :] - peak), axis=0, keepdims=True)
        shift = peak + jnp.log2(sums)
        for begin in range(0, total, reach):
            rows = slice(begin, begin + reach)
            plan_ref[rows, :] = jnp.exp2(p_ref[rows, :] - shift).astype(jnp.bfloat16)

    mapped_ref[...] = jnp.dot(coords[...], plan_ref[...], preferred_element_type=jnp.float32)


def swap(value, count, step):
    return lax.ppermute(value, AXIS, [(source, source ^ step) for source in range(count)])


def chip_stages(count):
    high, stages = count.bit_length() - 1, []
    while high > 1:
        width = min(2, high - 1)
        stages.append((high - width, width))
        high -= width
    return stages


def gather_stage(parts, count, low, width):
    held = parts[0] if len(parts) == 1 else jnp.concatenate(parts, axis=0)
    return [held] + [swap(held, count, digit << low) for digit in range(1, 1 << width)]


def gather_chips(block, count):
    parts = [block[None]]
    for low, width in chip_stages(count):
        parts = gather_stage(parts, count, low, width)
    return parts


def gather_line(block, count):
    parts = [block[None]]
    for low, width in chip_stages(count)[:-1]:
        parts = gather_stage(parts, count, low, width)
    return jnp.concatenate(parts, axis=0)


def on_device(source_points, target_points, source_logw, target_logw, inverse_eps, count):
    feat, own_sources = source_points.shape
    own_targets = target_points.shape[1]
    extra_rows = own_sources // LANES
    pad = -(1 + extra_rows) % 16
    packed = jnp.concatenate(
        [
            target_points,
            target_logw[None, :],
            source_logw.reshape(extra_rows, LANES),
            jnp.zeros((pad, own_targets), target_points.dtype),
        ],
        axis=0,
    )
    f32, bf16 = jnp.float32, jnp.bfloat16
    total = count * own_targets
    small = total <= 4096
    width = 2 * LANES if small else LANES
    vmem = pl.BlockSpec(memory_space=pltpu.VMEM)
    smem = pl.BlockSpec(memory_space=pltpu.SMEM)
    params = pltpu.CompilerParams(vmem_limit_bytes=(24 if small else 63) << 20)
    line = jax.ShapeDtypeStruct((1, total), f32)

    def call(kernel, operands, outs, scratch=(), scalars=1):
        return pl.pallas_call(
            kernel,
            out_shape=outs,
            in_specs=[smem] * scalars + [vmem] * (len(operands) - scalars),
            out_specs=[vmem] * len(outs),
            scratch_shapes=list(scratch),
            compiler_params=params,
        )(*operands)

    def staged_shape(parts):
        rows = sum(part.shape[0] for part in parts) * own_targets
        return jax.ShapeDtypeStruct((rows, DEPTH), bf16)

    def logw_line(parts):
        rows = [part[:, feat + 1 : feat + 1 + extra_rows] for part in parts]
        return jnp.concatenate(rows, axis=0).reshape(1, -1).astype(f32)

    mine = gather_chips(packed, count)
    theirs = [swap(part, count, 1) for part in mine]
    parts, low = len(mine), chip_stages(count)[-1][0]
    ts = mine + theirs
    (taug_mine,) = call(
        functools.partial(part_kernel, feat),
        [inverse_eps, mine[0]],
        [staged_shape(mine[:1])],
    )
    taug_theirs, points = call(
        functools.partial(part_copy_kernel, feat),
        [inverse_eps, source_points, theirs[0]],
        [staged_shape(theirs[:1]), jax.ShapeDtypeStruct((feat, own_sources), bf16)],
    )
    (taug_rest,) = call(
        functools.partial(part_kernel, feat),
        [inverse_eps] + mine[1:],
        [staged_shape(mine[1:])],
    )
    xs = gather_line(points, count)
    logws = logw_line(mine[:1])
    rows = logws.shape[1]

    p_scratch = pltpu.VMEM((total, width), f32)
    scratch = [
        p_scratch,
        p_scratch if small else pltpu.VMEM((8, LANES), f32),
        pltpu.VMEM((total, LANES), f32),
    ]
    xaug, taug, sums, logw, q = call(
        functools.partial(near_kernel, parts, feat),
        [inverse_eps, logws, xs, taug_mine, taug_rest, taug_theirs] + ts,
        [
            jax.ShapeDtypeStruct((DEPTH, rows), bf16),
            jax.ShapeDtypeStruct((total, DEPTH), bf16),
            line,
            line,
            line,
        ],
        scratch,
    )
    flips = [(core, digit) for core in range(2) for digit in range(parts)]

    def exchange(own):
        held = [own] + [swap(own, count, digit << low) for digit in range(1, parts)]
        return held + [swap(value, count, 1) for value in held]

    g = logw
    for _ in range(ITERS - 1):
        sums, g = call(
            functools.partial(next_kernel, flips, parts),
            [logws, xaug, taug, g, q, logw] + exchange(sums),
            [line, line],
            [pltpu.VMEM((total, DEPTH), bf16)] + scratch,
            scalars=0,
        )
    mapped, potential = call(
        functools.partial(map_kernel, flips, parts, len(ts), feat),
        [xaug if small else xaug[:, :own_sources], taug, g, q, logw] + exchange(sums) + ts,
        [
            jax.ShapeDtypeStruct((feat, own_sources), f32),
            jax.ShapeDtypeStruct((1, own_targets), f32),
        ],
        [
            pltpu.VMEM((total, DEPTH), bf16),
            pltpu.VMEM((total, own_sources), f32),
            pltpu.VMEM((total, own_sources), bf16),
            pltpu.VMEM((feat, total), bf16),
        ],
        scalars=0,
    )
    return (mapped, potential.reshape(own_targets))


def solution(mesh):
    count = mesh.shape[AXIS]
    placed = (
        P(None, ("grp", "wide")),
        P(None, ("grp", "wide")),
        P(("grp", "wide")),
        P(("grp", "wide")),
        P(),
    )

    def body(*blocks):
        return on_device(*blocks, count)

    return jax.shard_map(
        body,
        mesh=mesh,
        in_specs=placed,
        out_specs=(P(None, ("grp", "wide")), P(("grp", "wide"))),
        check_vma=False,
    )
```

```python
import functools
import math

import jax
import jax.numpy as jnp
from jax import lax
from jax.experimental import pallas as pl
from jax.experimental.pallas import tpu as pltpu
from jax.sharding import PartitionSpec as P

ITERS = 2
AXIS = "wide"
LOG2E = math.log2(math.e)
LANES = 128
DEPTH = 256
SMALL_ROW = 2.0**-64
SMALL_COL = 2.0**-32
LARGE_COL = 2.0**100
FLOOR = -1e30


def three_terms(value):
    high = value.astype(jnp.bfloat16)
    rest = value - high.astype(jnp.float32)
    middle = rest.astype(jnp.bfloat16)
    low = (rest - middle.astype(jnp.float32)).astype(jnp.bfloat16)
    return high, middle, low


def pick_rows(shape, rows):
    index = lax.broadcasted_iota(jnp.int32, shape, 0)
    out = jnp.zeros(shape, jnp.float32)
    for place, row in enumerate(rows):
        out = jnp.where(index == place, row, out)
    return out


def stage_source(points, scale, xaug, at):
    feat, count = points.shape
    wide = points.astype(jnp.float32)
    shift = scale * jnp.sum(wide * wide, axis=0, keepdims=True)
    shift = shift.astype(jnp.bfloat16).astype(jnp.float32)
    xaug[0:feat, at] = pick_rows((feat, count), [1.0, 1.0, 1.0, -shift]).astype(jnp.bfloat16)
    for place, term in enumerate(three_terms(2.0 * scale * wide)):
        xaug[(place + 1) * feat : (place + 2) * feat, at] = term


def stage_sources(parts, scale, xaug, begin=0):
    for part in parts:
        count = part.shape[2]
        for block in range(part.shape[0]):
            stage_source(part[block], scale, xaug, slice(begin, begin + count))
            begin += count


def target_lines(part, block, scale, feat):
    wide = part[block, :feat, :].astype(jnp.float32)
    logw = part[block, feat : feat + 16, :].astype(jnp.float32)[0:1]
    return scale * jnp.sum(wide * wide, axis=0, keepdims=True), logw * LOG2E


def stage_targets(parts, scale, taug, begin, feat):
    for part in parts:
        for block in range(part.shape[0]):
            q, logw = target_lines(part, block, scale, feat)
            terms = [term.astype(jnp.float32) for term in three_terms(logw - q)]
            extras = pick_rows((feat, LANES), terms + [1.0])
            wide = part[block, :feat, :].astype(jnp.float32)
            turned = jnp.concatenate([extras, wide], axis=0).T
            lane = lax.broadcasted_iota(jnp.int32, turned.shape, 1)
            twice = jnp.where(lane < feat, pltpu.roll(turned, feat, 1), turned)
            taug[begin : begin + LANES, 0:LANES] = turned.astype(jnp.bfloat16)
            taug[begin : begin + LANES, LANES:DEPTH] = twice.astype(jnp.bfloat16)
            begin += LANES


def renew_targets(lines, flips, parts, g, q, logw, taug):
    total = lines[0].shape[1]
    size = total // (2 * parts)
    held = []
    for line, (core, digit) in zip(lines, flips):
        value = line[...]
        places = [(block ^ (core * parts)) ^ digit for block in range(2 * parts)]
        pieces = [value[:, place * size : (place + 1) * size] for place in places]
        held.append(jnp.concatenate(pieces, axis=1))
    peak = functools.reduce(jnp.maximum, held)
    added = functools.reduce(jnp.add, [jnp.exp2(value - peak) for value in held])
    potential = g - (peak + jnp.log2(added))
    g = potential + logw
    terms = [term.astype(jnp.float32) for term in three_terms(g - jnp.max(g) - q)]
    for begin in range(0, total, LANES):
        rows = slice(begin, begin + LANES)
        extras = pick_rows((8, LANES), [term[:, rows] for term in terms] + [1.0])
        taug[rows, 0:8] = extras.T.astype(jnp.bfloat16)
    return potential, g


def exponents(left, right):
    return jnp.dot(left, right, preferred_element_type=jnp.float32)


def spread_rows(taug, right, p_ref, beside):
    total, width = taug.shape[0], right.shape[1]
    reach = min(total, 512)
    sums = jnp.zeros((8, width), jnp.float32)
    for begin in range(0, total, reach):
        e = exponents(taug[begin : begin + reach, :], right)
        for inner in range(0, reach, LANES):
            rows = slice(begin + inner, begin + inner + LANES)
            beside(rows)
            p = jnp.exp2(e[inner : inner + LANES])
            p_ref[rows, :] = p
            sums = sums + jnp.sum(p.reshape(LANES // 8, 8, width), axis=0)
    return jnp.sum(sums, axis=0, keepdims=True)


def add_columns(p_ref, weight, col_ref, rows):
    width = weight.shape[1]
    added = p_ref[rows, 0:LANES] * weight[:, 0:LANES]
    for lane in range(LANES, width, LANES):
        added = added + p_ref[rows, lane : lane + LANES] * weight[:, lane : lane + LANES]
    col_ref[rows, :] += added


def tile_columns(tile, width):
    if isinstance(tile, int):
        return pl.ds(tile * width, width)
    return pl.ds(pl.multiple_of(tile * width, width), width)


def add_sources(xaug, logws, taug, p_refs, col_ref):
    total = taug.shape[0]
    width = p_refs[0].shape[1]
    tiles = xaug.shape[1] // width
    if p_refs[1].shape != p_refs[0].shape:
        p_refs = (p_refs[0], p_refs[0])

    def step(tile, slot, held):
        def beside(rows):
            if held is not None:
                add_columns(p_refs[1 - slot], held, col_ref, rows)

        at = tile_columns(tile, width)
        s = spread_rows(taug, xaug[:, at], p_refs[slot], beside)
        return s, jnp.exp2(logws[:, at] * LOG2E) / s

    def two_steps(pair, carry):
        least, weight = carry
        s1, weight1 = step(2 * pair + 1, 1, weight)
        s0, weight0 = step(2 * pair + 2, 0, weight1)
        return jnp.minimum(least, jnp.minimum(s0, s1)), weight0

    s, weight = step(0, 0, None)
    least, weight = lax.fori_loop(0, tiles // 2 - 1, two_steps, (s, weight))
    s, weight = step(tiles - 1, 1, weight)
    for begin in range(0, total, LANES):
        add_columns(p_refs[1], weight, col_ref, slice(begin, begin + LANES))
    return jnp.minimum(least, s)


def lane_totals(col_ref, out_ref):
    total = col_ref.shape[0]
    reach = min(total, 2048)
    ones = jnp.ones((16, 2 * LANES), jnp.bfloat16)
    for begin in range(0, total, reach):
        high, middle, _ = three_terms(col_ref[begin : begin + reach, :])
        both = jnp.concatenate([high, middle], axis=1)
        added = lax.dot_general(
            ones, both, (((1,), (1,)), ((), ())), preferred_element_type=jnp.float32
        )
        out_ref[:, begin : begin + reach] = added[0:1]


def finish_sums(xaug, logws, taug, least, p_ref, col_ref, out_ref):
    total = taug.shape[0]
    lane_totals(col_ref, out_ref)
    cols = out_ref[...]
    out_ref[...] = jnp.log2(cols)
    fine = jnp.logical_and(
        jnp.min(least) >= SMALL_ROW,
        jnp.logical_and(jnp.min(cols) >= SMALL_COL, jnp.max(cols) <= LARGE_COL),
    )

    top_ref = p_ref.at[:, 0:LANES]

    @pl.when(jnp.logical_not(fine))
    def _():
        col_ref[...] = jnp.zeros_like(col_ref)
        top_ref[...] = jnp.full_like(top_ref, FLOOR)
        blocks = total // LANES

        def block_rows(block):
            return pl.ds(pl.multiple_of(block * LANES, LANES), LANES)

        def careful(tile, carry):
            at = tile_columns(tile, LANES)
            right = xaug[:, at]

            def highest(block, peak):
                e = exponents(taug[block_rows(block), :], right)
                return jnp.maximum(peak, jnp.max(e, axis=0, keepdims=True))

            peak = lax.fori_loop(0, blocks, highest, jnp.full((1, LANES), FLOOR, jnp.float32))

            def summed(block, s):
                e = exponents(taug[block_rows(block), :], right)
                return s + jnp.sum(jnp.exp2(e - peak), axis=0, keepdims=True)

            s = lax.fori_loop(0, blocks, summed, jnp.zeros((1, LANES), jnp.float32))
            shift = logws[:, at] * LOG2E - peak - jnp.log2(s)

            def collected(block, carry):
                rows = block_rows(block)
                term = exponents(taug[rows, :], right) + shift
                old = top_ref[rows, :]
                top = jnp.maximum(old, term)
                col_ref[rows, :] = col_ref[rows, :] * jnp.exp2(old - top) + jnp.exp2(term - top)
                top_ref[rows, :] = top
                return carry

            return lax.fori_loop(0, blocks, collected, carry)

        lax.fori_loop(0, xaug.shape[1] // LANES, careful, 0)

        def turned(block, carry):
            rows = block_rows(block)
            tops = top_ref[rows, :].T
            top = jnp.max(tops, axis=0, keepdims=True)
            added = jnp.sum(col_ref[rows, :].T * jnp.exp2(tops - top), axis=0, keepdims=True)
            out_ref[:, rows] = top + jnp.log2(added)
            return carry

        lax.fori_loop(0, blocks, turned, 0)


def part_kernel(feat, inverse, *refs):
    stage_targets(refs[:-1], inverse[0] * LOG2E, refs[-1], 0, feat)


def near_kernel(parts, feat, inverse, logws, xs, mine, rest, theirs, *refs):
    ts, refs = refs[: 2 * parts], refs[2 * parts :]
    xaug, taug, out_ref, g_ref, q_ref, p0, p1, col_ref = refs
    scale = inverse[0] * LOG2E
    stage_sources([xs], scale, xaug)
    place = 0
    for part in ts:
        for block in range(part.shape[0]):
            at = slice(place * LANES, (place + 1) * LANES)
            q_ref[:, at], g_ref[:, at] = target_lines(part, block, scale, feat)
            place += 1
    begin = 0
    for part in (mine, rest, theirs):
        taug[begin : begin + part.shape[0], :] = part[...]
        begin += part.shape[0]
    stage_targets(ts[parts + 1 :], scale, taug, begin, feat)
    col_ref[...] = jnp.zeros_like(col_ref)
    least = add_sources(xaug, logws, taug, (p0, p1), col_ref)
    finish_sums(xaug, logws, taug, least, p0, col_ref, out_ref)


def next_kernel(flips, parts, logws, xaug, old, g, q, logw, *refs):
    lines, refs = refs[: len(flips)], refs[len(flips) :]
    out_ref, g_ref, taug, p0, p1, col_ref = refs
    taug[...] = old[...]
    g_ref[...] = renew_targets(lines, flips, parts, g[...], q[...], logw[...], taug)[1]
    col_ref[...] = jnp.zeros_like(col_ref)
    least = add_sources(xaug, logws, taug, (p0, p1), col_ref)
    finish_sums(xaug, logws, taug, least, p0, col_ref, out_ref)


def map_kernel(flips, parts, n_t, feat, xaug, old, g, q, logw, *refs):
    lines, refs = refs[: len(flips)], refs[len(flips) :]
    ts = refs[:n_t]
    mapped_ref, pot_ref, taug, p_ref, plan_ref, coords = refs[n_t:]
    taug[...] = old[...]
    potential = renew_targets(lines, flips, parts, g[...], q[...], logw[...], taug)[0]
    pot_ref[...] = potential[:, :LANES] * (1.0 / LOG2E)
    place = 0
    for part in ts:
        for block in range(part.shape[0]):
            coords[:, place * LANES : (place + 1) * LANES] = part[block, :feat, :]
            place += 1
    total = taug.shape[0]
    right = xaug[:, : p_ref.shape[1]]
    s = spread_rows(taug, right, p_ref, lambda rows: None)
    weight = 1.0 / s
    for begin in range(0, total, LANES):
        rows = slice(begin, begin + LANES)
        plan_ref[rows, :] = (p_ref[rows, :] * weight).astype(jnp.bfloat16)

    @pl.when(jnp.logical_not(jnp.min(s) >= SMALL_ROW))
    def _():
        reach = min(total, 2048)
        peak = jnp.full(s.shape, FLOOR, jnp.float32)
        for begin in range(0, total, reach):
            rows = slice(begin, begin + reach)
            p_ref[rows, :] = exponents(taug[rows, :], right)
            peak = jnp.maximum(peak, jnp.max(p_ref[rows, :], axis=0, keepdims=True))
        sums = jnp.zeros(s.shape, jnp.float32)
        for begin in range(0, total, reach):
            rows = slice(begin, begin + reach)
            sums += jnp.sum(jnp.exp2(p_ref[rows, :] - peak), axis=0, keepdims=True)
        shift = peak + jnp.log2(sums)
        for begin in range(0, total, reach):
            rows = slice(begin, begin + reach)
            plan_ref[rows, :] = jnp.exp2(p_ref[rows, :] - shift).astype(jnp.bfloat16)

    mapped_ref[...] = jnp.dot(coords[...], plan_ref[...], preferred_element_type=jnp.float32)


def swap(value, count, step):
    return lax.ppermute(value, AXIS, [(source, source ^ step) for source in range(count)])


def chip_stages(count):
    high, stages = count.bit_length() - 1, []
    while high > 1:
        width = min(2, high - 1)
        stages.append((high - width, width))
        high -= width
    return stages


def gather_stage(parts, count, low, width):
    held = parts[0] if len(parts) == 1 else jnp.concatenate(parts, axis=0)
    return [held] + [swap(held, count, digit << low) for digit in range(1, 1 << width)]


def gather_chips(block, count):
    parts = [block[None]]
    for low, width in chip_stages(count):
        parts = gather_stage(parts, count, low, width)
    return parts


def gather_line(block, count):
    parts = [block[None]]
    for low, width in chip_stages(count)[:-1]:
        parts = gather_stage(parts, count, low, width)
    return jnp.concatenate(parts, axis=0)


def on_device(source_points, target_points, source_logw, target_logw, inverse_eps, count):
    feat, own_sources = source_points.shape
    own_targets = target_points.shape[1]
    extra_rows = own_sources // LANES
    pad = -(1 + extra_rows) % 16
    packed = jnp.concatenate(
        [
            target_points,
            target_logw[None, :],
            source_logw.reshape(extra_rows, LANES),
            jnp.zeros((pad, own_targets), target_points.dtype),
        ],
        axis=0,
    )
    f32, bf16 = jnp.float32, jnp.bfloat16
    total = count * own_targets
    small = total <= 4096
    width = 2 * LANES if small else LANES
    vmem = pl.BlockSpec(memory_space=pltpu.VMEM)
    smem = pl.BlockSpec(memory_space=pltpu.SMEM)
    params = pltpu.CompilerParams(vmem_limit_bytes=(24 if small else 63) << 20)
    line = jax.ShapeDtypeStruct((1, total), f32)

    def call(kernel, operands, outs, scratch=(), scalars=1):
        return pl.pallas_call(
            kernel,
            out_shape=outs,
            in_specs=[smem] * scalars + [vmem] * (len(operands) - scalars),
            out_specs=[vmem] * len(outs),
            scratch_shapes=list(scratch),
            compiler_params=params,
        )(*operands)

    def staged_shape(parts):
        rows = sum(part.shape[0] for part in parts) * own_targets
        return jax.ShapeDtypeStruct((rows, DEPTH), bf16)

    def logw_line(parts):
        rows = [part[:, feat + 1 : feat + 1 + extra_rows] for part in parts]
        return jnp.concatenate(rows, axis=0).reshape(1, -1).astype(f32)

    packed, points = lax.optimization_barrier((packed, source_points))
    mine = gather_chips(packed, count)
    theirs = [swap(part, count, 1) for part in mine]
    parts, low = len(mine), chip_stages(count)[-1][0]
    ts = mine + theirs
    (taug_mine,) = call(
        functools.partial(part_kernel, feat),
        [inverse_eps, mine[0]],
        [staged_shape(mine[:1])],
    )
    (taug_theirs,) = call(
        functools.partial(part_kernel, feat),
        [inverse_eps, theirs[0]],
        [staged_shape(theirs[:1])],
    )
    (taug_rest,) = call(
        functools.partial(part_kernel, feat),
        [inverse_eps] + mine[1:],
        [staged_shape(mine[1:])],
    )
    xs = gather_line(points, count)
    logws = logw_line(mine[:1])
    rows = logws.shape[1]

    p_scratch = pltpu.VMEM((total, width), f32)
    scratch = [
        p_scratch,
        p_scratch if small else pltpu.VMEM((8, LANES), f32),
        pltpu.VMEM((total, LANES), f32),
    ]
    xaug, taug, sums, logw, q = call(
        functools.partial(near_kernel, parts, feat),
        [inverse_eps, logws, xs, taug_mine, taug_rest, taug_theirs] + ts,
        [
            jax.ShapeDtypeStruct((DEPTH, rows), bf16),
            jax.ShapeDtypeStruct((total, DEPTH), bf16),
            line,
            line,
            line,
        ],
        scratch,
    )
    flips = [(core, digit) for core in range(2) for digit in range(parts)]

    def exchange(own):
        held = [own] + [swap(own, count, digit << low) for digit in range(1, parts)]
        return held + [swap(value, count, 1) for value in held]

    g = logw
    for _ in range(ITERS - 1):
        sums, g = call(
            functools.partial(next_kernel, flips, parts),
            [logws, xaug, taug, g, q, logw] + exchange(sums),
            [line, line],
            [pltpu.VMEM((total, DEPTH), bf16)] + scratch,
            scalars=0,
        )
    mapped, potential = call(
        functools.partial(map_kernel, flips, parts, len(ts), feat),
        [xaug if small else xaug[:, :own_sources], taug, g, q, logw] + exchange(sums) + ts,
        [
            jax.ShapeDtypeStruct((feat, own_sources), f32),
            jax.ShapeDtypeStruct((1, own_targets), f32),
        ],
        [
            pltpu.VMEM((total, DEPTH), bf16),
            pltpu.VMEM((total, own_sources), f32),
            pltpu.VMEM((total, own_sources), bf16),
            pltpu.VMEM((feat, total), bf16),
        ],
        scalars=0,
    )
    return (mapped, potential.reshape(own_targets))


def solution(mesh):
    count = mesh.shape[AXIS]
    placed = (
        P(None, ("grp", "wide")),
        P(None, ("grp", "wide")),
        P(("grp", "wide")),
        P(("grp", "wide")),
        P(),
    )

    def body(*blocks):
        return on_device(*blocks, count)

    return jax.shard_map(
        body,
        mesh=mesh,
        in_specs=placed,
        out_specs=(P(None, ("grp", "wide")), P(("grp", "wide"))),
        check_vma=False,
    )
```

```python
import functools
import math

import jax
import jax.numpy as jnp
from jax import lax
from jax.experimental import pallas as pl
from jax.experimental.pallas import tpu as pltpu
from jax.sharding import PartitionSpec as P

ITERS = 2
AXIS = "wide"
LOG2E = math.log2(math.e)
LANES = 128
DEPTH = 256
SMALL_ROW = 2.0**-64
SMALL_COL = 2.0**-32
LARGE_COL = 2.0**100
FLOOR = -1e30


def three_terms(value):
    high = value.astype(jnp.bfloat16)
    rest = value - high.astype(jnp.float32)
    middle = rest.astype(jnp.bfloat16)
    low = (rest - middle.astype(jnp.float32)).astype(jnp.bfloat16)
    return high, middle, low


def pick_rows(shape, rows):
    index = lax.broadcasted_iota(jnp.int32, shape, 0)
    out = jnp.zeros(shape, jnp.float32)
    for place, row in enumerate(rows):
        out = jnp.where(index == place, row, out)
    return out


def stage_source(points, scale, xaug, at):
    feat, count = points.shape
    wide = points.astype(jnp.float32)
    shift = scale * jnp.sum(wide * wide, axis=0, keepdims=True)
    shift = shift.astype(jnp.bfloat16).astype(jnp.float32)
    xaug[0:feat, at] = pick_rows((feat, count), [1.0, 1.0, 1.0, -shift]).astype(jnp.bfloat16)
    for place, term in enumerate(three_terms(2.0 * scale * wide)):
        xaug[(place + 1) * feat : (place + 2) * feat, at] = term


def stage_sources(parts, scale, xaug, begin=0):
    for part in parts:
        count = part.shape[2]
        for block in range(part.shape[0]):
            stage_source(part[block], scale, xaug, slice(begin, begin + count))
            begin += count


def stage_targets(parts, scale, taug, q_ref, logw_ref, begin, feat):
    for part in parts:
        for block in range(part.shape[0]):
            wide = part[block, :feat, :].astype(jnp.float32)
            q = scale * jnp.sum(wide * wide, axis=0, keepdims=True)
            logw = part[block, feat : feat + 16, :].astype(jnp.float32)[0:1] * LOG2E
            q_ref[:, begin : begin + LANES] = q
            logw_ref[:, begin : begin + LANES] = logw
            terms = [term.astype(jnp.float32) for term in three_terms(logw - q)]
            extras = pick_rows((feat, LANES), terms + [1.0])
            turned = jnp.concatenate([extras, wide], axis=0).T
            lane = lax.broadcasted_iota(jnp.int32, turned.shape, 1)
            twice = jnp.where(lane < feat, pltpu.roll(turned, feat, 1), turned)
            taug[begin : begin + LANES, 0:LANES] = turned.astype(jnp.bfloat16)
            taug[begin : begin + LANES, LANES:DEPTH] = twice.astype(jnp.bfloat16)
            begin += LANES


def renew_targets(lines, flips, parts, g, q, logw, taug):
    total = lines[0].shape[1]
    size = total // (2 * parts)
    held = []
    for line, (core, digit) in zip(lines, flips):
        value = line[...]
        places = [(block ^ (core * parts)) ^ digit for block in range(2 * parts)]
        pieces = [value[:, place * size : (place + 1) * size] for place in places]
        held.append(jnp.concatenate(pieces, axis=1))
    peak = functools.reduce(jnp.maximum, held)
    added = functools.reduce(jnp.add, [jnp.exp2(value - peak) for value in held])
    potential = g - (peak + jnp.log2(added))
    g = potential + logw
    terms = [term.astype(jnp.float32) for term in three_terms(g - jnp.max(g) - q)]
    for begin in range(0, total, LANES):
        rows = slice(begin, begin + LANES)
        extras = pick_rows((8, LANES), [term[:, rows] for term in terms] + [1.0])
        taug[rows, 0:8] = extras.T.astype(jnp.bfloat16)
    return potential, g


def exponents(left, right):
    return jnp.dot(left, right, preferred_element_type=jnp.float32)


def spread_rows(taug, right, p_ref, beside):
    total, width = taug.shape[0], right.shape[1]
    reach = min(total, 512)
    sums = jnp.zeros((8, width), jnp.float32)
    for begin in range(0, total, reach):
        e = exponents(taug[begin : begin + reach, :], right)
        for inner in range(0, reach, LANES):
            rows = slice(begin + inner, begin + inner + LANES)
            beside(rows)
            p = jnp.exp2(e[inner : inner + LANES])
            p_ref[rows, :] = p
            sums = sums + jnp.sum(p.reshape(LANES // 8, 8, width), axis=0)
    return jnp.sum(sums, axis=0, keepdims=True)


def add_columns(p_ref, weight, col_ref, rows):
    width = weight.shape[1]
    added = p_ref[rows, 0:LANES] * weight[:, 0:LANES]
    for lane in range(LANES, width, LANES):
        added = added + p_ref[rows, lane : lane + LANES] * weight[:, lane : lane + LANES]
    col_ref[rows, :] += added


def tile_columns(tile, width):
    if isinstance(tile, int):
        return pl.ds(tile * width, width)
    return pl.ds(pl.multiple_of(tile * width, width), width)


def add_sources(xaug, logws, taug, p_refs, col_ref):
    total = taug.shape[0]
    width = p_refs[0].shape[1]
    tiles = xaug.shape[1] // width
    if p_refs[1].shape != p_refs[0].shape:
        p_refs = (p_refs[0], p_refs[0])

    def step(tile, slot, held):
        def beside(rows):
            if held is not None:
                add_columns(p_refs[1 - slot], held, col_ref, rows)

        at = tile_columns(tile, width)
        s = spread_rows(taug, xaug[:, at], p_refs[slot], beside)
        return s, jnp.exp2(logws[:, at] * LOG2E) / s

    def two_steps(pair, carry):
        least, weight = carry
        s1, weight1 = step(2 * pair + 1, 1, weight)
        s0, weight0 = step(2 * pair + 2, 0, weight1)
        return jnp.minimum(least, jnp.minimum(s0, s1)), weight0

    s, weight = step(0, 0, None)
    least, weight = lax.fori_loop(0, tiles // 2 - 1, two_steps, (s, weight))
    s, weight = step(tiles - 1, 1, weight)
    for begin in range(0, total, LANES):
        add_columns(p_refs[1], weight, col_ref, slice(begin, begin + LANES))
    return jnp.minimum(least, s)


def lane_totals(col_ref, out_ref):
    total = col_ref.shape[0]
    reach = min(total, 2048)
    ones = jnp.ones((16, 2 * LANES), jnp.bfloat16)
    for begin in range(0, total, reach):
        high, middle, _ = three_terms(col_ref[begin : begin + reach, :])
        both = jnp.concatenate([high, middle], axis=1)
        added = lax.dot_general(
            ones, both, (((1,), (1,)), ((), ())), preferred_element_type=jnp.float32
        )
        out_ref[:, begin : begin + reach] = added[0:1]


def finish_sums(xaug, logws, taug, least, p_ref, col_ref, out_ref):
    total = taug.shape[0]
    lane_totals(col_ref, out_ref)
    cols = out_ref[...]
    out_ref[...] = jnp.log2(cols)
    fine = jnp.logical_and(
        jnp.min(least) >= SMALL_ROW,
        jnp.logical_and(jnp.min(cols) >= SMALL_COL, jnp.max(cols) <= LARGE_COL),
    )

    top_ref = p_ref.at[:, 0:LANES]

    @pl.when(jnp.logical_not(fine))
    def _():
        col_ref[...] = jnp.zeros_like(col_ref)
        top_ref[...] = jnp.full_like(top_ref, FLOOR)
        blocks = total // LANES

        def block_rows(block):
            return pl.ds(pl.multiple_of(block * LANES, LANES), LANES)

        def careful(tile, carry):
            at = tile_columns(tile, LANES)
            right = xaug[:, at]

            def highest(block, peak):
                e = exponents(taug[block_rows(block), :], right)
                return jnp.maximum(peak, jnp.max(e, axis=0, keepdims=True))

            peak = lax.fori_loop(0, blocks, highest, jnp.full((1, LANES), FLOOR, jnp.float32))

            def summed(block, s):
                e = exponents(taug[block_rows(block), :], right)
                return s + jnp.sum(jnp.exp2(e - peak), axis=0, keepdims=True)

            s = lax.fori_loop(0, blocks, summed, jnp.zeros((1, LANES), jnp.float32))
            shift = logws[:, at] * LOG2E - peak - jnp.log2(s)

            def collected(block, carry):
                rows = block_rows(block)
                term = exponents(taug[rows, :], right) + shift
                old = top_ref[rows, :]
                top = jnp.maximum(old, term)
                col_ref[rows, :] = col_ref[rows, :] * jnp.exp2(old - top) + jnp.exp2(term - top)
                top_ref[rows, :] = top
                return carry

            return lax.fori_loop(0, blocks, collected, carry)

        lax.fori_loop(0, xaug.shape[1] // LANES, careful, 0)

        def turned(block, carry):
            rows = block_rows(block)
            tops = top_ref[rows, :].T
            top = jnp.max(tops, axis=0, keepdims=True)
            added = jnp.sum(col_ref[rows, :].T * jnp.exp2(tops - top), axis=0, keepdims=True)
            out_ref[:, rows] = top + jnp.log2(added)
            return carry

        lax.fori_loop(0, blocks, turned, 0)


def targets_kernel(feat, inverse, *refs):
    taug, q_ref, logw_ref = refs[-3:]
    stage_targets(refs[:-3], inverse[0] * LOG2E, taug, q_ref, logw_ref, 0, feat)


def sources_kernel(inverse, *refs):
    stage_sources(refs[:-1], inverse[0] * LOG2E, refs[-1])


def near_kernel(late, feat, inverse, logws, xaug, *refs):
    staged, refs = refs[:9], refs[9:]
    ts, refs = refs[:late], refs[late:]
    taug, out_ref, q_ref, logw_ref, p0, p1, col_ref = refs
    begin = 0
    for part, q, logw in zip(staged[0::3], staged[1::3], staged[2::3]):
        end = begin + part.shape[0]
        taug[begin:end, :] = part[...]
        q_ref[:, begin:end] = q[...]
        logw_ref[:, begin:end] = logw[...]
        begin = end
    stage_targets(ts, inverse[0] * LOG2E, taug, q_ref, logw_ref, begin, feat)
    col_ref[...] = jnp.zeros_like(col_ref)
    least = add_sources(xaug, logws, taug, (p0, p1), col_ref)
    finish_sums(xaug, logws, taug, least, p0, col_ref, out_ref)


def next_kernel(flips, parts, logws, xaug, old, g, q, logw, *refs):
    lines, refs = refs[: len(flips)], refs[len(flips) :]
    out_ref, g_ref, taug, p0, p1, col_ref = refs
    taug[...] = old[...]
    g_ref[...] = renew_targets(lines, flips, parts, g[...], q[...], logw[...], taug)[1]
    col_ref[...] = jnp.zeros_like(col_ref)
    least = add_sources(xaug, logws, taug, (p0, p1), col_ref)
    finish_sums(xaug, logws, taug, least, p0, col_ref, out_ref)


def map_kernel(flips, parts, n_t, feat, place, xaug, old, g, q, logw, *refs):
    lines, refs = refs[: len(flips)], refs[len(flips) :]
    ts = refs[:n_t]
    mapped_ref, pot_ref, g_ref, taug, p_ref, plan_ref, coords = refs[n_t:]
    taug[...] = old[...]
    potential = renew_targets(lines, flips, parts, g[...], q[...], logw[...], taug)[0]
    g_ref[...] = potential
    at = pl.ds(pl.multiple_of(place[0] * LANES, LANES), LANES)
    pot_ref[...] = g_ref[:, at] * (1.0 / LOG2E)
    begin = 0
    for part in ts:
        for block in range(part.shape[0]):
            coords[:, begin : begin + LANES] = part[block, :feat, :]
            begin += LANES
    total, width = p_ref.shape
    if xaug.shape[1] == width:
        right = xaug[...]
    else:
        right = xaug[:, pl.ds(pl.multiple_of(place[0] * width, LANES), width)]
    s = spread_rows(taug, right, p_ref, lambda rows: None)
    weight = 1.0 / s
    for begin in range(0, total, LANES):
        rows = slice(begin, begin + LANES)
        plan_ref[rows, :] = (p_ref[rows, :] * weight).astype(jnp.bfloat16)

    @pl.when(jnp.logical_not(jnp.min(s) >= SMALL_ROW))
    def _():
        reach = min(total, 2048)
        peak = jnp.full(s.shape, FLOOR, jnp.float32)
        for begin in range(0, total, reach):
            rows = slice(begin, begin + reach)
            p_ref[rows, :] = exponents(taug[rows, :], right)
            peak = jnp.maximum(peak, jnp.max(p_ref[rows, :], axis=0, keepdims=True))
        sums = jnp.zeros(s.shape, jnp.float32)
        for begin in range(0, total, reach):
            rows = slice(begin, begin + reach)
            sums += jnp.sum(jnp.exp2(p_ref[rows, :] - peak), axis=0, keepdims=True)
        shift = peak + jnp.log2(sums)
        for begin in range(0, total, reach):
            rows = slice(begin, begin + reach)
            plan_ref[rows, :] = jnp.exp2(p_ref[rows, :] - shift).astype(jnp.bfloat16)

    mapped_ref[...] = jnp.dot(coords[...], plan_ref[...], preferred_element_type=jnp.float32)


def swap(value, count, step):
    return lax.ppermute(value, AXIS, [(source, source ^ step) for source in range(count)])


def chip_stages(count):
    high, stages = count.bit_length() - 1, []
    while high > 1:
        width = min(2, high - 1)
        stages.append((high - width, width))
        high -= width
    return stages


def gather_stage(parts, count, low, width):
    held = parts[0] if len(parts) == 1 else jnp.concatenate(parts, axis=0)
    return [held] + [swap(held, count, digit << low) for digit in range(1, 1 << width)]


def line_blocks(block, count, low, width):
    span = 1 << width
    mask = (span - 1) << low
    groups = [
        [base | (digit << low) for digit in range(span)]
        for base in range(count)
        if base & mask == 0
    ]
    spread = jnp.broadcast_to(block[None], (span,) + block.shape)
    return lax.all_to_all(spread, AXIS, 0, 0, axis_index_groups=groups, tiled=True)


def gather_chips(block, count):
    parts = [block[None]]
    for place, (low, width) in enumerate(chip_stages(count)):
        if place == 0:
            parts = [line_blocks(block, count, low, width)]
        else:
            parts = gather_stage(parts, count, low, width)
    return parts


def gather_line(block, count):
    parts = [block[None]]
    for place, (low, width) in enumerate(chip_stages(count)[:-1]):
        if place == 0:
            parts = [line_blocks(block, count, low, width)]
        else:
            parts = gather_stage(parts, count, low, width)
    return parts


def on_device(source_points, target_points, source_logw, target_logw, inverse_eps, count):
    feat, own_sources = source_points.shape
    own_targets = target_points.shape[1]
    extra_rows = own_sources // LANES
    pad = -(1 + extra_rows) % 16
    packed = jnp.concatenate(
        [
            target_points,
            target_logw[None, :],
            source_logw.reshape(extra_rows, LANES),
            jnp.zeros((pad, own_targets), target_points.dtype),
        ],
        axis=0,
    )
    f32, bf16 = jnp.float32, jnp.bfloat16
    total = count * own_targets
    small = total <= 4096
    width = 2 * LANES if small else LANES
    vmem = pl.BlockSpec(memory_space=pltpu.VMEM)
    smem = pl.BlockSpec(memory_space=pltpu.SMEM)
    params = pltpu.CompilerParams(vmem_limit_bytes=(24 if small else 63) << 20)
    line = jax.ShapeDtypeStruct((1, total), f32)

    def call(kernel, operands, outs, scratch=(), scalars=1):
        return pl.pallas_call(
            kernel,
            out_shape=outs,
            in_specs=[smem] * scalars + [vmem] * (len(operands) - scalars),
            out_specs=[vmem] * len(outs),
            scratch_shapes=list(scratch),
            compiler_params=params,
        )(*operands)

    def stage(parts):
        rows = sum(part.shape[0] for part in parts) * own_targets
        lines = [jax.ShapeDtypeStruct((1, rows), f32)] * 2
        staged = call(
            functools.partial(targets_kernel, feat),
            [inverse_eps] + parts,
            [jax.ShapeDtypeStruct((rows, DEPTH), bf16)] + lines,
        )
        return list(staged)

    def logw_line(parts):
        rows = [part[:, feat + 1 : feat + 1 + extra_rows] for part in parts]
        return jnp.concatenate(rows, axis=0).reshape(1, -1).astype(f32)

    packed, points = lax.optimization_barrier((packed, source_points))
    mine = gather_chips(packed, count)
    theirs = [swap(part, count, 1) for part in mine]
    parts, low = len(mine), chip_stages(count)[-1][0]
    first_low, first_width = chip_stages(count)[0]
    place = (lax.axis_index(AXIS) >> first_low) & ((1 << first_width) - 1)
    place = place.astype(jnp.int32).reshape(1)
    ts = mine + theirs
    staged = stage(mine[:1]) + stage(mine[1:]) + stage(theirs[:1])
    xs = gather_line(points, count)
    logws = logw_line(mine[:1])
    rows = logws.shape[1]
    (xaug,) = call(
        sources_kernel,
        [inverse_eps] + xs,
        [jax.ShapeDtypeStruct((DEPTH, rows), bf16)],
    )

    p_scratch = pltpu.VMEM((total, width), f32)
    scratch = [
        p_scratch,
        p_scratch if small else pltpu.VMEM((8, LANES), f32),
        pltpu.VMEM((total, LANES), f32),
    ]
    taug, sums, q, logw = call(
        functools.partial(near_kernel, parts - 1, feat),
        [inverse_eps, logws, xaug] + staged + theirs[1:],
        [jax.ShapeDtypeStruct((total, DEPTH), bf16), line, line, line],
        scratch,
    )
    flips = [(core, digit) for core in range(2) for digit in range(parts)]

    def exchange(own):
        held = [own] + [swap(own, count, digit << low) for digit in range(1, parts)]
        return held + [swap(value, count, 1) for value in held]

    g = logw
    for _ in range(ITERS - 1):
        sums, g = call(
            functools.partial(next_kernel, flips, parts),
            [logws, xaug, taug, g, q, logw] + exchange(sums),
            [line, line],
            [pltpu.VMEM((total, DEPTH), bf16)] + scratch,
            scalars=0,
        )
    if not small:
        xaug = lax.dynamic_slice_in_dim(xaug, place[0] * own_sources, own_sources, 1)
    mapped, potential = call(
        functools.partial(map_kernel, flips, parts, len(ts), feat),
        [place, xaug, taug, g, q, logw] + exchange(sums) + ts,
        [
            jax.ShapeDtypeStruct((feat, own_sources), f32),
            jax.ShapeDtypeStruct((1, own_targets), f32),
        ],
        [
            pltpu.VMEM((1, total), f32),
            pltpu.VMEM((total, DEPTH), bf16),
            pltpu.VMEM((total, own_sources), f32),
            pltpu.VMEM((total, own_sources), bf16),
            pltpu.VMEM((feat, total), bf16),
        ],
    )
    return (mapped, potential.reshape(own_targets))


def solution(mesh):
    count = mesh.shape[AXIS]
    placed = (
        P(None, ("grp", "wide")),
        P(None, ("grp", "wide")),
        P(("grp", "wide")),
        P(("grp", "wide")),
        P(),
    )

    def body(*blocks):
        return on_device(*blocks, count)

    return jax.shard_map(
        body,
        mesh=mesh,
        in_specs=placed,
        out_specs=(P(None, ("grp", "wide")), P(("grp", "wide"))),
        check_vma=False,
    )
```

```python
import functools
import math

import jax
import jax.numpy as jnp
from jax import lax
from jax.experimental import pallas as pl
from jax.experimental.pallas import tpu as pltpu
from jax.sharding import PartitionSpec as P

ITERS = 2
AXIS = "wide"
LOG2E = math.log2(math.e)
LANES = 128
DEPTH = 256
SMALL_ROW = 2.0**-64
SMALL_COL = 2.0**-32
LARGE_COL = 2.0**100
FLOOR = -1e30


def three_terms(value):
    high = value.astype(jnp.bfloat16)
    rest = value - high.astype(jnp.float32)
    middle = rest.astype(jnp.bfloat16)
    low = (rest - middle.astype(jnp.float32)).astype(jnp.bfloat16)
    return high, middle, low


def pick_rows(shape, rows):
    index = lax.broadcasted_iota(jnp.int32, shape, 0)
    out = jnp.zeros(shape, jnp.float32)
    for place, row in enumerate(rows):
        out = jnp.where(index == place, row, out)
    return out


def stage_source(points, scale, xaug, at):
    feat, count = points.shape
    wide = points.astype(jnp.float32)
    shift = scale * jnp.sum(wide * wide, axis=0, keepdims=True)
    shift = shift.astype(jnp.bfloat16).astype(jnp.float32)
    xaug[0:feat, at] = pick_rows((feat, count), [1.0, 1.0, 1.0, -shift]).astype(jnp.bfloat16)
    for place, term in enumerate(three_terms(2.0 * scale * wide)):
        xaug[(place + 1) * feat : (place + 2) * feat, at] = term


def stage_sources(parts, scale, xaug, begin=0):
    for part in parts:
        count = part.shape[2]
        for block in range(part.shape[0]):
            stage_source(part[block], scale, xaug, slice(begin, begin + count))
            begin += count


def target_lines(part, block, scale, feat):
    wide = part[block, :feat, :].astype(jnp.float32)
    logw = part[block, feat : feat + 16, :].astype(jnp.float32)[0:1]
    return scale * jnp.sum(wide * wide, axis=0, keepdims=True), logw * LOG2E


def stage_targets(parts, scale, taug, begin, feat):
    for part in parts:
        for block in range(part.shape[0]):
            q, logw = target_lines(part, block, scale, feat)
            terms = [term.astype(jnp.float32) for term in three_terms(logw - q)]
            extras = pick_rows((feat, LANES), terms + [1.0])
            wide = part[block, :feat, :].astype(jnp.float32)
            turned = jnp.concatenate([extras, wide], axis=0).T
            lane = lax.broadcasted_iota(jnp.int32, turned.shape, 1)
            twice = jnp.where(lane < feat, pltpu.roll(turned, feat, 1), turned)
            taug[begin : begin + LANES, 0:LANES] = turned.astype(jnp.bfloat16)
            taug[begin : begin + LANES, LANES:DEPTH] = twice.astype(jnp.bfloat16)
            begin += LANES


def renew_targets(lines, flips, parts, g, q, logw, taug):
    total = lines[0].shape[1]
    size = total // (2 * parts)
    held = []
    for line, (core, digit) in zip(lines, flips):
        value = line[...]
        places = [(block ^ (core * parts)) ^ digit for block in range(2 * parts)]
        pieces = [value[:, place * size : (place + 1) * size] for place in places]
        held.append(jnp.concatenate(pieces, axis=1))
    peak = functools.reduce(jnp.maximum, held)
    added = functools.reduce(jnp.add, [jnp.exp2(value - peak) for value in held])
    potential = g - (peak + jnp.log2(added))
    g = potential + logw
    terms = [term.astype(jnp.float32) for term in three_terms(g - jnp.max(g) - q)]
    for begin in range(0, total, LANES):
        rows = slice(begin, begin + LANES)
        extras = pick_rows((8, LANES), [term[:, rows] for term in terms] + [1.0])
        taug[rows, 0:8] = extras.T.astype(jnp.bfloat16)
    return potential, g


def exponents(left, right):
    return jnp.dot(left, right, preferred_element_type=jnp.float32)


def spread_rows(taug, right, p_ref, beside):
    total, width = taug.shape[0], right.shape[1]
    reach = min(total, 512)
    sums = jnp.zeros((8, width), jnp.float32)
    for begin in range(0, total, reach):
        e = exponents(taug[begin : begin + reach, :], right)
        for inner in range(0, reach, LANES):
            rows = slice(begin + inner, begin + inner + LANES)
            beside(rows)
            p = jnp.exp2(e[inner : inner + LANES])
            p_ref[rows, :] = p
            sums = sums + jnp.sum(p.reshape(LANES // 8, 8, width), axis=0)
    return jnp.sum(sums, axis=0, keepdims=True)


def add_columns(p_ref, weight, col_ref, rows):
    width = weight.shape[1]
    added = p_ref[rows, 0:LANES] * weight[:, 0:LANES]
    for lane in range(LANES, width, LANES):
        added = added + p_ref[rows, lane : lane + LANES] * weight[:, lane : lane + LANES]
    col_ref[rows, :] += added


def tile_columns(tile, width):
    if isinstance(tile, int):
        return pl.ds(tile * width, width)
    return pl.ds(pl.multiple_of(tile * width, width), width)


def add_sources(xaug, logws, taug, p_refs, col_ref):
    total = taug.shape[0]
    width = p_refs[0].shape[1]
    tiles = xaug.shape[1] // width
    if p_refs[1].shape != p_refs[0].shape:
        p_refs = (p_refs[0], p_refs[0])

    def step(tile, slot, held):
        def beside(rows):
            if held is not None:
                add_columns(p_refs[1 - slot], held, col_ref, rows)

        at = tile_columns(tile, width)
        s = spread_rows(taug, xaug[:, at], p_refs[slot], beside)
        return s, jnp.exp2(logws[:, at] * LOG2E) / s

    def two_steps(pair, carry):
        least, weight = carry
        s1, weight1 = step(2 * pair + 1, 1, weight)
        s0, weight0 = step(2 * pair + 2, 0, weight1)
        return jnp.minimum(least, jnp.minimum(s0, s1)), weight0

    s, weight = step(0, 0, None)
    least, weight = lax.fori_loop(0, tiles // 2 - 1, two_steps, (s, weight))
    s, weight = step(tiles - 1, 1, weight)
    for begin in range(0, total, LANES):
        add_columns(p_refs[1], weight, col_ref, slice(begin, begin + LANES))
    return jnp.minimum(least, s)


def lane_totals(col_ref, out_ref):
    total = col_ref.shape[0]
    reach = min(total, 2048)
    ones = jnp.ones((16, 2 * LANES), jnp.bfloat16)
    for begin in range(0, total, reach):
        high, middle, _ = three_terms(col_ref[begin : begin + reach, :])
        both = jnp.concatenate([high, middle], axis=1)
        added = lax.dot_general(
            ones, both, (((1,), (1,)), ((), ())), preferred_element_type=jnp.float32
        )
        out_ref[:, begin : begin + reach] = added[0:1]


def finish_sums(xaug, logws, taug, least, p_ref, col_ref, out_ref):
    total = taug.shape[0]
    lane_totals(col_ref, out_ref)
    cols = out_ref[...]
    out_ref[...] = jnp.log2(cols)
    fine = jnp.logical_and(
        jnp.min(least) >= SMALL_ROW,
        jnp.logical_and(jnp.min(cols) >= SMALL_COL, jnp.max(cols) <= LARGE_COL),
    )

    top_ref = p_ref.at[:, 0:LANES]

    @pl.when(jnp.logical_not(fine))
    def _():
        col_ref[...] = jnp.zeros_like(col_ref)
        top_ref[...] = jnp.full_like(top_ref, FLOOR)
        blocks = total // LANES

        def block_rows(block):
            return pl.ds(pl.multiple_of(block * LANES, LANES), LANES)

        def careful(tile, carry):
            at = tile_columns(tile, LANES)
            right = xaug[:, at]

            def highest(block, peak):
                e = exponents(taug[block_rows(block), :], right)
                return jnp.maximum(peak, jnp.max(e, axis=0, keepdims=True))

            peak = lax.fori_loop(0, blocks, highest, jnp.full((1, LANES), FLOOR, jnp.float32))

            def summed(block, s):
                e = exponents(taug[block_rows(block), :], right)
                return s + jnp.sum(jnp.exp2(e - peak), axis=0, keepdims=True)

            s = lax.fori_loop(0, blocks, summed, jnp.zeros((1, LANES), jnp.float32))
            shift = logws[:, at] * LOG2E - peak - jnp.log2(s)

            def collected(block, carry):
                rows = block_rows(block)
                term = exponents(taug[rows, :], right) + shift
                old = top_ref[rows, :]
                top = jnp.maximum(old, term)
                col_ref[rows, :] = col_ref[rows, :] * jnp.exp2(old - top) + jnp.exp2(term - top)
                top_ref[rows, :] = top
                return carry

            return lax.fori_loop(0, blocks, collected, carry)

        lax.fori_loop(0, xaug.shape[1] // LANES, careful, 0)

        def turned(block, carry):
            rows = block_rows(block)
            tops = top_ref[rows, :].T
            top = jnp.max(tops, axis=0, keepdims=True)
            added = jnp.sum(col_ref[rows, :].T * jnp.exp2(tops - top), axis=0, keepdims=True)
            out_ref[:, rows] = top + jnp.log2(added)
            return carry

        lax.fori_loop(0, blocks, turned, 0)


def part_kernel(feat, inverse, *refs):
    stage_targets(refs[:-1], inverse[0] * LOG2E, refs[-1], 0, feat)


def near_kernel(parts, feat, inverse, logws, xs, mine, rest, theirs, *refs):
    ts, refs = refs[: 2 * parts], refs[2 * parts :]
    xaug, taug, out_ref, g_ref, q_ref, p0, p1, col_ref = refs
    scale = inverse[0] * LOG2E
    stage_sources([xs], scale, xaug)
    place = 0
    for part in ts:
        for block in range(part.shape[0]):
            at = slice(place * LANES, (place + 1) * LANES)
            q_ref[:, at], g_ref[:, at] = target_lines(part, block, scale, feat)
            place += 1
    begin = 0
    for part in (mine, rest, theirs):
        taug[begin : begin + part.shape[0], :] = part[...]
        begin += part.shape[0]
    stage_targets(ts[parts + 1 :], scale, taug, begin, feat)
    col_ref[...] = jnp.zeros_like(col_ref)
    least = add_sources(xaug, logws, taug, (p0, p1), col_ref)
    finish_sums(xaug, logws, taug, least, p0, col_ref, out_ref)


def next_kernel(flips, parts, logws, xaug, old, g, q, logw, *refs):
    lines, refs = refs[: len(flips)], refs[len(flips) :]
    out_ref, g_ref, taug, p0, p1, col_ref = refs
    taug[...] = old[...]
    g_ref[...] = renew_targets(lines, flips, parts, g[...], q[...], logw[...], taug)[1]
    col_ref[...] = jnp.zeros_like(col_ref)
    least = add_sources(xaug, logws, taug, (p0, p1), col_ref)
    finish_sums(xaug, logws, taug, least, p0, col_ref, out_ref)


def map_kernel(flips, parts, n_t, feat, xaug, old, g, q, logw, *refs):
    lines, refs = refs[: len(flips)], refs[len(flips) :]
    ts = refs[:n_t]
    mapped_ref, pot_ref, taug, p_ref, plan_ref, coords = refs[n_t:]
    taug[...] = old[...]
    potential = renew_targets(lines, flips, parts, g[...], q[...], logw[...], taug)[0]
    pot_ref[...] = potential[:, :LANES] * (1.0 / LOG2E)
    place = 0
    for part in ts:
        for block in range(part.shape[0]):
            coords[:, place * LANES : (place + 1) * LANES] = part[block, :feat, :]
            place += 1
    total = taug.shape[0]
    right = xaug[:, : p_ref.shape[1]]
    s = spread_rows(taug, right, p_ref, lambda rows: None)
    weight = 1.0 / s
    for begin in range(0, total, LANES):
        rows = slice(begin, begin + LANES)
        plan_ref[rows, :] = (p_ref[rows, :] * weight).astype(jnp.bfloat16)

    @pl.when(jnp.logical_not(jnp.min(s) >= SMALL_ROW))
    def _():
        reach = min(total, 2048)
        peak = jnp.full(s.shape, FLOOR, jnp.float32)
        for begin in range(0, total, reach):
            rows = slice(begin, begin + reach)
            p_ref[rows, :] = exponents(taug[rows, :], right)
            peak = jnp.maximum(peak, jnp.max(p_ref[rows, :], axis=0, keepdims=True))
        sums = jnp.zeros(s.shape, jnp.float32)
        for begin in range(0, total, reach):
            rows = slice(begin, begin + reach)
            sums += jnp.sum(jnp.exp2(p_ref[rows, :] - peak), axis=0, keepdims=True)
        shift = peak + jnp.log2(sums)
        for begin in range(0, total, reach):
            rows = slice(begin, begin + reach)
            plan_ref[rows, :] = jnp.exp2(p_ref[rows, :] - shift).astype(jnp.bfloat16)

    mapped_ref[...] = jnp.dot(coords[...], plan_ref[...], preferred_element_type=jnp.float32)


def swap(value, count, step):
    return lax.ppermute(value, AXIS, [(source, source ^ step) for source in range(count)])


def chip_stages(count):
    high, stages = count.bit_length() - 1, []
    while high > 1:
        width = min(2, high - 1)
        stages.append((high - width, width))
        high -= width
    return stages


def gather_stage(parts, count, low, width):
    held = parts[0] if len(parts) == 1 else jnp.concatenate(parts, axis=0)
    return [held] + [swap(held, count, digit << low) for digit in range(1, 1 << width)]


def gather_chips(block, count):
    parts = [block[None]]
    for low, width in chip_stages(count):
        parts = gather_stage(parts, count, low, width)
    return parts


def gather_line(block, later, count):
    parts = [block[None]]
    for place, (low, width) in enumerate(chip_stages(count)[:-1]):
        if place == 0:
            for digit in range(1, 1 << width):
                source = block if digit <= 2 else later
                parts = parts + [swap(source[None], count, digit << low)]
        else:
            parts = gather_stage(parts, count, low, width)
    return jnp.concatenate(parts, axis=0)


def on_device(source_points, target_points, source_logw, target_logw, inverse_eps, count):
    feat, own_sources = source_points.shape
    own_targets = target_points.shape[1]
    extra_rows = own_sources // LANES
    pad = -(1 + extra_rows) % 16
    packed = jnp.concatenate(
        [
            target_points,
            target_logw[None, :],
            source_logw.reshape(extra_rows, LANES),
            jnp.zeros((pad, own_targets), target_points.dtype),
        ],
        axis=0,
    )
    f32, bf16 = jnp.float32, jnp.bfloat16
    total = count * own_targets
    small = total <= 4096
    width = 2 * LANES if small else LANES
    vmem = pl.BlockSpec(memory_space=pltpu.VMEM)
    smem = pl.BlockSpec(memory_space=pltpu.SMEM)
    params = pltpu.CompilerParams(vmem_limit_bytes=(24 if small else 63) << 20)
    line = jax.ShapeDtypeStruct((1, total), f32)

    def call(kernel, operands, outs, scratch=(), scalars=1):
        return pl.pallas_call(
            kernel,
            out_shape=outs,
            in_specs=[smem] * scalars + [vmem] * (len(operands) - scalars),
            out_specs=[vmem] * len(outs),
            scratch_shapes=list(scratch),
            compiler_params=params,
        )(*operands)

    def staged_shape(parts):
        rows = sum(part.shape[0] for part in parts) * own_targets
        return jax.ShapeDtypeStruct((rows, DEPTH), bf16)

    def logw_line(parts):
        rows = [part[:, feat + 1 : feat + 1 + extra_rows] for part in parts]
        return jnp.concatenate(rows, axis=0).reshape(1, -1).astype(f32)

    packed, points = lax.optimization_barrier((packed, source_points))
    mine = gather_chips(packed, count)
    theirs = [swap(part, count, 1) for part in mine]
    later, _ = lax.optimization_barrier((points, mine[0]))
    parts, low = len(mine), chip_stages(count)[-1][0]
    ts = mine + theirs
    (taug_mine,) = call(
        functools.partial(part_kernel, feat),
        [inverse_eps, mine[0]],
        [staged_shape(mine[:1])],
    )
    (taug_theirs,) = call(
        functools.partial(part_kernel, feat),
        [inverse_eps, theirs[0]],
        [staged_shape(theirs[:1])],
    )
    (taug_rest,) = call(
        functools.partial(part_kernel, feat),
        [inverse_eps] + mine[1:],
        [staged_shape(mine[1:])],
    )
    xs = gather_line(points, later, count)
    logws = logw_line(mine[:1])
    rows = logws.shape[1]

    p_scratch = pltpu.VMEM((total, width), f32)
    scratch = [
        p_scratch,
        p_scratch if small else pltpu.VMEM((8, LANES), f32),
        pltpu.VMEM((total, LANES), f32),
    ]
    xaug, taug, sums, logw, q = call(
        functools.partial(near_kernel, parts, feat),
        [inverse_eps, logws, xs, taug_mine, taug_rest, taug_theirs] + ts,
        [
            jax.ShapeDtypeStruct((DEPTH, rows), bf16),
            jax.ShapeDtypeStruct((total, DEPTH), bf16),
            line,
            line,
            line,
        ],
        scratch,
    )
    flips = [(core, digit) for core in range(2) for digit in range(parts)]

    def exchange(own):
        steps = [core | (digit << low) for core, digit in flips]
        return [own] + [swap(own, count, step) for step in steps[1:]]

    g = logw
    for _ in range(ITERS - 1):
        sums, g = call(
            functools.partial(next_kernel, flips, parts),
            [logws, xaug, taug, g, q, logw] + exchange(sums),
            [line, line],
            [pltpu.VMEM((total, DEPTH), bf16)] + scratch,
            scalars=0,
        )
    mapped, potential = call(
        functools.partial(map_kernel, flips, parts, len(ts), feat),
        [xaug if small else xaug[:, :own_sources], taug, g, q, logw] + exchange(sums) + ts,
        [
            jax.ShapeDtypeStruct((feat, own_sources), f32),
            jax.ShapeDtypeStruct((1, own_targets), f32),
        ],
        [
            pltpu.VMEM((total, DEPTH), bf16),
            pltpu.VMEM((total, own_sources), f32),
            pltpu.VMEM((total, own_sources), bf16),
            pltpu.VMEM((feat, total), bf16),
        ],
        scalars=0,
    )
    return (mapped, potential.reshape(own_targets))


def solution(mesh):
    count = mesh.shape[AXIS]
    placed = (
        P(None, ("grp", "wide")),
        P(None, ("grp", "wide")),
        P(("grp", "wide")),
        P(("grp", "wide")),
        P(),
    )

    def body(*blocks):
        return on_device(*blocks, count)

    return jax.shard_map(
        body,
        mesh=mesh,
        in_specs=placed,
        out_specs=(P(None, ("grp", "wide")), P(("grp", "wide"))),
        check_vma=False,
    )
```

```python
import functools
import math

import jax
import jax.numpy as jnp
from jax import lax
from jax.experimental import pallas as pl
from jax.experimental.pallas import tpu as pltpu
from jax.sharding import PartitionSpec as P

ITERS = 2
AXIS = "wide"
LOG2E = math.log2(math.e)
LANES = 128
DEPTH = 256
SMALL_ROW = 2.0**-64
SMALL_COL = 2.0**-32
LARGE_COL = 2.0**100
FLOOR = -1e30


def three_terms(value):
    high = value.astype(jnp.bfloat16)
    rest = value - high.astype(jnp.float32)
    middle = rest.astype(jnp.bfloat16)
    low = (rest - middle.astype(jnp.float32)).astype(jnp.bfloat16)
    return high, middle, low


def pick_rows(shape, rows):
    index = lax.broadcasted_iota(jnp.int32, shape, 0)
    out = jnp.zeros(shape, jnp.float32)
    for place, row in enumerate(rows):
        out = jnp.where(index == place, row, out)
    return out


def stage_source(points, scale, xaug, at):
    feat, count = points.shape
    wide = points.astype(jnp.float32)
    shift = scale * jnp.sum(wide * wide, axis=0, keepdims=True)
    shift = shift.astype(jnp.bfloat16).astype(jnp.float32)
    xaug[0:feat, at] = pick_rows((feat, count), [1.0, 1.0, 1.0, -shift]).astype(jnp.bfloat16)
    for place, term in enumerate(three_terms(2.0 * scale * wide)):
        xaug[(place + 1) * feat : (place + 2) * feat, at] = term


def stage_sources(parts, scale, xaug, begin=0):
    for part in parts:
        count = part.shape[2]
        for block in range(part.shape[0]):
            stage_source(part[block], scale, xaug, slice(begin, begin + count))
            begin += count


def target_lines(part, block, scale, feat):
    wide = part[block, :feat, :].astype(jnp.float32)
    logw = part[block, feat : feat + 16, :].astype(jnp.float32)[0:1]
    return scale * jnp.sum(wide * wide, axis=0, keepdims=True), logw * LOG2E


def stage_targets(parts, scale, taug, begin, feat):
    for part in parts:
        for block in range(part.shape[0]):
            q, logw = target_lines(part, block, scale, feat)
            terms = [term.astype(jnp.float32) for term in three_terms(logw - q)]
            extras = pick_rows((feat, LANES), terms + [1.0])
            wide = part[block, :feat, :].astype(jnp.float32)
            turned = jnp.concatenate([extras, wide], axis=0).T
            lane = lax.broadcasted_iota(jnp.int32, turned.shape, 1)
            twice = jnp.where(lane < feat, pltpu.roll(turned, feat, 1), turned)
            taug[begin : begin + LANES, 0:LANES] = turned.astype(jnp.bfloat16)
            taug[begin : begin + LANES, LANES:DEPTH] = twice.astype(jnp.bfloat16)
            begin += LANES


def join_lines(lines, flips, parts, g):
    total = lines[0].shape[1]
    size = total // (2 * parts)
    held = []
    for line, (core, digit) in zip(lines, flips):
        value = line[...]
        places = [(block ^ (core * parts)) ^ digit for block in range(2 * parts)]
        pieces = [value[:, place * size : (place + 1) * size] for place in places]
        held.append(jnp.concatenate(pieces, axis=1))
    peak = functools.reduce(jnp.maximum, held)
    added = functools.reduce(jnp.add, [jnp.exp2(value - peak) for value in held])
    return g - (peak + jnp.log2(added))


def renew_targets(g, q, taug):
    terms = [term.astype(jnp.float32) for term in three_terms(g - jnp.max(g) - q)]
    for begin in range(0, g.shape[1], LANES):
        rows = slice(begin, begin + LANES)
        extras = pick_rows((8, LANES), [term[:, rows] for term in terms] + [1.0])
        taug[rows, 0:8] = extras.T.astype(jnp.bfloat16)


def exponents(left, right):
    return jnp.dot(left, right, preferred_element_type=jnp.float32)


def spread_rows(taug, right, p_ref, beside):
    total, width = taug.shape[0], right.shape[1]
    reach = min(total, 512)
    sums = jnp.zeros((8, width), jnp.float32)
    for begin in range(0, total, reach):
        e = exponents(taug[begin : begin + reach, :], right)
        for inner in range(0, reach, LANES):
            rows = slice(begin + inner, begin + inner + LANES)
            beside(rows)
            p = jnp.exp2(e[inner : inner + LANES])
            p_ref[rows, :] = p
            sums = sums + jnp.sum(p.reshape(LANES // 8, 8, width), axis=0)
    return jnp.sum(sums, axis=0, keepdims=True)


def add_columns(p_ref, weight, col_ref, rows):
    width = weight.shape[1]
    added = p_ref[rows, 0:LANES] * weight[:, 0:LANES]
    for lane in range(LANES, width, LANES):
        added = added + p_ref[rows, lane : lane + LANES] * weight[:, lane : lane + LANES]
    col_ref[rows, :] += added


def tile_columns(tile, width):
    if isinstance(tile, int):
        return pl.ds(tile * width, width)
    return pl.ds(pl.multiple_of(tile * width, width), width)


def add_sources(xaug, logws, taug, p_refs, col_ref):
    total = taug.shape[0]
    width = p_refs[0].shape[1]
    tiles = xaug.shape[1] // width
    if p_refs[1].shape != p_refs[0].shape:
        p_refs = (p_refs[0], p_refs[0])

    def step(tile, slot, held):
        def beside(rows):
            if held is not None:
                add_columns(p_refs[1 - slot], held, col_ref, rows)

        at = tile_columns(tile, width)
        s = spread_rows(taug, xaug[:, at], p_refs[slot], beside)
        return s, jnp.exp2(logws[:, at] * LOG2E) / s

    def two_steps(pair, carry):
        least, weight = carry
        s1, weight1 = step(2 * pair + 1, 1, weight)
        s0, weight0 = step(2 * pair + 2, 0, weight1)
        return jnp.minimum(least, jnp.minimum(s0, s1)), weight0

    s, weight = step(0, 0, None)
    least, weight = lax.fori_loop(0, tiles // 2 - 1, two_steps, (s, weight))
    s, weight = step(tiles - 1, 1, weight)
    for begin in range(0, total, LANES):
        add_columns(p_refs[1], weight, col_ref, slice(begin, begin + LANES))
    return jnp.minimum(least, s)


def keep_sources(xaug, logws, taug, p_ref, col_ref):
    total, sources = p_ref.shape
    width = 2 * LANES
    held, least = None, None
    for begin in range(0, sources + width, width):

        def beside(rows):
            if held is not None:
                add_columns(p_ref.at[:, begin - width : begin], held, col_ref, rows)

        if begin == sources:
            for first in range(0, total, LANES):
                beside(slice(first, first + LANES))
            return least
        at = slice(begin, begin + width)
        s = spread_rows(taug, xaug[:, at], p_ref.at[:, at], beside)
        held = jnp.exp2(logws[:, at] * LOG2E) / s
        least = s if least is None else jnp.minimum(least, s)


def lane_totals(col_ref, out_ref):
    total = col_ref.shape[0]
    reach = min(total, 2048)
    ones = jnp.ones((16, 2 * LANES), jnp.bfloat16)
    for begin in range(0, total, reach):
        high, middle, _ = three_terms(col_ref[begin : begin + reach, :])
        both = jnp.concatenate([high, middle], axis=1)
        added = lax.dot_general(
            ones, both, (((1,), (1,)), ((), ())), preferred_element_type=jnp.float32
        )
        out_ref[:, begin : begin + reach] = added[0:1]


def finish_sums(xaug, logws, taug, renew, factor, least, top_ref, col_ref, out_ref):
    total = taug.shape[0]
    lane_totals(col_ref, out_ref)
    cols = out_ref[...]
    out_ref[...] = jnp.log2(cols) + factor
    fine = jnp.logical_and(
        jnp.min(least) >= SMALL_ROW,
        jnp.logical_and(jnp.min(cols) >= SMALL_COL, jnp.max(cols) <= LARGE_COL),
    )


    @pl.when(jnp.logical_not(fine))
    def _():
        renew()
        col_ref[...] = jnp.zeros_like(col_ref)
        top_ref[...] = jnp.full_like(top_ref, FLOOR)
        blocks = total // LANES

        def block_rows(block):
            return pl.ds(pl.multiple_of(block * LANES, LANES), LANES)

        def careful(tile, carry):
            at = tile_columns(tile, LANES)
            right = xaug[:, at]

            def highest(block, peak):
                e = exponents(taug[block_rows(block), :], right)
                return jnp.maximum(peak, jnp.max(e, axis=0, keepdims=True))

            peak = lax.fori_loop(0, blocks, highest, jnp.full((1, LANES), FLOOR, jnp.float32))

            def summed(block, s):
                e = exponents(taug[block_rows(block), :], right)
                return s + jnp.sum(jnp.exp2(e - peak), axis=0, keepdims=True)

            s = lax.fori_loop(0, blocks, summed, jnp.zeros((1, LANES), jnp.float32))
            shift = logws[:, at] * LOG2E - peak - jnp.log2(s)

            def collected(block, carry):
                rows = block_rows(block)
                term = exponents(taug[rows, :], right) + shift
                old = top_ref[rows, :]
                top = jnp.maximum(old, term)
                col_ref[rows, :] = col_ref[rows, :] * jnp.exp2(old - top) + jnp.exp2(term - top)
                top_ref[rows, :] = top
                return carry

            return lax.fori_loop(0, blocks, collected, carry)

        lax.fori_loop(0, xaug.shape[1] // LANES, careful, 0)

        def turned(block, carry):
            rows = block_rows(block)
            tops = top_ref[rows, :].T
            top = jnp.max(tops, axis=0, keepdims=True)
            added = jnp.sum(col_ref[rows, :].T * jnp.exp2(tops - top), axis=0, keepdims=True)
            out_ref[:, rows] = top + jnp.log2(added)
            return carry

        lax.fori_loop(0, blocks, turned, 0)


def part_kernel(feat, inverse, *refs):
    stage_targets(refs[:-1], inverse[0] * LOG2E, refs[-1], 0, feat)


def near_kernel(parts, feat, inverse, logws, xs, mine, rest, theirs, *refs):
    ts, refs = refs[: 2 * parts], refs[2 * parts :]
    xaug, taug, out_ref, g_ref, q_ref = refs[:5]
    p_refs, (col_ref, top_ref) = refs[5:-2], refs[-2:]
    scale = inverse[0] * LOG2E
    stage_sources([xs], scale, xaug)
    place = 0
    for part in ts:
        for block in range(part.shape[0]):
            at = slice(place * LANES, (place + 1) * LANES)
            q_ref[:, at], g_ref[:, at] = target_lines(part, block, scale, feat)
            place += 1
    begin = 0
    for part in (mine, rest, theirs):
        taug[begin : begin + part.shape[0], :] = part[...]
        begin += part.shape[0]
    stage_targets(ts[parts + 1 :], scale, taug, begin, feat)
    col_ref[...] = jnp.zeros_like(col_ref)
    if len(p_refs) == 1:
        least = keep_sources(xaug, logws, taug, p_refs[0], col_ref)
    else:
        least = add_sources(xaug, logws, taug, p_refs, col_ref)
    finish_sums(xaug, logws, taug, lambda: None, 0.0, least, top_ref, col_ref, out_ref)


def next_kernel(flips, parts, logws, xaug, old, g, q, logw, *refs):
    lines, refs = refs[: len(flips)], refs[len(flips) :]
    out_ref, g_ref, taug, p0, p1, col_ref, top_ref = refs
    taug[...] = old[...]
    g_ref[...] = join_lines(lines, flips, parts, g[...]) + logw[...]
    renew_targets(g_ref[...], q[...], taug)
    col_ref[...] = jnp.zeros_like(col_ref)
    least = add_sources(xaug, logws, taug, (p0, p1), col_ref)
    finish_sums(xaug, logws, taug, lambda: None, 0.0, least, top_ref, col_ref, out_ref)


def spread_factors(exponent, factor_ref):
    f = jnp.exp2(exponent)
    for begin in range(0, f.shape[1], LANES):
        rows = slice(begin, begin + LANES)
        turned = pick_rows((8, LANES), [f[:, rows]]).T
        factor_ref[rows, :] = jnp.broadcast_to(turned[:, 0:1], (LANES, LANES))


def factor_sums(p, factor_ref):
    total, width = p.shape
    reach = 4 * LANES

    def advance(step, sums):
        for inner in range(0, reach, LANES):
            rows = pl.ds(pl.multiple_of(step * reach + inner, LANES), LANES)
            factor = factor_ref[rows, :]
            sums = [
                held
                + jnp.sum(
                    (p[rows, place * LANES : (place + 1) * LANES] * factor).reshape(-1, 8, LANES),
                    axis=0,
                )
                for place, held in enumerate(sums)
            ]
        return tuple(sums)

    start = (jnp.zeros((8, LANES), jnp.float32),) * (width // LANES)
    sums = lax.fori_loop(0, total // reach, advance, start)
    return [jnp.sum(held, axis=0, keepdims=True) for held in sums]


def kept_kernel(flips, parts, logws, xaug, old, g, q, logw, p, *refs):
    lines, refs = refs[: len(flips)], refs[len(flips) :]
    out_ref, g_ref, taug, factor_ref, col_ref, top_ref = refs
    potential = join_lines(lines, flips, parts, g[...])
    g_ref[...] = potential + logw[...]
    change = potential - jnp.max(potential)
    spread_factors(change, factor_ref)
    sums = factor_sums(p, factor_ref)
    tiles = [slice(place * LANES, (place + 1) * LANES) for place in range(len(sums))]
    weights = [
        jnp.broadcast_to(jnp.exp2(logws[:, tile] * LOG2E) / s, (8, LANES))
        for tile, s in zip(tiles, sums)
    ]
    reach = 4 * LANES

    def collect(step, carry):
        for inner in range(0, reach, LANES):
            rows = pl.ds(pl.multiple_of(step * reach + inner, LANES), LANES)
            added = [
                p[rows, tile].reshape(-1, 8, LANES) * weight[None]
                for tile, weight in zip(tiles, weights)
            ]
            col_ref[rows, :] = functools.reduce(jnp.add, added).reshape(LANES, LANES)
        return carry

    lax.fori_loop(0, p.shape[0] // reach, collect, 0)

    def renew():
        taug[...] = old[...]
        renew_targets(g_ref[...], q[...], taug)

    least = functools.reduce(jnp.minimum, sums)
    finish_sums(xaug, logws, taug, renew, change, least, top_ref, col_ref, out_ref)


def write_coords(ts, feat, coords):
    begin = 0
    for part in ts:
        for block in range(part.shape[0]):
            coords[:, begin : begin + LANES] = part[block, :feat, :]
            begin += LANES


def careful_plan(taug, right, p_ref, plan_ref):
    total = taug.shape[0]
    reach = min(total, 2048)
    pieces = [slice(begin, begin + reach) for begin in range(0, total, reach)]
    peak = jnp.full((1, p_ref.shape[1]), FLOOR, jnp.float32)
    for rows in pieces:
        p_ref[rows, :] = exponents(taug[rows, :], right)
        peak = jnp.maximum(peak, jnp.max(p_ref[rows, :], axis=0, keepdims=True))
    sums = jnp.zeros(peak.shape, jnp.float32)
    for rows in pieces:
        sums += jnp.sum(jnp.exp2(p_ref[rows, :] - peak), axis=0, keepdims=True)
    shift = peak + jnp.log2(sums)
    for rows in pieces:
        plan_ref[rows, :] = jnp.exp2(p_ref[rows, :] - shift).astype(jnp.bfloat16)


def map_kernel(flips, parts, n_t, feat, xaug, old, g, q, logw, *refs):
    lines, refs = refs[: len(flips)], refs[len(flips) :]
    ts = refs[:n_t]
    mapped_ref, pot_ref, taug, p_ref, plan_ref, coords = refs[n_t:]
    taug[...] = old[...]
    potential = join_lines(lines, flips, parts, g[...])
    renew_targets(potential + logw[...], q[...], taug)
    pot_ref[...] = potential[:, :LANES] * (1.0 / LOG2E)
    write_coords(ts, feat, coords)
    total = taug.shape[0]
    right = xaug[:, : p_ref.shape[1]]
    s = spread_rows(taug, right, p_ref, lambda rows: None)
    weight = 1.0 / s
    for begin in range(0, total, LANES):
        rows = slice(begin, begin + LANES)
        plan_ref[rows, :] = (p_ref[rows, :] * weight).astype(jnp.bfloat16)

    @pl.when(jnp.logical_not(jnp.min(s) >= SMALL_ROW))
    def _():
        careful_plan(taug, right, p_ref, plan_ref)

    mapped_ref[...] = jnp.dot(coords[...], plan_ref[...], preferred_element_type=jnp.float32)


def map_kept_kernel(flips, parts, n_t, feat, xaug, old, g, q, logw, p, *refs):
    lines, refs = refs[: len(flips)], refs[len(flips) :]
    ts = refs[:n_t]
    mapped_ref, pot_ref, taug, p_ref, plan_ref, coords, factor_ref = refs[n_t:]
    potential = join_lines(lines, flips, parts, g[...])
    pot_ref[...] = potential[:, :LANES] * (1.0 / LOG2E)
    write_coords(ts, feat, coords)
    spread_factors(potential - jnp.max(potential), factor_ref)
    total, width = p_ref.shape
    sums = factor_sums(p.at[:, 0:width], factor_ref)
    for place, s in enumerate(sums):
        tile = slice(place * LANES, (place + 1) * LANES)
        weight = 1.0 / s
        for begin in range(0, total, LANES):
            rows = slice(begin, begin + LANES)
            value = p[rows, tile] * factor_ref[rows, :] * weight
            plan_ref[rows, tile] = value.astype(jnp.bfloat16)

    @pl.when(jnp.logical_not(jnp.min(functools.reduce(jnp.minimum, sums)) >= SMALL_ROW))
    def _():
        taug[...] = old[...]
        renew_targets(potential + logw[...], q[...], taug)
        careful_plan(taug, xaug[:, 0:width], p_ref, plan_ref)

    mapped_ref[...] = jnp.dot(coords[...], plan_ref[...], preferred_element_type=jnp.float32)


def swap(value, count, step):
    return lax.ppermute(value, AXIS, [(source, source ^ step) for source in range(count)])


def chip_stages(count):
    high, stages = count.bit_length() - 1, []
    while high > 1:
        width = min(2, high - 1)
        stages.append((high - width, width))
        high -= width
    return stages


def gather_stage(parts, count, low, width):
    held = parts[0] if len(parts) == 1 else jnp.concatenate(parts, axis=0)
    return [held] + [swap(held, count, digit << low) for digit in range(1, 1 << width)]


def gather_chips(block, count):
    parts = [block[None]]
    for low, width in chip_stages(count):
        parts = gather_stage(parts, count, low, width)
    return parts


def gather_line(block, count):
    parts = [block[None]]
    for low, width in chip_stages(count)[:-1]:
        parts = gather_stage(parts, count, low, width)
    return jnp.concatenate(parts, axis=0)


def on_device(source_points, target_points, source_logw, target_logw, inverse_eps, count):
    feat, own_sources = source_points.shape
    own_targets = target_points.shape[1]
    extra_rows = own_sources // LANES
    pad = -(1 + extra_rows) % 16
    packed = jnp.concatenate(
        [
            target_points,
            target_logw[None, :],
            source_logw.reshape(extra_rows, LANES),
            jnp.zeros((pad, own_targets), target_points.dtype),
        ],
        axis=0,
    )
    f32, bf16 = jnp.float32, jnp.bfloat16
    total = count * own_targets
    small = total <= 4096
    vmem = pl.BlockSpec(memory_space=pltpu.VMEM)
    smem = pl.BlockSpec(memory_space=pltpu.SMEM)
    params = pltpu.CompilerParams(vmem_limit_bytes=(24 if small else 63) << 20)
    line = jax.ShapeDtypeStruct((1, total), f32)

    def call(kernel, operands, outs, scratch=(), scalars=1):
        return pl.pallas_call(
            kernel,
            out_shape=outs,
            in_specs=[smem] * scalars + [vmem] * (len(operands) - scalars),
            out_specs=[vmem] * len(outs),
            scratch_shapes=list(scratch),
            compiler_params=params,
        )(*operands)

    def staged_shape(parts):
        rows = sum(part.shape[0] for part in parts) * own_targets
        return jax.ShapeDtypeStruct((rows, DEPTH), bf16)

    def logw_line(parts):
        rows = [part[:, feat + 1 : feat + 1 + extra_rows] for part in parts]
        return jnp.concatenate(rows, axis=0).reshape(1, -1).astype(f32)

    packed, points = lax.optimization_barrier((packed, source_points))
    mine = gather_chips(packed, count)
    theirs = [swap(part, count, 1) for part in mine]
    parts, low = len(mine), chip_stages(count)[-1][0]
    ts = mine + theirs
    (taug_mine,) = call(
        functools.partial(part_kernel, feat),
        [inverse_eps, mine[0]],
        [staged_shape(mine[:1])],
    )
    (taug_theirs,) = call(
        functools.partial(part_kernel, feat),
        [inverse_eps, theirs[0]],
        [staged_shape(theirs[:1])],
    )
    (taug_rest,) = call(
        functools.partial(part_kernel, feat),
        [inverse_eps] + mine[1:],
        [staged_shape(mine[1:])],
    )
    xs = gather_line(points, count)
    logws = logw_line(mine[:1])
    rows = logws.shape[1]

    flips = [(core, digit) for digit in range(parts) for core in range(2)]
    kept = [jax.ShapeDtypeStruct((total, rows), f32)] if small else []
    lanes_scratch = pltpu.VMEM((total, LANES), f32)
    taug_scratch = pltpu.VMEM((total, DEPTH), bf16)
    p_scratch = [] if small else [pltpu.VMEM((total, LANES), f32), pltpu.VMEM((8, LANES), f32)]

    def exchange(own):
        return [own] + [swap(own, count, core | (digit << low)) for core, digit in flips[1:]]

    xaug, taug, sums, logw, q, *p = call(
        functools.partial(near_kernel, parts, feat),
        [inverse_eps, logws, xs, taug_mine, taug_rest, taug_theirs] + ts,
        [
            jax.ShapeDtypeStruct((DEPTH, rows), bf16),
            jax.ShapeDtypeStruct((total, DEPTH), bf16),
            line,
            line,
            line,
        ]
        + kept,
        p_scratch + [lanes_scratch, lanes_scratch],
    )
    g = logw
    for _ in range(ITERS - 1):
        sums, g = call(
            functools.partial(kept_kernel if small else next_kernel, flips, parts),
            [logws, xaug, taug, g, q, logw] + p + exchange(sums),
            [line, line],
            [taug_scratch]
            + ([lanes_scratch] if small else p_scratch)
            + [lanes_scratch, lanes_scratch],
            scalars=0,
        )
    mapped, potential = call(
        functools.partial(map_kept_kernel if small else map_kernel, flips, parts, len(ts), feat),
        [xaug if small else xaug[:, :own_sources], taug, g, q, logw] + p + exchange(sums) + ts,
        [
            jax.ShapeDtypeStruct((feat, own_sources), f32),
            jax.ShapeDtypeStruct((1, own_targets), f32),
        ],
        [
            taug_scratch,
            pltpu.VMEM((total, own_sources), f32),
            pltpu.VMEM((total, own_sources), bf16),
            pltpu.VMEM((feat, total), bf16),
        ]
        + ([lanes_scratch] if small else []),
        scalars=0,
    )
    return (mapped, potential.reshape(own_targets))


def solution(mesh):
    count = mesh.shape[AXIS]
    placed = (
        P(None, ("grp", "wide")),
        P(None, ("grp", "wide")),
        P(("grp", "wide")),
        P(("grp", "wide")),
        P(),
    )

    def body(*blocks):
        return on_device(*blocks, count)

    return jax.shard_map(
        body,
        mesh=mesh,
        in_specs=placed,
        out_specs=(P(None, ("grp", "wide")), P(("grp", "wide"))),
        check_vma=False,
    )
```

```python
import functools
import math

import jax
import jax.numpy as jnp
from jax import lax
from jax.experimental import pallas as pl
from jax.experimental.pallas import tpu as pltpu
from jax.sharding import PartitionSpec as P

ITERS = 2
AXIS = "wide"
LOG2E = math.log2(math.e)
LANES = 128
DEPTH = 256
SMALL_ROW = 2.0**-64
SMALL_COL = 2.0**-32
LARGE_COL = 2.0**100
FLOOR = -1e30


def three_terms(value):
    high = value.astype(jnp.bfloat16)
    rest = value - high.astype(jnp.float32)
    middle = rest.astype(jnp.bfloat16)
    low = (rest - middle.astype(jnp.float32)).astype(jnp.bfloat16)
    return high, middle, low


def pick_rows(shape, rows):
    index = lax.broadcasted_iota(jnp.int32, shape, 0)
    out = jnp.zeros(shape, jnp.float32)
    for place, row in enumerate(rows):
        out = jnp.where(index == place, row, out)
    return out


def stage_source(points, scale, xaug, at):
    feat, count = points.shape
    wide = points.astype(jnp.float32)
    shift = scale * jnp.sum(wide * wide, axis=0, keepdims=True)
    shift = shift.astype(jnp.bfloat16).astype(jnp.float32)
    xaug[0:feat, at] = pick_rows((feat, count), [1.0, 1.0, 1.0, -shift]).astype(jnp.bfloat16)
    for place, term in enumerate(three_terms(2.0 * scale * wide)):
        xaug[(place + 1) * feat : (place + 2) * feat, at] = term


def stage_sources(parts, scale, xaug, begin=0):
    for part in parts:
        count = part.shape[2]
        for block in range(part.shape[0]):
            stage_source(part[block], scale, xaug, slice(begin, begin + count))
            begin += count


def target_lines(part, block, scale, feat):
    wide = part[block, :feat, :].astype(jnp.float32)
    logw = part[block, feat : feat + 16, :].astype(jnp.float32)[0:1]
    return scale * jnp.sum(wide * wide, axis=0, keepdims=True), logw * LOG2E


def stage_targets(parts, scale, taug, begin, feat):
    for part in parts:
        for block in range(part.shape[0]):
            q, logw = target_lines(part, block, scale, feat)
            terms = [term.astype(jnp.float32) for term in three_terms(logw - q)]
            extras = pick_rows((feat, LANES), terms + [1.0])
            wide = part[block, :feat, :].astype(jnp.float32)
            turned = jnp.concatenate([extras, wide], axis=0).T
            lane = lax.broadcasted_iota(jnp.int32, turned.shape, 1)
            twice = jnp.where(lane < feat, pltpu.roll(turned, feat, 1), turned)
            taug[begin : begin + LANES, 0:LANES] = turned.astype(jnp.bfloat16)
            taug[begin : begin + LANES, LANES:DEPTH] = twice.astype(jnp.bfloat16)
            begin += LANES


def renew_targets(lines, flips, parts, g, q, logw, taug):
    total = lines[0].shape[1]
    size = total // (2 * parts)
    held = []
    for line, (core, digit) in zip(lines, flips):
        value = line[...]
        places = [(block ^ (core * parts)) ^ digit for block in range(2 * parts)]
        pieces = [value[:, place * size : (place + 1) * size] for place in places]
        held.append(jnp.concatenate(pieces, axis=1))
    peak = functools.reduce(jnp.maximum, held)
    added = functools.reduce(jnp.add, [jnp.exp2(value - peak) for value in held])
    potential = g - (peak + jnp.log2(added))
    g = potential + logw
    terms = [term.astype(jnp.float32) for term in three_terms(g - jnp.max(g) - q)]
    for begin in range(0, total, LANES):
        rows = slice(begin, begin + LANES)
        extras = pick_rows((8, LANES), [term[:, rows] for term in terms] + [1.0])
        taug[rows, 0:8] = extras.T.astype(jnp.bfloat16)
    return potential, g


def exponents(left, right):
    return jnp.dot(left, right, preferred_element_type=jnp.float32)


def spread_rows(taug, right, p_ref, beside):
    total, width = taug.shape[0], right.shape[1]
    reach = min(total, 512)
    sums = jnp.zeros((8, width), jnp.float32)
    for begin in range(0, total, reach):
        e = exponents(taug[begin : begin + reach, :], right)
        for inner in range(0, reach, LANES):
            rows = slice(begin + inner, begin + inner + LANES)
            beside(rows)
            p = jnp.exp2(e[inner : inner + LANES])
            p_ref[rows, :] = p
            sums = sums + jnp.sum(p.reshape(LANES // 8, 8, width), axis=0)
    return jnp.sum(sums, axis=0, keepdims=True)


def add_columns(p_ref, weight, col_ref, rows):
    width = weight.shape[1]
    added = p_ref[rows, 0:LANES] * weight[:, 0:LANES]
    for lane in range(LANES, width, LANES):
        added = added + p_ref[rows, lane : lane + LANES] * weight[:, lane : lane + LANES]
    col_ref[rows, :] += added


def tile_columns(tile, width):
    if isinstance(tile, int):
        return pl.ds(tile * width, width)
    return pl.ds(pl.multiple_of(tile * width, width), width)


def add_sources(xaug, logws, taug, p_ref, col_ref):
    buffers, total, width = p_ref.shape
    tiles = xaug.shape[1] // width

    def step(tile, held):
        def beside(rows):
            if held is not None:
                add_columns(p_ref.at[(tile + 1) % buffers], held, col_ref, rows)

        at = tile_columns(tile, width)
        s = spread_rows(taug, xaug[:, at], p_ref.at[tile % buffers], beside)
        return s, jnp.exp2(logws[:, at] * LOG2E) / s

    def advance(tile, carry):
        s, weight = step(tile, carry[1])
        return jnp.minimum(carry[0], s), weight

    least, weight = lax.fori_loop(1, tiles, advance, step(0, None))
    for begin in range(0, total, LANES):
        rows = slice(begin, begin + LANES)
        add_columns(p_ref.at[(tiles - 1) % buffers], weight, col_ref, rows)
    return least


def lane_totals(col_ref, out_ref):
    total = col_ref.shape[0]
    reach = min(total, 2048)
    ones = jnp.ones((16, 2 * LANES), jnp.bfloat16)
    for begin in range(0, total, reach):
        high, middle, _ = three_terms(col_ref[begin : begin + reach, :])
        both = jnp.concatenate([high, middle], axis=1)
        added = lax.dot_general(
            ones, both, (((1,), (1,)), ((), ())), preferred_element_type=jnp.float32
        )
        out_ref[:, begin : begin + reach] = added[0:1]


def finish_sums(xaug, logws, taug, least, p_ref, col_ref, out_ref):
    total = taug.shape[0]
    lane_totals(col_ref, out_ref)
    cols = out_ref[...]
    out_ref[...] = jnp.log2(cols)
    fine = jnp.logical_and(
        jnp.min(least) >= SMALL_ROW,
        jnp.logical_and(jnp.min(cols) >= SMALL_COL, jnp.max(cols) <= LARGE_COL),
    )

    top_ref = p_ref.at[:, 0:LANES]

    @pl.when(jnp.logical_not(fine))
    def _():
        col_ref[...] = jnp.zeros_like(col_ref)
        top_ref[...] = jnp.full_like(top_ref, FLOOR)
        blocks = total // LANES

        def block_rows(block):
            return pl.ds(pl.multiple_of(block * LANES, LANES), LANES)

        def careful(tile, carry):
            at = tile_columns(tile, LANES)
            right = xaug[:, at]

            def highest(block, peak):
                e = exponents(taug[block_rows(block), :], right)
                return jnp.maximum(peak, jnp.max(e, axis=0, keepdims=True))

            peak = lax.fori_loop(0, blocks, highest, jnp.full((1, LANES), FLOOR, jnp.float32))

            def summed(block, s):
                e = exponents(taug[block_rows(block), :], right)
                return s + jnp.sum(jnp.exp2(e - peak), axis=0, keepdims=True)

            s = lax.fori_loop(0, blocks, summed, jnp.zeros((1, LANES), jnp.float32))
            shift = logws[:, at] * LOG2E - peak - jnp.log2(s)

            def collected(block, carry):
                rows = block_rows(block)
                term = exponents(taug[rows, :], right) + shift
                old = top_ref[rows, :]
                top = jnp.maximum(old, term)
                col_ref[rows, :] = col_ref[rows, :] * jnp.exp2(old - top) + jnp.exp2(term - top)
                top_ref[rows, :] = top
                return carry

            return lax.fori_loop(0, blocks, collected, carry)

        lax.fori_loop(0, xaug.shape[1] // LANES, careful, 0)

        def turned(block, carry):
            rows = block_rows(block)
            tops = top_ref[rows, :].T
            top = jnp.max(tops, axis=0, keepdims=True)
            added = jnp.sum(col_ref[rows, :].T * jnp.exp2(tops - top), axis=0, keepdims=True)
            out_ref[:, rows] = top + jnp.log2(added)
            return carry

        lax.fori_loop(0, blocks, turned, 0)


def part_kernel(feat, inverse, *refs):
    stage_targets(refs[:-1], inverse[0] * LOG2E, refs[-1], 0, feat)


def near_kernel(parts, feat, inverse, logws, xs, mine, rest, theirs, *refs):
    ts, refs = refs[: 2 * parts], refs[2 * parts :]
    xaug, taug, out_ref, g_ref, q_ref, p_ref, col_ref = refs
    scale = inverse[0] * LOG2E
    stage_sources([xs], scale, xaug)
    place = 0
    for part in ts:
        for block in range(part.shape[0]):
            at = slice(place * LANES, (place + 1) * LANES)
            q_ref[:, at], g_ref[:, at] = target_lines(part, block, scale, feat)
            place += 1
    begin = 0
    for part in (mine, rest, theirs):
        taug[begin : begin + part.shape[0], :] = part[...]
        begin += part.shape[0]
    stage_targets(ts[parts + 1 :], scale, taug, begin, feat)
    col_ref[...] = jnp.zeros_like(col_ref)
    least = add_sources(xaug, logws, taug, p_ref, col_ref)
    finish_sums(xaug, logws, taug, least, p_ref.at[0], col_ref, out_ref)


def next_kernel(flips, parts, logws, xaug, old, g, q, logw, *refs):
    lines, refs = refs[: len(flips)], refs[len(flips) :]
    out_ref, g_ref, taug, p_ref, col_ref = refs
    taug[...] = old[...]
    g_ref[...] = renew_targets(lines, flips, parts, g[...], q[...], logw[...], taug)[1]
    col_ref[...] = jnp.zeros_like(col_ref)
    least = add_sources(xaug, logws, taug, p_ref, col_ref)
    finish_sums(xaug, logws, taug, least, p_ref.at[0], col_ref, out_ref)


def map_kernel(flips, parts, n_t, feat, xaug, old, g, q, logw, *refs):
    lines, refs = refs[: len(flips)], refs[len(flips) :]
    ts = refs[:n_t]
    mapped_ref, pot_ref, taug, p_ref, plan_ref, coords = refs[n_t:]
    taug[...] = old[...]
    potential = renew_targets(lines, flips, parts, g[...], q[...], logw[...], taug)[0]
    pot_ref[...] = potential[:, :LANES] * (1.0 / LOG2E)
    place = 0
    for part in ts:
        for block in range(part.shape[0]):
            coords[:, place * LANES : (place + 1) * LANES] = part[block, :feat, :]
            place += 1
    total = taug.shape[0]
    right = xaug[:, : p_ref.shape[1]]
    s = spread_rows(taug, right, p_ref, lambda rows: None)
    weight = 1.0 / s
    for begin in range(0, total, LANES):
        rows = slice(begin, begin + LANES)
        plan_ref[rows, :] = (p_ref[rows, :] * weight).astype(jnp.bfloat16)

    @pl.when(jnp.logical_not(jnp.min(s) >= SMALL_ROW))
    def _():
        reach = min(total, 2048)
        peak = jnp.full(s.shape, FLOOR, jnp.float32)
        for begin in range(0, total, reach):
            rows = slice(begin, begin + reach)
            p_ref[rows, :] = exponents(taug[rows, :], right)
            peak = jnp.maximum(peak, jnp.max(p_ref[rows, :], axis=0, keepdims=True))
        sums = jnp.zeros(s.shape, jnp.float32)
        for begin in range(0, total, reach):
            rows = slice(begin, begin + reach)
            sums += jnp.sum(jnp.exp2(p_ref[rows, :] - peak), axis=0, keepdims=True)
        shift = peak + jnp.log2(sums)
        for begin in range(0, total, reach):
            rows = slice(begin, begin + reach)
            plan_ref[rows, :] = jnp.exp2(p_ref[rows, :] - shift).astype(jnp.bfloat16)

    mapped_ref[...] = jnp.dot(coords[...], plan_ref[...], preferred_element_type=jnp.float32)


def swap(value, count, step):
    return lax.ppermute(value, AXIS, [(source, source ^ step) for source in range(count)])


def chip_stages(count):
    high, stages = count.bit_length() - 1, []
    while high > 1:
        width = min(2, high - 1)
        stages.append((high - width, width))
        high -= width
    return stages


def gather_stage(parts, count, low, width):
    held = parts[0] if len(parts) == 1 else jnp.concatenate(parts, axis=0)
    return [held] + [swap(held, count, digit << low) for digit in range(1, 1 << width)]


def gather_chips(block, count):
    parts = [block[None]]
    for low, width in chip_stages(count):
        parts = gather_stage(parts, count, low, width)
    return parts


def gather_line(block, count):
    parts = [block[None]]
    for low, width in chip_stages(count)[:-1]:
        parts = gather_stage(parts, count, low, width)
    return jnp.concatenate(parts, axis=0)


def on_device(source_points, target_points, source_logw, target_logw, inverse_eps, count):
    feat, own_sources = source_points.shape
    own_targets = target_points.shape[1]
    extra_rows = own_sources // LANES
    pad = -(1 + extra_rows) % 16
    packed = jnp.concatenate(
        [
            target_points,
            target_logw[None, :],
            source_logw.reshape(extra_rows, LANES),
            jnp.zeros((pad, own_targets), target_points.dtype),
        ],
        axis=0,
    )
    f32, bf16 = jnp.float32, jnp.bfloat16
    total = count * own_targets
    small = total <= 4096
    width = 2 * LANES if small else LANES
    vmem = pl.BlockSpec(memory_space=pltpu.VMEM)
    smem = pl.BlockSpec(memory_space=pltpu.SMEM)
    params = pltpu.CompilerParams(vmem_limit_bytes=(24 if small else 63) << 20)
    line = jax.ShapeDtypeStruct((1, total), f32)

    def call(kernel, operands, outs, scratch=(), scalars=1):
        return pl.pallas_call(
            kernel,
            out_shape=outs,
            in_specs=[smem] * scalars + [vmem] * (len(operands) - scalars),
            out_specs=[vmem] * len(outs),
            scratch_shapes=list(scratch),
            compiler_params=params,
        )(*operands)

    def staged_shape(parts):
        rows = sum(part.shape[0] for part in parts) * own_targets
        return jax.ShapeDtypeStruct((rows, DEPTH), bf16)

    def logw_line(parts):
        rows = [part[:, feat + 1 : feat + 1 + extra_rows] for part in parts]
        return jnp.concatenate(rows, axis=0).reshape(1, -1).astype(f32)

    packed, points = lax.optimization_barrier((packed, source_points))
    mine = gather_chips(packed, count)
    theirs = [swap(part, count, 1) for part in mine]
    parts, low = len(mine), chip_stages(count)[-1][0]
    ts = mine + theirs
    (taug_mine,) = call(
        functools.partial(part_kernel, feat),
        [inverse_eps, mine[0]],
        [staged_shape(mine[:1])],
    )
    (taug_theirs,) = call(
        functools.partial(part_kernel, feat),
        [inverse_eps, theirs[0]],
        [staged_shape(theirs[:1])],
    )
    (taug_rest,) = call(
        functools.partial(part_kernel, feat),
        [inverse_eps] + mine[1:],
        [staged_shape(mine[1:])],
    )
    xs = gather_line(points, count)
    logws = logw_line(mine[:1])
    rows = logws.shape[1]

    scratch = [
        pltpu.VMEM((2 if small else 1, total, width), f32),
        pltpu.VMEM((total, LANES), f32),
    ]
    xaug, taug, sums, logw, q = call(
        functools.partial(near_kernel, parts, feat),
        [inverse_eps, logws, xs, taug_mine, taug_rest, taug_theirs] + ts,
        [
            jax.ShapeDtypeStruct((DEPTH, rows), bf16),
            jax.ShapeDtypeStruct((total, DEPTH), bf16),
            line,
            line,
            line,
        ],
        scratch,
    )
    flips = [(core, digit) for digit in range(parts) for core in range(2)]

    def exchange(own):
        return [own] + [swap(own, count, core | (digit << low)) for core, digit in flips[1:]]

    g = logw
    for _ in range(ITERS - 1):
        sums, g = call(
            functools.partial(next_kernel, flips, parts),
            [logws, xaug, taug, g, q, logw] + exchange(sums),
            [line, line],
            [pltpu.VMEM((total, DEPTH), bf16)] + scratch,
            scalars=0,
        )
    mapped, potential = call(
        functools.partial(map_kernel, flips, parts, len(ts), feat),
        [xaug if small else xaug[:, :own_sources], taug, g, q, logw] + exchange(sums) + ts,
        [
            jax.ShapeDtypeStruct((feat, own_sources), f32),
            jax.ShapeDtypeStruct((1, own_targets), f32),
        ],
        [
            pltpu.VMEM((total, DEPTH), bf16),
            pltpu.VMEM((total, own_sources), f32),
            pltpu.VMEM((total, own_sources), bf16),
            pltpu.VMEM((feat, total), bf16),
        ],
        scalars=0,
    )
    return (mapped, potential.reshape(own_targets))


def solution(mesh):
    count = mesh.shape[AXIS]
    placed = (
        P(None, ("grp", "wide")),
        P(None, ("grp", "wide")),
        P(("grp", "wide")),
        P(("grp", "wide")),
        P(),
    )

    def body(*blocks):
        return on_device(*blocks, count)

    return jax.shard_map(
        body,
        mesh=mesh,
        in_specs=placed,
        out_specs=(P(None, ("grp", "wide")), P(("grp", "wide"))),
        check_vma=False,
    )
```

```python
import functools
import math

import jax
import jax.numpy as jnp
from jax import lax
from jax.experimental import pallas as pl
from jax.experimental.pallas import tpu as pltpu
from jax.sharding import PartitionSpec as P

ITERS = 2
AXIS = "wide"
LOG2E = math.log2(math.e)
LANES = 128
DEPTH = 256
SMALL_ROW = 2.0**-64
SMALL_COL = 2.0**-32
LARGE_COL = 2.0**100
FLOOR = -1e30


def three_terms(value):
    high = value.astype(jnp.bfloat16)
    rest = value - high.astype(jnp.float32)
    middle = rest.astype(jnp.bfloat16)
    low = (rest - middle.astype(jnp.float32)).astype(jnp.bfloat16)
    return high, middle, low


def pick_rows(shape, rows):
    index = lax.broadcasted_iota(jnp.int32, shape, 0)
    out = jnp.zeros(shape, jnp.float32)
    for place, row in enumerate(rows):
        out = jnp.where(index == place, row, out)
    return out


def stage_source(points, scale, xaug, at):
    feat, count = points.shape
    wide = points.astype(jnp.float32)
    shift = scale * jnp.sum(wide * wide, axis=0, keepdims=True)
    shift = shift.astype(jnp.bfloat16).astype(jnp.float32)
    xaug[0:feat, at] = pick_rows((feat, count), [1.0, 1.0, 1.0, -shift]).astype(jnp.bfloat16)
    for place, term in enumerate(three_terms(2.0 * scale * wide)):
        xaug[(place + 1) * feat : (place + 2) * feat, at] = term


def stage_sources(parts, scale, xaug, begin=0):
    for part in parts:
        count = part.shape[2]
        for block in range(part.shape[0]):
            stage_source(part[block], scale, xaug, slice(begin, begin + count))
            begin += count


def target_lines(part, block, scale, feat):
    wide = part[block, :feat, :].astype(jnp.float32)
    logw = part[block, feat : feat + 16, :].astype(jnp.float32)[0:1]
    return scale * jnp.sum(wide * wide, axis=0, keepdims=True), logw * LOG2E


def stage_targets(parts, scale, taug, begin, feat):
    for part in parts:
        for block in range(part.shape[0]):
            q, logw = target_lines(part, block, scale, feat)
            terms = [term.astype(jnp.float32) for term in three_terms(logw - q)]
            extras = pick_rows((feat, LANES), terms + [1.0])
            wide = part[block, :feat, :].astype(jnp.float32)
            turned = jnp.concatenate([extras, wide], axis=0).T
            lane = lax.broadcasted_iota(jnp.int32, turned.shape, 1)
            twice = jnp.where(lane < feat, pltpu.roll(turned, feat, 1), turned)
            taug[begin : begin + LANES, 0:LANES] = turned.astype(jnp.bfloat16)
            taug[begin : begin + LANES, LANES:DEPTH] = twice.astype(jnp.bfloat16)
            begin += LANES


def renew_targets(lines, flips, parts, g, q, logw, taug):
    total = lines[0].shape[1]
    size = total // (2 * parts)
    held = []
    for line, (core, digit) in zip(lines, flips):
        value = line[...]
        places = [(block ^ (core * parts)) ^ digit for block in range(2 * parts)]
        pieces = [value[:, place * size : (place + 1) * size] for place in places]
        held.append(jnp.concatenate(pieces, axis=1))
    peak = functools.reduce(jnp.maximum, held)
    added = functools.reduce(jnp.add, [jnp.exp2(value - peak) for value in held])
    potential = g - (peak + jnp.log2(added))
    g = potential + logw
    terms = [term.astype(jnp.float32) for term in three_terms(g - jnp.max(g) - q)]
    for begin in range(0, total, LANES):
        rows = slice(begin, begin + LANES)
        extras = pick_rows((8, LANES), [term[:, rows] for term in terms] + [1.0])
        taug[rows, 0:8] = extras.T.astype(jnp.bfloat16)
    return potential, g


def exponents(left, right):
    return jnp.dot(left, right, preferred_element_type=jnp.float32)


def spread_rows(taug, right, p_ref, beside):
    total, width = taug.shape[0], right.shape[1]
    reach = min(total, 512)
    sums = jnp.zeros((8, width), jnp.float32)
    for begin in range(0, total, reach):
        e = exponents(taug[begin : begin + reach, :], right)
        for inner in range(0, reach, LANES):
            rows = slice(begin + inner, begin + inner + LANES)
            beside(rows)
            p = jnp.exp2(e[inner : inner + LANES])
            p_ref[rows, :] = p
            sums = sums + jnp.sum(p.reshape(LANES // 8, 8, width), axis=0)
    return jnp.sum(sums, axis=0, keepdims=True)


def add_columns(p_ref, weight, col_refs, rows):
    width = weight.shape[1]
    added = p_ref[rows, 0:LANES] * weight[:, 0:LANES]
    for lane in range(LANES, width, LANES):
        added = added + p_ref[rows, lane : lane + LANES] * weight[:, lane : lane + LANES]
    col_ref, at = column_block(col_refs, rows)
    col_ref[at, :] += added


def column_block(col_refs, rows):
    size = col_refs[0].shape[0]
    place = rows.start // size
    return col_refs[place], slice(rows.start - place * size, rows.stop - place * size)


def tile_columns(tile, width):
    if isinstance(tile, int):
        return pl.ds(tile * width, width)
    return pl.ds(pl.multiple_of(tile * width, width), width)


def add_sources(xaug, logws, taug, p_refs, col_refs):
    total = taug.shape[0]
    width = p_refs[0].shape[1]
    tiles = xaug.shape[1] // width
    if p_refs[1].shape != p_refs[0].shape:
        p_refs = (p_refs[0], p_refs[0])

    def step(tile, slot, held):
        def beside(rows):
            if held is not None:
                add_columns(p_refs[1 - slot], held, col_refs, rows)

        at = tile_columns(tile, width)
        s = spread_rows(taug, xaug[:, at], p_refs[slot], beside)
        return s, jnp.exp2(logws[:, at] * LOG2E) / s

    def two_steps(pair, carry):
        least, weight = carry
        s1, weight1 = step(2 * pair + 1, 1, weight)
        s0, weight0 = step(2 * pair + 2, 0, weight1)
        return jnp.minimum(least, jnp.minimum(s0, s1)), weight0

    s, weight = step(0, 0, None)
    least, weight = lax.fori_loop(0, tiles // 2 - 1, two_steps, (s, weight))
    s, weight = step(tiles - 1, 1, weight)
    for begin in range(0, total, LANES):
        add_columns(p_refs[1], weight, col_refs, slice(begin, begin + LANES))
    return jnp.minimum(least, s)


def lane_totals(col_refs, out_ref):
    total = sum(col_ref.shape[0] for col_ref in col_refs)
    reach = min(total, 2048)
    ones = jnp.ones((16, 2 * LANES), jnp.bfloat16)
    sizes = col_refs[0].shape[0]
    for begin in range(0, total, reach):
        refs = col_refs[begin // sizes : (begin + reach) // sizes]
        high, middle, _ = three_terms(jnp.concatenate([col_ref[...] for col_ref in refs], axis=0))
        both = jnp.concatenate([high, middle], axis=1)
        added = lax.dot_general(
            ones, both, (((1,), (1,)), ((), ())), preferred_element_type=jnp.float32
        )
        out_ref[:, begin : begin + reach] = added[0:1]


def finish_sums(xaug, logws, taug, least, p_ref, col_refs, out_ref):
    total = taug.shape[0]
    lane_totals(col_refs, out_ref)
    cols = out_ref[...]
    out_ref[...] = jnp.log2(cols)
    fine = jnp.logical_and(
        jnp.min(least) >= SMALL_ROW,
        jnp.logical_and(jnp.min(cols) >= SMALL_COL, jnp.max(cols) <= LARGE_COL),
    )
    top_ref = p_ref.at[:, 0:LANES]

    @pl.when(jnp.logical_not(fine))
    def _():
        for col_ref in col_refs:
            col_ref[...] = jnp.zeros_like(col_ref)
        top_ref[...] = jnp.full_like(top_ref, FLOOR)

        def careful(tile, carry):
            at = tile_columns(tile, LANES)
            right = xaug[:, at]

            def block_rows(block):
                return pl.ds(pl.multiple_of(block * LANES, LANES), LANES)

            def highest(block, peak):
                e = exponents(taug[block_rows(block), :], right)
                return jnp.maximum(peak, jnp.max(e, axis=0, keepdims=True))

            peak = jnp.full((1, LANES), FLOOR, jnp.float32)
            peak = lax.fori_loop(0, total // LANES, highest, peak)

            def summed(block, s):
                e = exponents(taug[block_rows(block), :], right)
                return s + jnp.sum(jnp.exp2(e - peak), axis=0, keepdims=True)

            s = lax.fori_loop(0, total // LANES, summed, jnp.zeros((1, LANES), jnp.float32))
            shift = logws[:, at] * LOG2E - peak - jnp.log2(s)

            size = col_refs[0].shape[0]
            for place, col_ref in enumerate(col_refs):

                def collected(block, carry, place=place, col_ref=col_ref):
                    rows = block_rows(place * (size // LANES) + block)
                    term = exponents(taug[rows, :], right) + shift
                    old = top_ref[rows, :]
                    top = jnp.maximum(old, term)
                    here = block_rows(block)
                    col = col_ref[here, :] * jnp.exp2(old - top) + jnp.exp2(term - top)
                    col_ref[here, :] = col
                    top_ref[rows, :] = top
                    return carry

                lax.fori_loop(0, size // LANES, collected, 0)
            return carry

        lax.fori_loop(0, xaug.shape[1] // LANES, careful, 0)
        for begin in range(0, total, LANES):
            rows = slice(begin, begin + LANES)
            col_ref, at = column_block(col_refs, rows)
            tops = top_ref[rows, :].T
            top = jnp.max(tops, axis=0, keepdims=True)
            added = jnp.sum(col_ref[at, :].T * jnp.exp2(tops - top), axis=0, keepdims=True)
            out_ref[:, rows] = top + jnp.log2(added)


def part_kernel(feat, inverse, *refs):
    stage_targets(refs[:-1], inverse[0] * LOG2E, refs[-1], 0, feat)


def near_kernel(parts, feat, inverse, logws, xs, mine, rest, theirs, *refs):
    ts, refs = refs[: 2 * parts], refs[2 * parts :]
    xaug, taug, out_ref, g_ref, q_ref, p0, p1, *col_refs = refs
    scale = inverse[0] * LOG2E
    stage_sources([xs], scale, xaug)
    place = 0
    for part in ts:
        for block in range(part.shape[0]):
            at = slice(place * LANES, (place + 1) * LANES)
            q_ref[:, at], g_ref[:, at] = target_lines(part, block, scale, feat)
            place += 1
    begin = 0
    for part in (mine, rest, theirs):
        taug[begin : begin + part.shape[0], :] = part[...]
        begin += part.shape[0]
    stage_targets(ts[parts + 1 :], scale, taug, begin, feat)
    for col_ref in col_refs:
        col_ref[...] = jnp.zeros_like(col_ref)
    least = add_sources(xaug, logws, taug, (p0, p1), col_refs)
    finish_sums(xaug, logws, taug, least, p0, col_refs, out_ref)


def next_kernel(flips, parts, logws, xaug, old, g, q, logw, *refs):
    lines, refs = refs[: len(flips)], refs[len(flips) :]
    out_ref, g_ref, taug, p0, p1, *col_refs = refs
    taug[...] = old[...]
    g_ref[...] = renew_targets(lines, flips, parts, g[...], q[...], logw[...], taug)[1]
    for col_ref in col_refs:
        col_ref[...] = jnp.zeros_like(col_ref)
    least = add_sources(xaug, logws, taug, (p0, p1), col_refs)
    finish_sums(xaug, logws, taug, least, p0, col_refs, out_ref)


def map_kernel(flips, parts, n_t, feat, xaug, old, g, q, logw, *refs):
    lines, refs = refs[: len(flips)], refs[len(flips) :]
    ts = refs[:n_t]
    mapped_ref, pot_ref, taug, p_ref, plan_ref, coords = refs[n_t:]
    taug[...] = old[...]
    potential = renew_targets(lines, flips, parts, g[...], q[...], logw[...], taug)[0]
    pot_ref[...] = potential[:, :LANES] * (1.0 / LOG2E)
    place = 0
    for part in ts:
        for block in range(part.shape[0]):
            coords[:, place * LANES : (place + 1) * LANES] = part[block, :feat, :]
            place += 1
    total = taug.shape[0]
    right = xaug[:, : p_ref.shape[1]]
    s = spread_rows(taug, right, p_ref, lambda rows: None)
    weight = 1.0 / s
    for begin in range(0, total, LANES):
        rows = slice(begin, begin + LANES)
        plan_ref[rows, :] = (p_ref[rows, :] * weight).astype(jnp.bfloat16)

    @pl.when(jnp.logical_not(jnp.min(s) >= SMALL_ROW))
    def _():
        reach = min(total, 2048)
        peak = jnp.full(s.shape, FLOOR, jnp.float32)
        for begin in range(0, total, reach):
            rows = slice(begin, begin + reach)
            p_ref[rows, :] = exponents(taug[rows, :], right)
            peak = jnp.maximum(peak, jnp.max(p_ref[rows, :], axis=0, keepdims=True))
        sums = jnp.zeros(s.shape, jnp.float32)
        for begin in range(0, total, reach):
            rows = slice(begin, begin + reach)
            sums += jnp.sum(jnp.exp2(p_ref[rows, :] - peak), axis=0, keepdims=True)
        shift = peak + jnp.log2(sums)
        for begin in range(0, total, reach):
            rows = slice(begin, begin + reach)
            plan_ref[rows, :] = jnp.exp2(p_ref[rows, :] - shift).astype(jnp.bfloat16)

    mapped_ref[...] = jnp.dot(coords[...], plan_ref[...], preferred_element_type=jnp.float32)


def swap(value, count, step):
    return lax.ppermute(value, AXIS, [(source, source ^ step) for source in range(count)])


def chip_stages(count):
    high, stages = count.bit_length() - 1, []
    while high > 1:
        width = min(2, high - 1)
        stages.append((high - width, width))
        high -= width
    return stages


def gather_stage(parts, count, low, width):
    held = parts[0] if len(parts) == 1 else jnp.concatenate(parts, axis=0)
    return [held] + [swap(held, count, digit << low) for digit in range(1, 1 << width)]


def gather_chips(block, count):
    parts = [block[None]]
    for low, width in chip_stages(count):
        parts = gather_stage(parts, count, low, width)
    return parts


def gather_line(block, count):
    parts = [block[None]]
    for low, width in chip_stages(count)[:-1]:
        parts = gather_stage(parts, count, low, width)
    return jnp.concatenate(parts, axis=0)


def on_device(source_points, target_points, source_logw, target_logw, inverse_eps, count):
    feat, own_sources = source_points.shape
    own_targets = target_points.shape[1]
    extra_rows = own_sources // LANES
    pad = -(1 + extra_rows) % 16
    packed = jnp.concatenate(
        [
            target_points,
            target_logw[None, :],
            source_logw.reshape(extra_rows, LANES),
            jnp.zeros((pad, own_targets), target_points.dtype),
        ],
        axis=0,
    )
    f32, bf16 = jnp.float32, jnp.bfloat16
    total = count * own_targets
    small = total <= 4096
    width = 2 * LANES if small else LANES
    vmem = pl.BlockSpec(memory_space=pltpu.VMEM)
    smem = pl.BlockSpec(memory_space=pltpu.SMEM)
    params = pltpu.CompilerParams(vmem_limit_bytes=(24 if small else 63) << 20)
    line = jax.ShapeDtypeStruct((1, total), f32)

    def call(kernel, operands, outs, scratch=(), scalars=1):
        return pl.pallas_call(
            kernel,
            out_shape=outs,
            in_specs=[smem] * scalars + [vmem] * (len(operands) - scalars),
            out_specs=[vmem] * len(outs),
            scratch_shapes=list(scratch),
            compiler_params=params,
        )(*operands)

    def staged_shape(parts):
        rows = sum(part.shape[0] for part in parts) * own_targets
        return jax.ShapeDtypeStruct((rows, DEPTH), bf16)

    def logw_line(parts):
        rows = [part[:, feat + 1 : feat + 1 + extra_rows] for part in parts]
        return jnp.concatenate(rows, axis=0).reshape(1, -1).astype(f32)

    packed, points = lax.optimization_barrier((packed, source_points))
    mine = gather_chips(packed, count)
    theirs = [swap(part, count, 1) for part in mine]
    parts, low = len(mine), chip_stages(count)[-1][0]
    ts = mine + theirs
    (taug_mine,) = call(
        functools.partial(part_kernel, feat),
        [inverse_eps, mine[0]],
        [staged_shape(mine[:1])],
    )
    (taug_theirs,) = call(
        functools.partial(part_kernel, feat),
        [inverse_eps, theirs[0]],
        [staged_shape(theirs[:1])],
    )
    (taug_rest,) = call(
        functools.partial(part_kernel, feat),
        [inverse_eps] + mine[1:],
        [staged_shape(mine[1:])],
    )
    xs = gather_line(points, count)
    logws = logw_line(mine[:1])
    rows = logws.shape[1]

    p_scratch = pltpu.VMEM((total, width), f32)
    scratch = [
        p_scratch,
        p_scratch if small else pltpu.VMEM((8, LANES), f32),
    ] + [pltpu.VMEM((total // 16, LANES), f32)] * 16
    xaug, taug, sums, logw, q = call(
        functools.partial(near_kernel, parts, feat),
        [inverse_eps, logws, xs, taug_mine, taug_rest, taug_theirs] + ts,
        [
            jax.ShapeDtypeStruct((DEPTH, rows), bf16),
            jax.ShapeDtypeStruct((total, DEPTH), bf16),
            line,
            line,
            line,
        ],
        scratch,
    )
    flips = [(core, digit) for digit in range(parts) for core in range(2)]

    def exchange(own):
        return [own] + [swap(own, count, core | (digit << low)) for core, digit in flips[1:]]

    g = logw
    for _ in range(ITERS - 1):
        sums, g = call(
            functools.partial(next_kernel, flips, parts),
            [logws, xaug, taug, g, q, logw] + exchange(sums),
            [line, line],
            [pltpu.VMEM((total, DEPTH), bf16)] + scratch,
            scalars=0,
        )
    mapped, potential = call(
        functools.partial(map_kernel, flips, parts, len(ts), feat),
        [xaug if small else xaug[:, :own_sources], taug, g, q, logw] + exchange(sums) + ts,
        [
            jax.ShapeDtypeStruct((feat, own_sources), f32),
            jax.ShapeDtypeStruct((1, own_targets), f32),
        ],
        [
            pltpu.VMEM((total, DEPTH), bf16),
            pltpu.VMEM((total, own_sources), f32),
            pltpu.VMEM((total, own_sources), bf16),
            pltpu.VMEM((feat, total), bf16),
        ],
        scalars=0,
    )
    return (mapped, potential.reshape(own_targets))


def solution(mesh):
    count = mesh.shape[AXIS]
    placed = (
        P(None, ("grp", "wide")),
        P(None, ("grp", "wide")),
        P(("grp", "wide")),
        P(("grp", "wide")),
        P(),
    )

    def body(*blocks):
        return on_device(*blocks, count)

    return jax.shard_map(
        body,
        mesh=mesh,
        in_specs=placed,
        out_specs=(P(None, ("grp", "wide")), P(("grp", "wide"))),
        check_vma=False,
    )
```

```python
import functools
import math

import jax
import jax.numpy as jnp
from jax import lax
from jax.experimental import pallas as pl
from jax.experimental.pallas import tpu as pltpu
from jax.sharding import PartitionSpec as P

ITERS = 2
AXIS = "wide"
LOG2E = math.log2(math.e)
LANES = 128
DEPTH = 256
SMALL_ROW = 2.0**-64
SMALL_COL = 2.0**-32
LARGE_COL = 2.0**100
FLOOR = -1e30


def three_terms(value):
    high = value.astype(jnp.bfloat16)
    rest = value - high.astype(jnp.float32)
    middle = rest.astype(jnp.bfloat16)
    low = (rest - middle.astype(jnp.float32)).astype(jnp.bfloat16)
    return high, middle, low


def pick_rows(shape, rows):
    index = lax.broadcasted_iota(jnp.int32, shape, 0)
    out = jnp.zeros(shape, jnp.float32)
    for place, row in enumerate(rows):
        out = jnp.where(index == place, row, out)
    return out


def stage_source(points, scale, xaug, at):
    feat, count = points.shape
    wide = points.astype(jnp.float32)
    shift = scale * jnp.sum(wide * wide, axis=0, keepdims=True)
    shift = shift.astype(jnp.bfloat16).astype(jnp.float32)
    xaug[0:feat, at] = pick_rows((feat, count), [1.0, 1.0, 1.0, -shift]).astype(jnp.bfloat16)
    for place, term in enumerate(three_terms(2.0 * scale * wide)):
        xaug[(place + 1) * feat : (place + 2) * feat, at] = term


def stage_sources(parts, scale, xaug, begin=0):
    for part in parts:
        count = part.shape[2]
        for block in range(part.shape[0]):
            stage_source(part[block], scale, xaug, slice(begin, begin + count))
            begin += count


def target_lines(part, block, scale, feat):
    wide = part[block, :feat, :].astype(jnp.float32)
    logw = part[block, feat : feat + 16, :].astype(jnp.float32)[0:1]
    return scale * jnp.sum(wide * wide, axis=0, keepdims=True), logw * LOG2E


def stage_targets(parts, scale, taug, begin, feat):
    for part in parts:
        for block in range(part.shape[0]):
            q, logw = target_lines(part, block, scale, feat)
            terms = [term.astype(jnp.float32) for term in three_terms(logw - q)]
            extras = pick_rows((feat, LANES), terms + [1.0])
            wide = part[block, :feat, :].astype(jnp.float32)
            turned = jnp.concatenate([extras, wide], axis=0).T
            lane = lax.broadcasted_iota(jnp.int32, turned.shape, 1)
            twice = jnp.where(lane < feat, pltpu.roll(turned, feat, 1), turned)
            taug[begin : begin + LANES, 0:LANES] = turned.astype(jnp.bfloat16)
            taug[begin : begin + LANES, LANES:DEPTH] = twice.astype(jnp.bfloat16)
            begin += LANES


def renew_targets(lines, flips, parts, g, q, logw, taug):
    total = lines[0].shape[1]
    size = total // (2 * parts)
    held = []
    for line, (core, digit) in zip(lines, flips):
        value = line[...]
        places = [(block ^ (core * parts)) ^ digit for block in range(2 * parts)]
        pieces = [value[:, place * size : (place + 1) * size] for place in places]
        held.append(jnp.concatenate(pieces, axis=1))
    peak = functools.reduce(jnp.maximum, held)
    added = functools.reduce(jnp.add, [jnp.exp2(value - peak) for value in held])
    potential = g - (peak + jnp.log2(added))
    g = potential + logw
    terms = [term.astype(jnp.float32) for term in three_terms(g - jnp.max(g) - q)]
    for begin in range(0, total, LANES):
        rows = slice(begin, begin + LANES)
        extras = pick_rows((8, LANES), [term[:, rows] for term in terms] + [1.0])
        taug[rows, 0:8] = extras.T.astype(jnp.bfloat16)
    return potential, g


def exponents(left, right):
    return jnp.dot(left, right, preferred_element_type=jnp.float32)


def spread_rows(taug, right, p_ref, beside):
    total, width = taug.shape[0], right.shape[1]
    reach = min(total, 512)
    sums = jnp.zeros((8, width), jnp.float32)
    for begin in range(0, total, reach):
        e = exponents(taug[begin : begin + reach, :], right)
        for inner in range(0, reach, LANES):
            rows = slice(begin + inner, begin + inner + LANES)
            beside(rows)
            p = jnp.exp2(e[inner : inner + LANES])
            p_ref[rows, :] = p
            sums = sums + jnp.sum(p.reshape(LANES // 8, 8, width), axis=0)
    return jnp.sum(sums, axis=0, keepdims=True)


def add_columns(p_ref, weight, col_refs, rows):
    width = weight.shape[1]
    added = p_ref[rows, 0:LANES] * weight[:, 0:LANES]
    for lane in range(LANES, width, LANES):
        added = added + p_ref[rows, lane : lane + LANES] * weight[:, lane : lane + LANES]
    col_ref, at = column_block(col_refs, rows)
    col_ref[at, :] += added


def column_block(col_refs, rows):
    size = col_refs[0].shape[0]
    place = rows.start // size
    return col_refs[place], slice(rows.start - place * size, rows.stop - place * size)


def tile_columns(tile, width):
    if isinstance(tile, int):
        return pl.ds(tile * width, width)
    return pl.ds(pl.multiple_of(tile * width, width), width)


def add_sources(xaug, logws, taug, p_refs, col_refs):
    total = taug.shape[0]
    width = p_refs[0].shape[1]
    tiles = xaug.shape[1] // width
    if p_refs[1].shape != p_refs[0].shape:
        p_refs = (p_refs[0], p_refs[0])

    def step(tile, slot, held):
        def beside(rows):
            if held is not None:
                add_columns(p_refs[1 - slot], held, col_refs, rows)

        at = tile_columns(tile, width)
        s = spread_rows(taug, xaug[:, at], p_refs[slot], beside)
        return s, jnp.exp2(logws[:, at] * LOG2E) / s

    def two_steps(pair, carry):
        least, weight = carry
        s1, weight1 = step(2 * pair + 1, 1, weight)
        s0, weight0 = step(2 * pair + 2, 0, weight1)
        return jnp.minimum(least, jnp.minimum(s0, s1)), weight0

    s, weight = step(0, 0, None)
    least, weight = lax.fori_loop(0, tiles // 2 - 1, two_steps, (s, weight))
    s, weight = step(tiles - 1, 1, weight)
    for begin in range(0, total, LANES):
        add_columns(p_refs[1], weight, col_refs, slice(begin, begin + LANES))
    return jnp.minimum(least, s)


def lane_tiles(width):
    return [slice(begin, begin + LANES) for begin in range(0, width, LANES)]


def lane_totals(col_refs, out_ref):
    total = sum(col_ref.shape[0] for col_ref in col_refs)
    reach = min(total, 2048)
    ones = jnp.ones((16, 2 * LANES), jnp.bfloat16)
    sizes = col_refs[0].shape[0]
    for begin in range(0, total, reach):
        refs = col_refs[begin // sizes : (begin + reach) // sizes]
        high, middle, _ = three_terms(jnp.concatenate([col_ref[...] for col_ref in refs], axis=0))
        both = jnp.concatenate([high, middle], axis=1)
        added = lax.dot_general(
            ones, both, (((1,), (1,)), ((), ())), preferred_element_type=jnp.float32
        )
        out_ref[:, begin : begin + reach] = added[0:1]


def finish_sums(xaug, logws, taug, least, p0, p1, col_refs, out_ref):
    total = taug.shape[0]
    lane_totals(col_refs, out_ref)
    cols = out_ref[...]
    out_ref[...] = jnp.log2(cols)
    margins = [least[:, at] / SMALL_ROW for at in lane_tiles(least.shape[1])]
    for at in lane_tiles(total):
        margins += [cols[:, at] / SMALL_COL, LARGE_COL / cols[:, at]]
    fine = jnp.min(functools.reduce(jnp.minimum, margins)) >= 1.0
    halves = total // p0.shape[0]
    tops_refs = [p_ref.at[:, 0:LANES] for p_ref in (p0, p1)[:halves]]

    @pl.when(jnp.logical_not(fine))
    def _():
        for col_ref in col_refs:
            col_ref[...] = jnp.zeros_like(col_ref)
        for top_ref in tops_refs:
            top_ref[...] = jnp.full(top_ref.shape, FLOOR, jnp.float32)

        def careful(tile, carry):
            at = tile_columns(tile, LANES)
            right = xaug[:, at]

            def block_rows(block):
                return pl.ds(pl.multiple_of(block * LANES, LANES), LANES)

            def highest(block, peak):
                e = exponents(taug[block_rows(block), :], right)
                return jnp.maximum(peak, jnp.max(e, axis=0, keepdims=True))

            peak = jnp.full((1, LANES), FLOOR, jnp.float32)
            peak = lax.fori_loop(0, total // LANES, highest, peak)

            def summed(block, s):
                e = exponents(taug[block_rows(block), :], right)
                return s + jnp.sum(jnp.exp2(e - peak), axis=0, keepdims=True)

            s = lax.fori_loop(0, total // LANES, summed, jnp.zeros((1, LANES), jnp.float32))
            shift = logws[:, at] * LOG2E - peak - jnp.log2(s)

            size = col_refs[0].shape[0]
            for place, col_ref in enumerate(col_refs):
                top_ref = tops_refs[place * size // tops_refs[0].shape[0]]
                skipped = place * size % tops_refs[0].shape[0] // LANES

                def collected(
                    block, carry, place=place, col_ref=col_ref, top_ref=top_ref, skipped=skipped
                ):
                    rows = block_rows(place * (size // LANES) + block)
                    term = exponents(taug[rows, :], right) + shift
                    rows = block_rows(skipped + block)
                    old = top_ref[rows, :]
                    top = jnp.maximum(old, term)
                    here = block_rows(block)
                    col = col_ref[here, :] * jnp.exp2(old - top) + jnp.exp2(term - top)
                    col_ref[here, :] = col
                    top_ref[rows, :] = top
                    return carry

                lax.fori_loop(0, size // LANES, collected, 0)
            return carry

        lax.fori_loop(0, xaug.shape[1] // LANES, careful, 0)
        for begin in range(0, total, LANES):
            rows = slice(begin, begin + LANES)
            col_ref, at = column_block(col_refs, rows)
            top_ref, here = column_block(tops_refs, rows)
            tops = top_ref[here, :].T
            top = jnp.max(tops, axis=0, keepdims=True)
            added = jnp.sum(col_ref[at, :].T * jnp.exp2(tops - top), axis=0, keepdims=True)
            out_ref[:, rows] = top + jnp.log2(added)


def part_kernel(feat, inverse, *refs):
    stage_targets(refs[:-1], inverse[0] * LOG2E, refs[-1], 0, feat)


def near_kernel(parts, feat, inverse, logws, xs, mine, rest, theirs, *refs):
    ts, refs = refs[: 2 * parts], refs[2 * parts :]
    xaug, taug, out_ref, g_ref, q_ref, p0, p1, *col_refs = refs
    scale = inverse[0] * LOG2E
    stage_sources([xs], scale, xaug)
    place = 0
    for part in ts:
        for block in range(part.shape[0]):
            at = slice(place * LANES, (place + 1) * LANES)
            q_ref[:, at], g_ref[:, at] = target_lines(part, block, scale, feat)
            place += 1
    begin = 0
    for part in (mine, rest, theirs):
        taug[begin : begin + part.shape[0], :] = part[...]
        begin += part.shape[0]
    stage_targets(ts[parts + 1 :], scale, taug, begin, feat)
    for col_ref in col_refs:
        col_ref[...] = jnp.zeros_like(col_ref)
    least = add_sources(xaug, logws, taug, (p0, p1), col_refs)
    finish_sums(xaug, logws, taug, least, p0, p1, col_refs, out_ref)


def head_kernel(inverse, xs, *refs):
    ts, (xaug, p_ref, s_ref) = refs[:-3], refs[-3:]
    stage_sources([xs], inverse[0] * LOG2E, xaug)
    width = 2 * LANES
    tiles = xaug.shape[1] // width
    side = 3 if tiles % 3 == 0 else 1

    def advance(step, carry):
        for inner in range(side):
            at = tile_columns(step * side + inner, width)
            right, begin, s = xaug[:, at], 0, 0.0
            for part in ts:
                rows = pl.ds(begin, part.shape[0])
                s = s + spread_rows(part, right, p_ref.at[rows, at], lambda rows: None)
                begin += part.shape[0]
            s_ref[:, at] = s
        return carry

    lax.fori_loop(0, tiles // side, advance, 0)


def add_split_sources(xaug, logws, taug, ranges, p_head, s_head, p_refs, col_refs):
    width = p_refs[0].shape[1]
    tiles = xaug.shape[1] // width
    total = taug.shape[0]
    late = [row for begin, end in ranges for row in range(begin, end, LANES)]
    early = [row for row in range(0, total, LANES) if row not in late]
    share = -(-len(early) // len(late))

    def collect(row, value_of, weight):
        added = functools.reduce(
            jnp.add, [value_of(at) * weight[:, at] for at in lane_tiles(width)]
        )
        col_ref, at = column_block(col_refs, slice(row, row + LANES))
        col_ref[at, :] += added

    def head_values(tile, row):
        place = early.index(row) * LANES

        def value_of(at):
            begin = tile * width + at.start
            if not isinstance(tile, int):
                begin = pl.multiple_of(begin, LANES)
            return p_head[place : place + LANES, pl.ds(begin, LANES)]

        return value_of

    def late_values(p_ref, row):
        place = late.index(row) * LANES
        return lambda at: p_ref[place : place + LANES, at]

    def step(tile, slot, held):
        at = tile_columns(tile, width)
        right = xaug[:, at]
        sums = jnp.zeros((8, width), jnp.float32)
        for begin, end in ranges:
            for first in range(begin, end, 512):
                last = min(first + 512, end)
                e = exponents(taug[first:last, :], right)
                for row in range(first, last, LANES):
                    place = late.index(row)
                    if held is not None:
                        for other in early[place * share : (place + 1) * share]:
                            collect(other, head_values(tile - 1, other), held)
                        collect(row, late_values(p_refs[1 - slot], row), held)
                    p = jnp.exp2(e[row - first : row - first + LANES])
                    p_refs[slot][place * LANES : (place + 1) * LANES, :] = p
                    sums = sums + jnp.sum(p.reshape(LANES // 8, 8, width), axis=0)
        s = s_head[:, at] + jnp.sum(sums, axis=0, keepdims=True)
        return s, jnp.exp2(logws[:, at] * LOG2E) / s

    def two_steps(pair, carry):
        least, weight = carry
        s1, weight1 = step(2 * pair + 1, 1, weight)
        s0, weight0 = step(2 * pair + 2, 0, weight1)
        return jnp.minimum(least, jnp.minimum(s0, s1)), weight0

    s, weight = step(0, 0, None)
    least, weight = lax.fori_loop(0, tiles // 2 - 1, two_steps, (s, weight))
    s, weight = step(tiles - 1, 1, weight)
    for row in range(0, total, LANES):
        if row in late:
            collect(row, late_values(p_refs[1], row), weight)
        else:
            collect(row, head_values(tiles - 1, row), weight)
    return jnp.minimum(least, s)


def tail_kernel(parts, feat, inverse, logws, xaug, p_head, s_head, mine, rest, theirs, *refs):
    ts, refs = refs[: 2 * parts], refs[2 * parts :]
    taug, out_ref, g_ref, q_ref, p0, p1, *col_refs = refs
    scale = inverse[0] * LOG2E
    place = 0
    for part in ts:
        for block in range(part.shape[0]):
            at = slice(place * LANES, (place + 1) * LANES)
            q_ref[:, at], g_ref[:, at] = target_lines(part, block, scale, feat)
            place += 1
    begin, ranges = 0, []
    for part in (mine, rest, theirs):
        end = begin + part.shape[0]
        taug[begin:end, :] = part[...]
        if part is rest:
            ranges.append((begin, end))
        begin = end
    stage_targets(ts[parts + 1 :], scale, taug, begin, feat)
    ranges.append((begin, taug.shape[0]))
    for col_ref in col_refs:
        col_ref[...] = jnp.zeros_like(col_ref)
    least = add_split_sources(xaug, logws, taug, ranges, p_head, s_head, (p0, p1), col_refs)
    finish_sums(xaug, logws, taug, least, p0, p1, col_refs, out_ref)


def next_kernel(flips, parts, logws, xaug, old, g, q, logw, *refs):
    lines, refs = refs[: len(flips)], refs[len(flips) :]
    out_ref, g_ref, taug, p0, p1, *col_refs = refs
    taug[...] = old[...]
    g_ref[...] = renew_targets(lines, flips, parts, g[...], q[...], logw[...], taug)[1]
    for col_ref in col_refs:
        col_ref[...] = jnp.zeros_like(col_ref)
    least = add_sources(xaug, logws, taug, (p0, p1), col_refs)
    finish_sums(xaug, logws, taug, least, p0, p1, col_refs, out_ref)


def map_kernel(flips, parts, n_t, feat, xaug, old, g, q, logw, *refs):
    lines, refs = refs[: len(flips)], refs[len(flips) :]
    ts = refs[:n_t]
    mapped_ref, pot_ref, taug, p_ref, plan_ref, coords = refs[n_t:]
    taug[...] = old[...]
    potential = renew_targets(lines, flips, parts, g[...], q[...], logw[...], taug)[0]
    pot_ref[...] = potential[:, :LANES] * (1.0 / LOG2E)
    place = 0
    for part in ts:
        for block in range(part.shape[0]):
            coords[:, place * LANES : (place + 1) * LANES] = part[block, :feat, :]
            place += 1
    total = taug.shape[0]
    right = xaug[:, : p_ref.shape[1]]
    s = spread_rows(taug, right, p_ref, lambda rows: None)
    weight = 1.0 / s
    for begin in range(0, total, LANES):
        rows = slice(begin, begin + LANES)
        plan_ref[rows, :] = (p_ref[rows, :] * weight).astype(jnp.bfloat16)

    @pl.when(jnp.logical_not(jnp.min(s) >= SMALL_ROW))
    def _():
        reach = min(total, 2048)
        peak = jnp.full(s.shape, FLOOR, jnp.float32)
        for begin in range(0, total, reach):
            rows = slice(begin, begin + reach)
            p_ref[rows, :] = exponents(taug[rows, :], right)
            peak = jnp.maximum(peak, jnp.max(p_ref[rows, :], axis=0, keepdims=True))
        sums = jnp.zeros(s.shape, jnp.float32)
        for begin in range(0, total, reach):
            rows = slice(begin, begin + reach)
            sums += jnp.sum(jnp.exp2(p_ref[rows, :] - peak), axis=0, keepdims=True)
        shift = peak + jnp.log2(sums)
        for begin in range(0, total, reach):
            rows = slice(begin, begin + reach)
            plan_ref[rows, :] = jnp.exp2(p_ref[rows, :] - shift).astype(jnp.bfloat16)

    mapped_ref[...] = jnp.dot(coords[...], plan_ref[...], preferred_element_type=jnp.float32)


def swap(value, count, step):
    return lax.ppermute(value, AXIS, [(source, source ^ step) for source in range(count)])


def chip_stages(count):
    high, stages = count.bit_length() - 1, []
    while high > 1:
        width = min(2, high - 1)
        stages.append((high - width, width))
        high -= width
    return stages


def gather_stage(parts, count, low, width):
    held = parts[0] if len(parts) == 1 else jnp.concatenate(parts, axis=0)
    return [held] + [swap(held, count, digit << low) for digit in range(1, 1 << width)]


def gather_chips(block, count):
    parts = [block[None]]
    for low, width in chip_stages(count):
        parts = gather_stage(parts, count, low, width)
    return parts


def gather_line(block, count):
    parts = [block[None]]
    for low, width in chip_stages(count)[:-1]:
        parts = gather_stage(parts, count, low, width)
    return jnp.concatenate(parts, axis=0)


def on_device(source_points, target_points, source_logw, target_logw, inverse_eps, count):
    feat, own_sources = source_points.shape
    own_targets = target_points.shape[1]
    extra_rows = own_sources // LANES
    pad = -(1 + extra_rows) % 16
    packed = jnp.concatenate(
        [
            target_points,
            target_logw[None, :],
            source_logw.reshape(extra_rows, LANES),
            jnp.zeros((pad, own_targets), target_points.dtype),
        ],
        axis=0,
    )
    f32, bf16 = jnp.float32, jnp.bfloat16
    total = count * own_targets
    small = total <= 4096
    width = 2 * LANES if small else LANES
    vmem = pl.BlockSpec(memory_space=pltpu.VMEM)
    smem = pl.BlockSpec(memory_space=pltpu.SMEM)
    params = pltpu.CompilerParams(vmem_limit_bytes=(24 if small else 63) << 20)
    line = jax.ShapeDtypeStruct((1, total), f32)

    def call(kernel, operands, outs, scratch=(), scalars=1):
        return pl.pallas_call(
            kernel,
            out_shape=outs,
            in_specs=[smem] * scalars + [vmem] * (len(operands) - scalars),
            out_specs=[vmem] * len(outs),
            scratch_shapes=list(scratch),
            compiler_params=params,
        )(*operands)

    def staged_shape(parts):
        rows = sum(part.shape[0] for part in parts) * own_targets
        return jax.ShapeDtypeStruct((rows, DEPTH), bf16)

    def logw_line(parts):
        rows = [part[:, feat + 1 : feat + 1 + extra_rows] for part in parts]
        return jnp.concatenate(rows, axis=0).reshape(1, -1).astype(f32)

    packed, points = lax.optimization_barrier((packed, source_points))
    mine = gather_chips(packed, count)
    theirs = [swap(part, count, 1) for part in mine]
    parts, low = len(mine), chip_stages(count)[-1][0]
    ts = mine + theirs
    (taug_mine,) = call(
        functools.partial(part_kernel, feat),
        [inverse_eps, mine[0]],
        [staged_shape(mine[:1])],
    )
    (taug_theirs,) = call(
        functools.partial(part_kernel, feat),
        [inverse_eps, theirs[0]],
        [staged_shape(theirs[:1])],
    )
    (taug_rest,) = call(
        functools.partial(part_kernel, feat),
        [inverse_eps] + mine[1:],
        [staged_shape(mine[1:])],
    )
    xs = gather_line(points, count)
    logws = logw_line(mine[:1])
    rows = logws.shape[1]

    p_scratch = pltpu.VMEM((total, width), f32)
    scratch = [
        p_scratch,
        p_scratch if small else pltpu.VMEM((8, LANES), f32),
    ] + [pltpu.VMEM((total // 16, LANES), f32)] * 16
    shape = jax.ShapeDtypeStruct
    xaug_shape, taug_shape = shape((DEPTH, rows), bf16), shape((total, DEPTH), bf16)
    if small:
        head = (mine[0].shape[0] + theirs[0].shape[0]) * own_targets
        xaug, p_head, s_head = call(
            head_kernel,
            [inverse_eps, xs, taug_mine, taug_theirs],
            [xaug_shape, shape((head, rows), f32), shape((1, rows), f32)],
        )
        p_half = pltpu.VMEM((total - head, width), f32)
        taug, sums, logw, q = call(
            functools.partial(tail_kernel, parts, feat),
            [inverse_eps, logws, xaug, p_head, s_head, taug_mine, taug_rest, taug_theirs] + ts,
            [taug_shape, line, line, line],
            [p_half, p_half] + scratch[2:],
        )
    else:
        xaug, taug, sums, logw, q = call(
            functools.partial(near_kernel, parts, feat),
            [inverse_eps, logws, xs, taug_mine, taug_rest, taug_theirs] + ts,
            [xaug_shape, taug_shape, line, line, line],
            scratch,
        )
    flips = [(core, digit) for digit in range(parts) for core in range(2)]

    def exchange(own):
        return [own] + [swap(own, count, core | (digit << low)) for core, digit in flips[1:]]

    g = logw
    for _ in range(ITERS - 1):
        sums, g = call(
            functools.partial(next_kernel, flips, parts),
            [logws, xaug, taug, g, q, logw] + exchange(sums),
            [line, line],
            [pltpu.VMEM((total, DEPTH), bf16)] + scratch,
            scalars=0,
        )
    mapped, potential = call(
        functools.partial(map_kernel, flips, parts, len(ts), feat),
        [xaug if small else xaug[:, :own_sources], taug, g, q, logw] + exchange(sums) + ts,
        [
            jax.ShapeDtypeStruct((feat, own_sources), f32),
            jax.ShapeDtypeStruct((1, own_targets), f32),
        ],
        [
            pltpu.VMEM((total, DEPTH), bf16),
            pltpu.VMEM((total, own_sources), f32),
            pltpu.VMEM((total, own_sources), bf16),
            pltpu.VMEM((feat, total), bf16),
        ],
        scalars=0,
    )
    return (mapped, potential.reshape(own_targets))


def solution(mesh):
    count = mesh.shape[AXIS]
    placed = (
        P(None, ("grp", "wide")),
        P(None, ("grp", "wide")),
        P(("grp", "wide")),
        P(("grp", "wide")),
        P(),
    )

    def body(*blocks):
        return on_device(*blocks, count)

    return jax.shard_map(
        body,
        mesh=mesh,
        in_specs=placed,
        out_specs=(P(None, ("grp", "wide")), P(("grp", "wide"))),
        check_vma=False,
    )
```

```python
import functools
import math

import jax
import jax.numpy as jnp
from jax import lax
from jax.experimental import pallas as pl
from jax.experimental.pallas import tpu as pltpu
from jax.sharding import PartitionSpec as P

ITERS = 2
AXIS = "wide"
LOG2E = math.log2(math.e)
LANES = 128
DEPTH = 256
SMALL_ROW = 2.0**-64
SMALL_COL = 2.0**-32
LARGE_COL = 2.0**100
FLOOR = -1e30


def three_terms(value):
    high = value.astype(jnp.bfloat16)
    rest = value - high.astype(jnp.float32)
    middle = rest.astype(jnp.bfloat16)
    low = (rest - middle.astype(jnp.float32)).astype(jnp.bfloat16)
    return high, middle, low


def pick_rows(shape, rows):
    index = lax.broadcasted_iota(jnp.int32, shape, 0)
    out = jnp.zeros(shape, jnp.float32)
    for place, row in enumerate(rows):
        out = jnp.where(index == place, row, out)
    return out


def stage_source(points, scale, xaug, at):
    feat, count = points.shape
    wide = points.astype(jnp.float32)
    shift = scale * jnp.sum(wide * wide, axis=0, keepdims=True)
    shift = shift.astype(jnp.bfloat16).astype(jnp.float32)
    xaug[0:feat, at] = pick_rows((feat, count), [1.0, 1.0, 1.0, -shift]).astype(jnp.bfloat16)
    for place, term in enumerate(three_terms(2.0 * scale * wide)):
        xaug[(place + 1) * feat : (place + 2) * feat, at] = term


def stage_sources(parts, scale, xaug, begin=0):
    for part in parts:
        count = part.shape[2]
        for block in range(part.shape[0]):
            stage_source(part[block], scale, xaug, slice(begin, begin + count))
            begin += count


def target_lines(part, block, scale, feat):
    wide = part[block, :feat, :].astype(jnp.float32)
    logw = part[block, feat : feat + 16, :].astype(jnp.float32)[0:1]
    return scale * jnp.sum(wide * wide, axis=0, keepdims=True), logw * LOG2E


def stage_targets(parts, scale, taug, begin, feat):
    for part in parts:
        for block in range(part.shape[0]):
            q, logw = target_lines(part, block, scale, feat)
            terms = [term.astype(jnp.float32) for term in three_terms(logw - q)]
            extras = pick_rows((feat, LANES), terms + [1.0])
            wide = part[block, :feat, :].astype(jnp.float32)
            turned = jnp.concatenate([extras, wide], axis=0).T
            lane = lax.broadcasted_iota(jnp.int32, turned.shape, 1)
            twice = jnp.where(lane < feat, pltpu.roll(turned, feat, 1), turned)
            taug[begin : begin + LANES, 0:LANES] = turned.astype(jnp.bfloat16)
            taug[begin : begin + LANES, LANES:DEPTH] = twice.astype(jnp.bfloat16)
            begin += LANES


def renew_targets(lines, flips, parts, g, q, logw, taug):
    total = lines[0].shape[1]
    size = total // (2 * parts)
    held = []
    for line, (core, digit) in zip(lines, flips):
        value = line[...]
        places = [(block ^ (core * parts)) ^ digit for block in range(2 * parts)]
        pieces = [value[:, place * size : (place + 1) * size] for place in places]
        held.append(jnp.concatenate(pieces, axis=1))
    peak = functools.reduce(jnp.maximum, held)
    added = functools.reduce(jnp.add, [jnp.exp2(value - peak) for value in held])
    potential = g - (peak + jnp.log2(added))
    g = potential + logw
    terms = [term.astype(jnp.float32) for term in three_terms(g - jnp.max(g) - q)]
    for begin in range(0, total, LANES):
        rows = slice(begin, begin + LANES)
        extras = pick_rows((8, LANES), [term[:, rows] for term in terms] + [1.0])
        taug[rows, 0:8] = extras.T.astype(jnp.bfloat16)
    return potential, g


def exponents(left, right):
    return jnp.dot(left, right, preferred_element_type=jnp.float32)


def spread_rows(taug, right, p_ref, beside):
    total, width = taug.shape[0], right.shape[1]
    reach = min(total, 512)
    sums = jnp.zeros((8, width), jnp.float32)
    for begin in range(0, total, reach):
        e = exponents(taug[begin : begin + reach, :], right)
        for inner in range(0, reach, LANES):
            rows = slice(begin + inner, begin + inner + LANES)
            beside(rows)
            p = jnp.exp2(e[inner : inner + LANES])
            p_ref[rows, :] = p
            sums = sums + jnp.sum(p.reshape(LANES // 8, 8, width), axis=0)
    return jnp.sum(sums, axis=0, keepdims=True)


def add_columns(p_ref, weight, col_refs, rows):
    width = weight.shape[1]
    added = p_ref[rows, 0:LANES] * weight[:, 0:LANES]
    for lane in range(LANES, width, LANES):
        added = added + p_ref[rows, lane : lane + LANES] * weight[:, lane : lane + LANES]
    col_ref, at = column_block(col_refs, rows)
    col_ref[at, :] += added


def column_block(col_refs, rows):
    size = col_refs[0].shape[0]
    place = rows.start // size
    return col_refs[place], slice(rows.start - place * size, rows.stop - place * size)


def tile_columns(tile, width):
    if isinstance(tile, int):
        return pl.ds(tile * width, width)
    return pl.ds(pl.multiple_of(tile * width, width), width)


def add_sources(xaug, logws, taug, p_refs, col_refs):
    total = taug.shape[0]
    width = p_refs[0].shape[1]
    tiles = xaug.shape[1] // width
    if p_refs[1].shape != p_refs[0].shape:
        p_refs = (p_refs[0], p_refs[0])

    def step(tile, slot, held):
        def beside(rows):
            if held is not None:
                add_columns(p_refs[1 - slot], held, col_refs, rows)

        at = tile_columns(tile, width)
        s = spread_rows(taug, xaug[:, at], p_refs[slot], beside)
        return s, jnp.exp2(logws[:, at] * LOG2E) / s

    if tiles == 3:
        least, weight = step(0, 0, None)
        for tile in range(1, tiles):
            s, weight = step(tile, tile % 2, weight)
            least = jnp.minimum(least, s)
        for begin in range(0, total, LANES):
            add_columns(p_refs[0], weight, col_refs, slice(begin, begin + LANES))
        return least

    def two_steps(pair, carry):
        least, weight = carry
        s1, weight1 = step(2 * pair + 1, 1, weight)
        s0, weight0 = step(2 * pair + 2, 0, weight1)
        return jnp.minimum(least, jnp.minimum(s0, s1)), weight0

    s, weight = step(0, 0, None)
    least, weight = lax.fori_loop(0, tiles // 2 - 1, two_steps, (s, weight))
    s, weight = step(tiles - 1, 1, weight)
    for begin in range(0, total, LANES):
        add_columns(p_refs[1], weight, col_refs, slice(begin, begin + LANES))
    return jnp.minimum(least, s)


def lane_tiles(width):
    return [slice(begin, begin + LANES) for begin in range(0, width, LANES)]


def lane_totals(col_refs, out_ref):
    total = sum(col_ref.shape[0] for col_ref in col_refs)
    reach = min(total, 2048)
    ones = jnp.ones((16, 2 * LANES), jnp.bfloat16)
    sizes = col_refs[0].shape[0]
    for begin in range(0, total, reach):
        refs = col_refs[begin // sizes : (begin + reach) // sizes]
        high, middle, _ = three_terms(jnp.concatenate([col_ref[...] for col_ref in refs], axis=0))
        both = jnp.concatenate([high, middle], axis=1)
        added = lax.dot_general(
            ones, both, (((1,), (1,)), ((), ())), preferred_element_type=jnp.float32
        )
        out_ref[:, begin : begin + reach] = added[0:1]


def finish_sums(xaug, logws, taug, least, p_ref, col_refs, out_ref):
    total = taug.shape[0]
    lane_totals(col_refs, out_ref)
    cols = out_ref[...]
    out_ref[...] = jnp.log2(cols)
    fine = jnp.logical_and(
        jnp.min(least) >= SMALL_ROW,
        jnp.logical_and(jnp.min(cols) >= SMALL_COL, jnp.max(cols) <= LARGE_COL),
    )
    top_ref = p_ref.at[:, 0:LANES]

    @pl.when(jnp.logical_not(fine))
    def _():
        for col_ref in col_refs:
            col_ref[...] = jnp.zeros_like(col_ref)
        top_ref[...] = jnp.full_like(top_ref, FLOOR)

        def careful(tile, carry):
            at = tile_columns(tile, LANES)
            right = xaug[:, at]

            def block_rows(block):
                return pl.ds(pl.multiple_of(block * LANES, LANES), LANES)

            def highest(block, peak):
                e = exponents(taug[block_rows(block), :], right)
                return jnp.maximum(peak, jnp.max(e, axis=0, keepdims=True))

            peak = jnp.full((1, LANES), FLOOR, jnp.float32)
            peak = lax.fori_loop(0, total // LANES, highest, peak)

            def summed(block, s):
                e = exponents(taug[block_rows(block), :], right)
                return s + jnp.sum(jnp.exp2(e - peak), axis=0, keepdims=True)

            s = lax.fori_loop(0, total // LANES, summed, jnp.zeros((1, LANES), jnp.float32))
            shift = logws[:, at] * LOG2E - peak - jnp.log2(s)

            size = col_refs[0].shape[0]
            for place, col_ref in enumerate(col_refs):

                def collected(block, carry, place=place, col_ref=col_ref):
                    rows = block_rows(place * (size // LANES) + block)
                    term = exponents(taug[rows, :], right) + shift
                    old = top_ref[rows, :]
                    top = jnp.maximum(old, term)
                    here = block_rows(block)
                    col = col_ref[here, :] * jnp.exp2(old - top) + jnp.exp2(term - top)
                    col_ref[here, :] = col
                    top_ref[rows, :] = top
                    return carry

                lax.fori_loop(0, size // LANES, collected, 0)
            return carry

        lax.fori_loop(0, xaug.shape[1] // LANES, careful, 0)
        for begin in range(0, total, LANES):
            rows = slice(begin, begin + LANES)
            col_ref, at = column_block(col_refs, rows)
            tops = top_ref[rows, :].T
            top = jnp.max(tops, axis=0, keepdims=True)
            added = jnp.sum(col_ref[at, :].T * jnp.exp2(tops - top), axis=0, keepdims=True)
            out_ref[:, rows] = top + jnp.log2(added)


def part_kernel(feat, inverse, *refs):
    stage_targets(refs[:-1], inverse[0] * LOG2E, refs[-1], 0, feat)


def near_kernel(parts, feat, inverse, logws, xs, mine, rest, theirs, *refs):
    ts, refs = refs[: 2 * parts], refs[2 * parts :]
    xaug, taug, out_ref, g_ref, q_ref, p0, p1, *col_refs = refs
    scale = inverse[0] * LOG2E
    stage_sources([xs], scale, xaug)
    place = 0
    for part in ts:
        for block in range(part.shape[0]):
            at = slice(place * LANES, (place + 1) * LANES)
            q_ref[:, at], g_ref[:, at] = target_lines(part, block, scale, feat)
            place += 1
    begin = 0
    for part in (mine, rest, theirs):
        taug[begin : begin + part.shape[0], :] = part[...]
        begin += part.shape[0]
    stage_targets(ts[parts + 1 :], scale, taug, begin, feat)
    for col_ref in col_refs:
        col_ref[...] = jnp.zeros_like(col_ref)
    least = add_sources(xaug, logws, taug, (p0, p1), col_refs)
    finish_sums(xaug, logws, taug, least, p0, col_refs, out_ref)


def next_kernel(flips, parts, logws, xaug, old, g, q, logw, *refs):
    lines, refs = refs[: len(flips)], refs[len(flips) :]
    out_ref, g_ref, taug, p0, p1, *col_refs = refs
    taug[...] = old[...]
    g_ref[...] = renew_targets(lines, flips, parts, g[...], q[...], logw[...], taug)[1]
    for col_ref in col_refs:
        col_ref[...] = jnp.zeros_like(col_ref)
    least = add_sources(xaug, logws, taug, (p0, p1), col_refs)
    finish_sums(xaug, logws, taug, least, p0, col_refs, out_ref)


def careful_plan(taug, right, p_ref, plan_ref):
    total = taug.shape[0]
    reach = min(total, 2048)
    pieces = [slice(begin, begin + reach) for begin in range(0, total, reach)]
    peak = jnp.full((1, p_ref.shape[1]), FLOOR, jnp.float32)
    for rows in pieces:
        p_ref[rows, :] = exponents(taug[rows, :], right)
        peak = jnp.maximum(peak, jnp.max(p_ref[rows, :], axis=0, keepdims=True))
    sums = jnp.zeros(peak.shape, jnp.float32)
    for rows in pieces:
        sums += jnp.sum(jnp.exp2(p_ref[rows, :] - peak), axis=0, keepdims=True)
    shift = peak + jnp.log2(sums)
    for rows in pieces:
        plan_ref[rows, :] = jnp.exp2(p_ref[rows, :] - shift).astype(jnp.bfloat16)


def map_kernel(flips, parts, n_t, feat, xaug, old, g, q, logw, *refs):
    lines, refs = refs[: len(flips)], refs[len(flips) :]
    ts = refs[:n_t]
    mapped_ref, pot_ref, taug, *p_refs, coords = refs[n_t:]
    p_refs, plan_refs = p_refs[: len(p_refs) // 2], p_refs[len(p_refs) // 2 :]
    taug[...] = old[...]
    potential = renew_targets(lines, flips, parts, g[...], q[...], logw[...], taug)[0]
    pot_ref[...] = potential[:, :LANES] * (1.0 / LOG2E)
    place = 0
    for part in ts:
        for block in range(part.shape[0]):
            coords[:, place * LANES : (place + 1) * LANES] = part[block, :feat, :]
            place += 1
    sides, first = [], 0
    repeats = mapped_ref.shape[1] // p_refs[0].shape[1] if len(p_refs) == 1 else 1
    for p_ref, plan_ref in list(zip(p_refs, plan_refs)) * repeats:
        sides.append((slice(first, first + p_ref.shape[1]), p_ref, plan_ref))
        first += p_ref.shape[1]
    least = []
    for at, p_ref, plan_ref in sides:
        s = spread_rows(taug, xaug[:, at], p_ref, lambda rows: None)
        least += [s[:, tile] for tile in lane_tiles(s.shape[1])]
        weight = 1.0 / s
        for begin in range(0, taug.shape[0], LANES):
            rows = slice(begin, begin + LANES)
            plan_ref[rows, :] = (p_ref[rows, :] * weight).astype(jnp.bfloat16)
        mapped_ref[:, at] = jnp.dot(coords[...], plan_ref[...], preferred_element_type=jnp.float32)

    @pl.when(jnp.logical_not(jnp.min(functools.reduce(jnp.minimum, least)) >= SMALL_ROW))
    def _():
        for at, p_ref, plan_ref in sides:
            careful_plan(taug, xaug[:, at], p_ref, plan_ref)
            mapped_ref[:, at] = jnp.dot(
                coords[...], plan_ref[...], preferred_element_type=jnp.float32
            )


def swap(value, count, step):
    return lax.ppermute(value, AXIS, [(source, source ^ step) for source in range(count)])


def chip_stages(count):
    high, stages = count.bit_length() - 1, []
    while high > 1:
        width = min(2, high - 1)
        stages.append((high - width, width))
        high -= width
    return stages


def gather_stage(parts, count, low, width):
    held = parts[0] if len(parts) == 1 else jnp.concatenate(parts, axis=0)
    return [held] + [swap(held, count, digit << low) for digit in range(1, 1 << width)]


def gather_chips(block, count):
    parts = [block[None]]
    for low, width in chip_stages(count):
        parts = gather_stage(parts, count, low, width)
    return parts


def gather_line(block, count):
    parts = [block[None]]
    for low, width in chip_stages(count)[:-1]:
        parts = gather_stage(parts, count, low, width)
    return jnp.concatenate(parts, axis=0)


def on_device(source_points, target_points, source_logw, target_logw, inverse_eps, count):
    feat, own_sources = source_points.shape
    own_targets = target_points.shape[1]
    extra_rows = own_sources // LANES
    pad = -(1 + extra_rows) % 16
    packed = jnp.concatenate(
        [
            target_points,
            target_logw[None, :],
            source_logw.reshape(extra_rows, LANES),
            jnp.zeros((pad, own_targets), target_points.dtype),
        ],
        axis=0,
    )
    f32, bf16 = jnp.float32, jnp.bfloat16
    total = count * own_targets
    small = total <= 4096
    width = 2 * LANES if small else LANES
    vmem = pl.BlockSpec(memory_space=pltpu.VMEM)
    smem = pl.BlockSpec(memory_space=pltpu.SMEM)
    params = pltpu.CompilerParams(vmem_limit_bytes=(24 if small else 63) << 20)
    line = jax.ShapeDtypeStruct((1, total), f32)

    def call(kernel, operands, outs, scratch=(), scalars=1):
        return pl.pallas_call(
            kernel,
            out_shape=outs,
            in_specs=[smem] * scalars + [vmem] * (len(operands) - scalars),
            out_specs=[vmem] * len(outs),
            scratch_shapes=list(scratch),
            compiler_params=params,
        )(*operands)

    def staged_shape(parts):
        rows = sum(part.shape[0] for part in parts) * own_targets
        return jax.ShapeDtypeStruct((rows, DEPTH), bf16)

    def logw_line(parts):
        rows = [part[:, feat + 1 : feat + 1 + extra_rows] for part in parts]
        return jnp.concatenate(rows, axis=0).reshape(1, -1).astype(f32)

    packed, points = lax.optimization_barrier((packed, source_points))
    mine = gather_chips(packed, count)
    theirs = [swap(part, count, 1) for part in mine]
    parts, low = len(mine), chip_stages(count)[-1][0]
    ts = mine + theirs
    (taug_mine,) = call(
        functools.partial(part_kernel, feat),
        [inverse_eps, mine[0]],
        [staged_shape(mine[:1])],
    )
    (taug_theirs,) = call(
        functools.partial(part_kernel, feat),
        [inverse_eps, theirs[0]],
        [staged_shape(theirs[:1])],
    )
    (taug_rest,) = call(
        functools.partial(part_kernel, feat),
        [inverse_eps] + mine[1:],
        [staged_shape(mine[1:])],
    )
    xs = gather_line(points, count)
    logws = logw_line(mine[:1])
    rows = logws.shape[1]

    p_scratch = pltpu.VMEM((total, width), f32)
    scratch = [
        p_scratch,
        p_scratch if small else pltpu.VMEM((8, LANES), f32),
    ] + [pltpu.VMEM((total // 16, LANES), f32)] * 16
    p_wide = pltpu.VMEM((total, 4 * LANES), f32)
    wide_scratch = [p_wide, p_wide] + scratch[2:] if rows == 12 * LANES and small else scratch
    xaug, taug, sums, logw, q = call(
        functools.partial(near_kernel, parts, feat),
        [inverse_eps, logws, xs, taug_mine, taug_rest, taug_theirs] + ts,
        [
            jax.ShapeDtypeStruct((DEPTH, rows), bf16),
            jax.ShapeDtypeStruct((total, DEPTH), bf16),
            line,
            line,
            line,
        ],
        scratch,
    )
    flips = [(core, digit) for digit in range(parts) for core in range(2)]

    def exchange(own):
        return [own] + [swap(own, count, core | (digit << low)) for core, digit in flips[1:]]

    g = logw
    for _ in range(ITERS - 1):
        sums, g = call(
            functools.partial(next_kernel, flips, parts),
            [logws, xaug, taug, g, q, logw] + exchange(sums),
            [line, line],
            [pltpu.VMEM((total, DEPTH), bf16)] + wide_scratch,
            scalars=0,
        )
    sides = [2 * LANES, own_sources - 2 * LANES] if small else [LANES]
    mapped, potential = call(
        functools.partial(map_kernel, flips, parts, len(ts), feat),
        [xaug if small else xaug[:, :own_sources], taug, g, q, logw] + exchange(sums) + ts,
        [
            jax.ShapeDtypeStruct((feat, own_sources), f32),
            jax.ShapeDtypeStruct((1, own_targets), f32),
        ],
        [
            pltpu.VMEM((total, DEPTH), bf16),
        ]
        + [pltpu.VMEM((total, side), f32) for side in sides]
        + [pltpu.VMEM((total, side), bf16) for side in sides]
        + [pltpu.VMEM((feat, total), bf16)],
        scalars=0,
    )
    return (mapped, potential.reshape(own_targets))


def solution(mesh):
    count = mesh.shape[AXIS]
    placed = (
        P(None, ("grp", "wide")),
        P(None, ("grp", "wide")),
        P(("grp", "wide")),
        P(("grp", "wide")),
        P(),
    )

    def body(*blocks):
        return on_device(*blocks, count)

    return jax.shard_map(
        body,
        mesh=mesh,
        in_specs=placed,
        out_specs=(P(None, ("grp", "wide")), P(("grp", "wide"))),
        check_vma=False,
    )
```

```python
import functools
import math

import jax
import jax.numpy as jnp
from jax import lax
from jax.experimental import pallas as pl
from jax.experimental.pallas import tpu as pltpu
from jax.sharding import PartitionSpec as P

ITERS = 2
AXIS = "wide"
LOG2E = math.log2(math.e)
LANES = 128
DEPTH = 256
SMALL_ROW = 2.0**-64
SMALL_COL = 2.0**-32
LARGE_COL = 2.0**100
FLOOR = -1e30


def three_terms(value):
    high = value.astype(jnp.bfloat16)
    rest = value - high.astype(jnp.float32)
    middle = rest.astype(jnp.bfloat16)
    low = (rest - middle.astype(jnp.float32)).astype(jnp.bfloat16)
    return high, middle, low


def pick_rows(shape, rows):
    index = lax.broadcasted_iota(jnp.int32, shape, 0)
    out = jnp.zeros(shape, jnp.float32)
    for place, row in enumerate(rows):
        out = jnp.where(index == place, row, out)
    return out


def stage_source(points, scale, xaug, at):
    feat, count = points.shape
    wide = points.astype(jnp.float32)
    shift = scale * jnp.sum(wide * wide, axis=0, keepdims=True)
    shift = shift.astype(jnp.bfloat16).astype(jnp.float32)
    xaug[0:feat, at] = pick_rows((feat, count), [1.0, 1.0, 1.0, -shift]).astype(jnp.bfloat16)
    for place, term in enumerate(three_terms(2.0 * scale * wide)):
        xaug[(place + 1) * feat : (place + 2) * feat, at] = term


def stage_sources(parts, scale, xaug, begin=0):
    for part in parts:
        count = part.shape[2]
        for block in range(part.shape[0]):
            stage_source(part[block], scale, xaug, slice(begin, begin + count))
            begin += count


def target_lines(part, block, scale, feat):
    wide = part[block, :feat, :].astype(jnp.float32)
    logw = part[block, feat : feat + 16, :].astype(jnp.float32)[0:1]
    return scale * jnp.sum(wide * wide, axis=0, keepdims=True), logw * LOG2E


def stage_targets(parts, scale, taug, begin, feat):
    for part in parts:
        for block in range(part.shape[0]):
            q, logw = target_lines(part, block, scale, feat)
            terms = [term.astype(jnp.float32) for term in three_terms(logw - q)]
            extras = pick_rows((feat, LANES), terms + [1.0])
            wide = part[block, :feat, :].astype(jnp.float32)
            turned = jnp.concatenate([extras, wide], axis=0).T
            lane = lax.broadcasted_iota(jnp.int32, turned.shape, 1)
            twice = jnp.where(lane < feat, pltpu.roll(turned, feat, 1), turned)
            taug[begin : begin + LANES, 0:LANES] = turned.astype(jnp.bfloat16)
            taug[begin : begin + LANES, LANES:DEPTH] = twice.astype(jnp.bfloat16)
            begin += LANES


def renew_targets(lines, flips, parts, g, q, logw, taug):
    total = lines[0].shape[1]
    size = total // (2 * parts)
    held = []
    for line, (core, digit) in zip(lines, flips):
        value = line[...]
        places = [(block ^ (core * parts)) ^ digit for block in range(2 * parts)]
        pieces = [value[:, place * size : (place + 1) * size] for place in places]
        held.append(jnp.concatenate(pieces, axis=1))
    peak = functools.reduce(jnp.maximum, held)
    added = functools.reduce(jnp.add, [jnp.exp2(value - peak) for value in held])
    potential = g - (peak + jnp.log2(added))
    g = potential + logw
    terms = [term.astype(jnp.float32) for term in three_terms(g - jnp.max(g) - q)]
    for begin in range(0, total, LANES):
        rows = slice(begin, begin + LANES)
        extras = pick_rows((8, LANES), [term[:, rows] for term in terms] + [1.0])
        taug[rows, 0:8] = extras.T.astype(jnp.bfloat16)
    return potential, g


def exponents(left, right):
    return jnp.dot(left, right, preferred_element_type=jnp.float32)


def spread_rows(taug, right, p_ref, beside):
    total, width = taug.shape[0], right.shape[1]
    reach = min(total, 512)
    sums = jnp.zeros((8, width), jnp.float32)
    for begin in range(0, total, reach):
        e = exponents(taug[begin : begin + reach, :], right)
        for inner in range(0, reach, LANES):
            rows = slice(begin + inner, begin + inner + LANES)
            beside(rows)
            p = jnp.exp2(e[inner : inner + LANES])
            p_ref[rows, :] = p
            sums = sums + jnp.sum(p.reshape(LANES // 8, 8, width), axis=0)
    return jnp.sum(sums, axis=0, keepdims=True)


def add_columns(p_ref, weight, col_refs, rows):
    width = weight.shape[1]
    added = p_ref[rows, 0:LANES] * weight[:, 0:LANES]
    for lane in range(LANES, width, LANES):
        added = added + p_ref[rows, lane : lane + LANES] * weight[:, lane : lane + LANES]
    col_ref, at = column_block(col_refs, rows)
    col_ref[at, :] += added


def column_block(col_refs, rows):
    size = col_refs[0].shape[0]
    place = rows.start // size
    return col_refs[place], slice(rows.start - place * size, rows.stop - place * size)


def tile_columns(tile, width):
    if isinstance(tile, int):
        return pl.ds(tile * width, width)
    return pl.ds(pl.multiple_of(tile * width, width), width)


def add_sources(xaug, logws, taug, p_refs, col_refs):
    total = taug.shape[0]
    width = p_refs[0].shape[1]
    tiles = xaug.shape[1] // width
    if p_refs[1].shape != p_refs[0].shape:
        p_refs = (p_refs[0], p_refs[0])

    def step(tile, slot, held):
        def beside(rows):
            if held is not None:
                add_columns(p_refs[1 - slot], held, col_refs, rows)

        at = tile_columns(tile, width)
        s = spread_rows(taug, xaug[:, at], p_refs[slot], beside)
        return s, jnp.exp2(logws[:, at] * LOG2E) / s

    if tiles == 3:
        least, weight = step(0, 0, None)
        for tile in range(1, tiles):
            s, weight = step(tile, tile % 2, weight)
            least = jnp.minimum(least, s)
        for begin in range(0, total, LANES):
            add_columns(p_refs[0], weight, col_refs, slice(begin, begin + LANES))
        return least

    def two_steps(pair, carry):
        least, weight = carry
        s1, weight1 = step(2 * pair + 1, 1, weight)
        s0, weight0 = step(2 * pair + 2, 0, weight1)
        return jnp.minimum(least, jnp.minimum(s0, s1)), weight0

    s, weight = step(0, 0, None)
    least, weight = lax.fori_loop(0, tiles // 2 - 1, two_steps, (s, weight))
    s, weight = step(tiles - 1, 1, weight)
    for begin in range(0, total, LANES):
        add_columns(p_refs[1], weight, col_refs, slice(begin, begin + LANES))
    return jnp.minimum(least, s)


def lane_totals(col_refs, out_ref):
    total = sum(col_ref.shape[0] for col_ref in col_refs)
    reach = min(total, 2048)
    ones = jnp.ones((16, 2 * LANES), jnp.bfloat16)
    sizes = col_refs[0].shape[0]
    for begin in range(0, total, reach):
        refs = col_refs[begin // sizes : (begin + reach) // sizes]
        high, middle, _ = three_terms(jnp.concatenate([col_ref[...] for col_ref in refs], axis=0))
        both = jnp.concatenate([high, middle], axis=1)
        added = lax.dot_general(
            ones, both, (((1,), (1,)), ((), ())), preferred_element_type=jnp.float32
        )
        out_ref[:, begin : begin + reach] = added[0:1]


def finish_sums(xaug, logws, taug, least, p_ref, col_refs, out_ref):
    total = taug.shape[0]
    lane_totals(col_refs, out_ref)
    cols = out_ref[...]
    out_ref[...] = jnp.log2(cols)
    fine = jnp.logical_and(
        jnp.min(least) >= SMALL_ROW,
        jnp.logical_and(jnp.min(cols) >= SMALL_COL, jnp.max(cols) <= LARGE_COL),
    )
    top_ref = p_ref.at[:, 0:LANES]

    @pl.when(jnp.logical_not(fine))
    def _():
        for col_ref in col_refs:
            col_ref[...] = jnp.zeros_like(col_ref)
        top_ref[...] = jnp.full_like(top_ref, FLOOR)

        def careful(tile, carry):
            at = tile_columns(tile, LANES)
            right = xaug[:, at]

            def block_rows(block):
                return pl.ds(pl.multiple_of(block * LANES, LANES), LANES)

            def highest(block, peak):
                e = exponents(taug[block_rows(block), :], right)
                return jnp.maximum(peak, jnp.max(e, axis=0, keepdims=True))

            peak = jnp.full((1, LANES), FLOOR, jnp.float32)
            peak = lax.fori_loop(0, total // LANES, highest, peak)

            def summed(block, s):
                e = exponents(taug[block_rows(block), :], right)
                return s + jnp.sum(jnp.exp2(e - peak), axis=0, keepdims=True)

            s = lax.fori_loop(0, total // LANES, summed, jnp.zeros((1, LANES), jnp.float32))
            shift = logws[:, at] * LOG2E - peak - jnp.log2(s)

            size = col_refs[0].shape[0]
            for place, col_ref in enumerate(col_refs):

                def collected(block, carry, place=place, col_ref=col_ref):
                    rows = block_rows(place * (size // LANES) + block)
                    term = exponents(taug[rows, :], right) + shift
                    old = top_ref[rows, :]
                    top = jnp.maximum(old, term)
                    here = block_rows(block)
                    col = col_ref[here, :] * jnp.exp2(old - top) + jnp.exp2(term - top)
                    col_ref[here, :] = col
                    top_ref[rows, :] = top
                    return carry

                lax.fori_loop(0, size // LANES, collected, 0)
            return carry

        lax.fori_loop(0, xaug.shape[1] // LANES, careful, 0)
        for begin in range(0, total, LANES):
            rows = slice(begin, begin + LANES)
            col_ref, at = column_block(col_refs, rows)
            tops = top_ref[rows, :].T
            top = jnp.max(tops, axis=0, keepdims=True)
            added = jnp.sum(col_ref[at, :].T * jnp.exp2(tops - top), axis=0, keepdims=True)
            out_ref[:, rows] = top + jnp.log2(added)


def part_kernel(feat, inverse, *refs):
    stage_targets(refs[:-1], inverse[0] * LOG2E, refs[-1], 0, feat)


def near_kernel(parts, feat, inverse, logws, xs, mine, rest, theirs, *refs):
    ts, refs = refs[: 2 * parts], refs[2 * parts :]
    xaug, taug, out_ref, g_ref, q_ref, p0, p1, *col_refs = refs
    scale = inverse[0] * LOG2E
    stage_sources([xs], scale, xaug)
    place = 0
    for part in ts:
        for block in range(part.shape[0]):
            at = slice(place * LANES, (place + 1) * LANES)
            q_ref[:, at], g_ref[:, at] = target_lines(part, block, scale, feat)
            place += 1
    begin = 0
    for part in (mine, rest, theirs):
        taug[begin : begin + part.shape[0], :] = part[...]
        begin += part.shape[0]
    stage_targets(ts[parts + 1 :], scale, taug, begin, feat)
    for col_ref in col_refs:
        col_ref[...] = jnp.zeros_like(col_ref)
    least = add_sources(xaug, logws, taug, (p0, p1), col_refs)
    finish_sums(xaug, logws, taug, least, p0, col_refs, out_ref)


def next_kernel(flips, parts, logws, xaug, old, g, q, logw, *refs):
    lines, refs = refs[: len(flips)], refs[len(flips) :]
    out_ref, g_ref, taug, p0, p1, *col_refs = refs
    taug[...] = old[...]
    g_ref[...] = renew_targets(lines, flips, parts, g[...], q[...], logw[...], taug)[1]
    for col_ref in col_refs:
        col_ref[...] = jnp.zeros_like(col_ref)
    least = add_sources(xaug, logws, taug, (p0, p1), col_refs)
    finish_sums(xaug, logws, taug, least, p0, col_refs, out_ref)


def map_kernel(flips, parts, n_t, feat, xaug, old, g, q, logw, *refs):
    lines, refs = refs[: len(flips)], refs[len(flips) :]
    ts = refs[:n_t]
    mapped_ref, pot_ref, taug, p_ref, plan_ref, coords = refs[n_t:]
    taug[...] = old[...]
    potential = renew_targets(lines, flips, parts, g[...], q[...], logw[...], taug)[0]
    pot_ref[...] = potential[:, :LANES] * (1.0 / LOG2E)
    place = 0
    for part in ts:
        for block in range(part.shape[0]):
            coords[:, place * LANES : (place + 1) * LANES] = part[block, :feat, :]
            place += 1
    total = taug.shape[0]
    right = xaug[:, : p_ref.shape[1]]
    s = spread_rows(taug, right, p_ref, lambda rows: None)
    weight = 1.0 / s
    for begin in range(0, total, LANES):
        rows = slice(begin, begin + LANES)
        plan_ref[rows, :] = (p_ref[rows, :] * weight).astype(jnp.bfloat16)

    @pl.when(jnp.logical_not(jnp.min(s) >= SMALL_ROW))
    def _():
        reach = min(total, 2048)
        peak = jnp.full(s.shape, FLOOR, jnp.float32)
        for begin in range(0, total, reach):
            rows = slice(begin, begin + reach)
            p_ref[rows, :] = exponents(taug[rows, :], right)
            peak = jnp.maximum(peak, jnp.max(p_ref[rows, :], axis=0, keepdims=True))
        sums = jnp.zeros(s.shape, jnp.float32)
        for begin in range(0, total, reach):
            rows = slice(begin, begin + reach)
            sums += jnp.sum(jnp.exp2(p_ref[rows, :] - peak), axis=0, keepdims=True)
        shift = peak + jnp.log2(sums)
        for begin in range(0, total, reach):
            rows = slice(begin, begin + reach)
            plan_ref[rows, :] = jnp.exp2(p_ref[rows, :] - shift).astype(jnp.bfloat16)

    mapped_ref[...] = jnp.dot(coords[...], plan_ref[...], preferred_element_type=jnp.float32)


def swap(value, count, step):
    return lax.ppermute(value, AXIS, [(source, source ^ step) for source in range(count)])


def chip_stages(count):
    high, stages = count.bit_length() - 1, []
    while high > 1:
        width = min(2, high - 1)
        stages.append((high - width, width))
        high -= width
    return stages


def gather_stage(parts, count, low, width):
    held = parts[0] if len(parts) == 1 else jnp.concatenate(parts, axis=0)
    return [held] + [swap(held, count, digit << low) for digit in range(1, 1 << width)]


def gather_line(block, count):
    parts = [block[None]]
    for low, width in chip_stages(count)[:-1]:
        parts = gather_stage(parts, count, low, width)
    return jnp.concatenate(parts, axis=0)


def on_device(source_points, target_points, source_logw, target_logw, inverse_eps, count):
    feat, own_sources = source_points.shape
    own_targets = target_points.shape[1]
    extra_rows = own_sources // LANES
    pad = -(1 + extra_rows) % 16
    packed = jnp.concatenate(
        [
            target_points,
            target_logw[None, :],
            source_logw.reshape(extra_rows, LANES),
            jnp.zeros((pad, own_targets), target_points.dtype),
        ],
        axis=0,
    )
    f32, bf16 = jnp.float32, jnp.bfloat16
    total = count * own_targets
    small = total <= 4096
    width = LANES
    if small:
        width = 4 * LANES if source_points.shape[1] % (3 * LANES) == 0 else 2 * LANES
    vmem = pl.BlockSpec(memory_space=pltpu.VMEM)
    smem = pl.BlockSpec(memory_space=pltpu.SMEM)
    params = pltpu.CompilerParams(vmem_limit_bytes=(24 if small else 63) << 20)
    line = jax.ShapeDtypeStruct((1, total), f32)

    def call(kernel, operands, outs, scratch=(), scalars=1):
        return pl.pallas_call(
            kernel,
            out_shape=outs,
            in_specs=[smem] * scalars + [vmem] * (len(operands) - scalars),
            out_specs=[vmem] * len(outs),
            scratch_shapes=list(scratch),
            compiler_params=params,
        )(*operands)

    def staged_shape(parts):
        rows = sum(part.shape[0] for part in parts) * own_targets
        return jax.ShapeDtypeStruct((rows, DEPTH), bf16)

    def logw_line(parts):
        rows = [part[:, feat + 1 : feat + 1 + extra_rows] for part in parts]
        return jnp.concatenate(rows, axis=0).reshape(1, -1).astype(f32)

    packed, points = lax.optimization_barrier((packed, source_points))
    low, last_width = chip_stages(count)[-1]
    parts = 1 << last_width
    held = gather_line(packed, count)
    (taug_mine,) = call(
        functools.partial(part_kernel, feat),
        [inverse_eps, held],
        [staged_shape([held])],
    )
    last, _ = lax.optimization_barrier((held, taug_mine))
    both = [[held, swap(last, count, 1)]]
    for digit in range(1, parts):
        both.append([swap(held, count, core | (digit << low)) for core in range(2)])
    mine, theirs = [pair[0] for pair in both], [pair[1] for pair in both]
    ts = mine + theirs
    (taug_theirs,) = call(
        functools.partial(part_kernel, feat),
        [inverse_eps, theirs[0]],
        [staged_shape(theirs[:1])],
    )
    tied = lax.optimization_barrier((*mine[1:], taug_theirs))
    (taug_rest,) = call(
        functools.partial(part_kernel, feat),
        [inverse_eps] + list(tied[:-1]),
        [staged_shape(mine[1:])],
    )
    xs = gather_line(points, count)
    logws = logw_line(mine[:1])
    rows = logws.shape[1]

    p_scratch = pltpu.VMEM((total, width), f32)
    scratch = [
        p_scratch,
        p_scratch if small else pltpu.VMEM((8, LANES), f32),
    ] + [pltpu.VMEM((total // 16, LANES), f32)] * 16
    xaug, taug, sums, logw, q = call(
        functools.partial(near_kernel, parts, feat),
        [inverse_eps, logws, xs, taug_mine, taug_rest, taug_theirs] + ts,
        [
            jax.ShapeDtypeStruct((DEPTH, rows), bf16),
            jax.ShapeDtypeStruct((total, DEPTH), bf16),
            line,
            line,
            line,
        ],
        scratch,
    )
    flips = [(core, digit) for digit in range(parts) for core in range(2)]

    def exchange(own):
        return [own] + [swap(own, count, core | (digit << low)) for core, digit in flips[1:]]

    g = logw
    for _ in range(ITERS - 1):
        sums, g = call(
            functools.partial(next_kernel, flips, parts),
            [logws, xaug, taug, g, q, logw] + exchange(sums),
            [line, line],
            [pltpu.VMEM((total, DEPTH), bf16)] + scratch,
            scalars=0,
        )
    mapped, potential = call(
        functools.partial(map_kernel, flips, parts, len(ts), feat),
        [xaug if small else xaug[:, :own_sources], taug, g, q, logw] + exchange(sums) + ts,
        [
            jax.ShapeDtypeStruct((feat, own_sources), f32),
            jax.ShapeDtypeStruct((1, own_targets), f32),
        ],
        [
            pltpu.VMEM((total, DEPTH), bf16),
            pltpu.VMEM((total, own_sources), f32),
            pltpu.VMEM((total, own_sources), bf16),
            pltpu.VMEM((feat, total), bf16),
        ],
        scalars=0,
    )
    return (mapped, potential.reshape(own_targets))


def solution(mesh):
    count = mesh.shape[AXIS]
    placed = (
        P(None, ("grp", "wide")),
        P(None, ("grp", "wide")),
        P(("grp", "wide")),
        P(("grp", "wide")),
        P(),
    )

    def body(*blocks):
        return on_device(*blocks, count)

    return jax.shard_map(
        body,
        mesh=mesh,
        in_specs=placed,
        out_specs=(P(None, ("grp", "wide")), P(("grp", "wide"))),
        check_vma=False,
    )
```

```python
import functools
import math

import jax
import jax.numpy as jnp
from jax import lax
from jax.experimental import pallas as pl
from jax.experimental.pallas import tpu as pltpu
from jax.sharding import PartitionSpec as P

ITERS = 2
AXIS = "wide"
LOG2E = math.log2(math.e)
LANES = 128
DEPTH = 256
SMALL_ROW = 2.0**-64
SMALL_COL = 2.0**-32
LARGE_COL = 2.0**100
FLOOR = -1e30


def three_terms(value):
    high = value.astype(jnp.bfloat16)
    rest = value - high.astype(jnp.float32)
    middle = rest.astype(jnp.bfloat16)
    low = (rest - middle.astype(jnp.float32)).astype(jnp.bfloat16)
    return high, middle, low


def pick_rows(shape, rows):
    index = lax.broadcasted_iota(jnp.int32, shape, 0)
    out = jnp.zeros(shape, jnp.float32)
    for place, row in enumerate(rows):
        out = jnp.where(index == place, row, out)
    return out


def stage_source(points, scale, xaug, at):
    feat, count = points.shape
    wide = points.astype(jnp.float32)
    shift = scale * jnp.sum(wide * wide, axis=0, keepdims=True)
    shift = shift.astype(jnp.bfloat16).astype(jnp.float32)
    xaug[0:feat, at] = pick_rows((feat, count), [1.0, 1.0, 1.0, -shift]).astype(jnp.bfloat16)
    for place, term in enumerate(three_terms(2.0 * scale * wide)):
        xaug[(place + 1) * feat : (place + 2) * feat, at] = term


def stage_sources(parts, scale, xaug, begin=0):
    for part in parts:
        count = part.shape[2]
        for block in range(part.shape[0]):
            stage_source(part[block], scale, xaug, slice(begin, begin + count))
            begin += count


def target_lines(part, block, scale, feat):
    wide = part[block, :feat, :].astype(jnp.float32)
    logw = part[block, feat : feat + 16, :].astype(jnp.float32)[0:1]
    return scale * jnp.sum(wide * wide, axis=0, keepdims=True), logw * LOG2E


def stage_targets(parts, scale, taug, begin, feat):
    for part in parts:
        for block in range(part.shape[0]):
            q, logw = target_lines(part, block, scale, feat)
            terms = [term.astype(jnp.float32) for term in three_terms(logw - q)]
            extras = pick_rows((feat, LANES), terms + [1.0])
            wide = part[block, :feat, :].astype(jnp.float32)
            turned = jnp.concatenate([extras, wide], axis=0).T
            lane = lax.broadcasted_iota(jnp.int32, turned.shape, 1)
            twice = jnp.where(lane < feat, pltpu.roll(turned, feat, 1), turned)
            taug[begin : begin + LANES, 0:LANES] = turned.astype(jnp.bfloat16)
            taug[begin : begin + LANES, LANES:DEPTH] = twice.astype(jnp.bfloat16)
            begin += LANES


def renew_targets(lines, flips, parts, g, q, logw, taug):
    total = lines[0].shape[1]
    size = total // (2 * parts)
    held = []
    for line, (core, digit) in zip(lines, flips):
        value = line[...]
        places = [(block ^ (core * parts)) ^ digit for block in range(2 * parts)]
        pieces = [value[:, place * size : (place + 1) * size] for place in places]
        held.append(jnp.concatenate(pieces, axis=1))
    peak = functools.reduce(jnp.maximum, held)
    added = functools.reduce(jnp.add, [jnp.exp2(value - peak) for value in held])
    potential = g - (peak + jnp.log2(added))
    g = potential + logw
    terms = [term.astype(jnp.float32) for term in three_terms(g - jnp.max(g) - q)]
    for begin in range(0, total, LANES):
        rows = slice(begin, begin + LANES)
        extras = pick_rows((8, LANES), [term[:, rows] for term in terms] + [1.0])
        taug[rows, 0:8] = extras.T.astype(jnp.bfloat16)
    return potential, g


def exponents(left, right):
    return jnp.dot(left, right, preferred_element_type=jnp.float32)


def spread_rows(taug, right, p_ref, beside, reach=512):
    total, width = taug.shape[0], right.shape[1]
    reach = min(total, reach)
    sums = jnp.zeros((8, width), jnp.float32)
    for begin in range(0, total, reach):
        e = exponents(taug[begin : begin + reach, :], right)
        for inner in range(0, reach, LANES):
            rows = slice(begin + inner, begin + inner + LANES)
            beside(rows)
            p = jnp.exp2(e[inner : inner + LANES])
            p_ref[rows, :] = p
            sums = sums + jnp.sum(p.reshape(LANES // 8, 8, width), axis=0)
    return jnp.sum(sums, axis=0, keepdims=True)


def add_columns(p_ref, weight, col_refs, rows):
    width = weight.shape[1]
    added = p_ref[rows, 0:LANES] * weight[:, 0:LANES]
    for lane in range(LANES, width, LANES):
        added = added + p_ref[rows, lane : lane + LANES] * weight[:, lane : lane + LANES]
    col_ref, at = column_block(col_refs, rows)
    col_ref[at, :] += added


def column_block(col_refs, rows):
    size = col_refs[0].shape[0]
    place = rows.start // size
    return col_refs[place], slice(rows.start - place * size, rows.stop - place * size)


def tile_columns(tile, width):
    if isinstance(tile, int):
        return pl.ds(tile * width, width)
    return pl.ds(pl.multiple_of(tile * width, width), width)


def add_sources(xaug, logws, taug, p_refs, col_refs, reach=512):
    total = taug.shape[0]
    width = p_refs[0].shape[1]
    tiles = xaug.shape[1] // width
    if p_refs[1].shape != p_refs[0].shape:
        p_refs = (p_refs[0], p_refs[0])

    def step(tile, slot, held):
        def beside(rows):
            if held is not None:
                add_columns(p_refs[1 - slot], held, col_refs, rows)

        at = tile_columns(tile, width)
        s = spread_rows(taug, xaug[:, at], p_refs[slot], beside, reach)
        return s, jnp.exp2(logws[:, at] * LOG2E) / s

    if tiles == 3:
        least, weight = step(0, 0, None)
        for tile in range(1, tiles):
            s, weight = step(tile, tile % 2, weight)
            least = jnp.minimum(least, s)
        for begin in range(0, total, LANES):
            add_columns(p_refs[0], weight, col_refs, slice(begin, begin + LANES))
        return least

    def two_steps(pair, carry):
        least, weight = carry
        s1, weight1 = step(2 * pair + 1, 1, weight)
        s0, weight0 = step(2 * pair + 2, 0, weight1)
        return jnp.minimum(least, jnp.minimum(s0, s1)), weight0

    s, weight = step(0, 0, None)
    least, weight = lax.fori_loop(0, tiles // 2 - 1, two_steps, (s, weight))
    s, weight = step(tiles - 1, 1, weight)
    for begin in range(0, total, LANES):
        add_columns(p_refs[1], weight, col_refs, slice(begin, begin + LANES))
    return jnp.minimum(least, s)


def lane_totals(col_refs, out_ref):
    total = sum(col_ref.shape[0] for col_ref in col_refs)
    reach = min(total, 2048)
    ones = jnp.ones((16, 2 * LANES), jnp.bfloat16)
    sizes = col_refs[0].shape[0]
    for begin in range(0, total, reach):
        refs = col_refs[begin // sizes : (begin + reach) // sizes]
        high, middle, _ = three_terms(jnp.concatenate([col_ref[...] for col_ref in refs], axis=0))
        both = jnp.concatenate([high, middle], axis=1)
        added = lax.dot_general(
            ones, both, (((1,), (1,)), ((), ())), preferred_element_type=jnp.float32
        )
        out_ref[:, begin : begin + reach] = added[0:1]


def finish_sums(xaug, logws, taug, least, p_ref, col_refs, out_ref):
    total = taug.shape[0]
    lane_totals(col_refs, out_ref)
    cols = out_ref[...]
    out_ref[...] = jnp.log2(cols)
    fine = jnp.logical_and(
        jnp.min(least) >= SMALL_ROW,
        jnp.logical_and(jnp.min(cols) >= SMALL_COL, jnp.max(cols) <= LARGE_COL),
    )
    top_ref = p_ref.at[:, 0:LANES]

    @pl.when(jnp.logical_not(fine))
    def _():
        for col_ref in col_refs:
            col_ref[...] = jnp.zeros_like(col_ref)
        top_ref[...] = jnp.full_like(top_ref, FLOOR)

        def careful(tile, carry):
            at = tile_columns(tile, LANES)
            right = xaug[:, at]

            def block_rows(block):
                return pl.ds(pl.multiple_of(block * LANES, LANES), LANES)

            def highest(block, peak):
                e = exponents(taug[block_rows(block), :], right)
                return jnp.maximum(peak, jnp.max(e, axis=0, keepdims=True))

            peak = jnp.full((1, LANES), FLOOR, jnp.float32)
            peak = lax.fori_loop(0, total // LANES, highest, peak)

            def summed(block, s):
                e = exponents(taug[block_rows(block), :], right)
                return s + jnp.sum(jnp.exp2(e - peak), axis=0, keepdims=True)

            s = lax.fori_loop(0, total // LANES, summed, jnp.zeros((1, LANES), jnp.float32))
            shift = logws[:, at] * LOG2E - peak - jnp.log2(s)

            size = col_refs[0].shape[0]
            for place, col_ref in enumerate(col_refs):

                def collected(block, carry, place=place, col_ref=col_ref):
                    rows = block_rows(place * (size // LANES) + block)
                    term = exponents(taug[rows, :], right) + shift
                    old = top_ref[rows, :]
                    top = jnp.maximum(old, term)
                    here = block_rows(block)
                    col = col_ref[here, :] * jnp.exp2(old - top) + jnp.exp2(term - top)
                    col_ref[here, :] = col
                    top_ref[rows, :] = top
                    return carry

                lax.fori_loop(0, size // LANES, collected, 0)
            return carry

        lax.fori_loop(0, xaug.shape[1] // LANES, careful, 0)
        for begin in range(0, total, LANES):
            rows = slice(begin, begin + LANES)
            col_ref, at = column_block(col_refs, rows)
            tops = top_ref[rows, :].T
            top = jnp.max(tops, axis=0, keepdims=True)
            added = jnp.sum(col_ref[at, :].T * jnp.exp2(tops - top), axis=0, keepdims=True)
            out_ref[:, rows] = top + jnp.log2(added)


def part_kernel(feat, inverse, *refs):
    stage_targets(refs[:-1], inverse[0] * LOG2E, refs[-1], 0, feat)


def near_kernel(parts, feat, inverse, logws, xs, mine, rest, theirs, *refs):
    ts, refs = refs[: 2 * parts], refs[2 * parts :]
    xaug, taug, out_ref, g_ref, q_ref, p0, p1, *col_refs = refs
    scale = inverse[0] * LOG2E
    stage_sources([xs], scale, xaug)
    place = 0
    for part in ts:
        for block in range(part.shape[0]):
            at = slice(place * LANES, (place + 1) * LANES)
            q_ref[:, at], g_ref[:, at] = target_lines(part, block, scale, feat)
            place += 1
    begin = 0
    for part in (mine, rest, theirs):
        taug[begin : begin + part.shape[0], :] = part[...]
        begin += part.shape[0]
    stage_targets(ts[parts + 1 :], scale, taug, begin, feat)
    for col_ref in col_refs:
        col_ref[...] = jnp.zeros_like(col_ref)
    least = add_sources(xaug, logws, taug, (p0, p1), col_refs, 256)
    finish_sums(xaug, logws, taug, least, p0, col_refs, out_ref)


def next_kernel(flips, parts, logws, xaug, old, g, q, logw, *refs):
    lines, refs = refs[: len(flips)], refs[len(flips) :]
    out_ref, g_ref, taug, p0, p1, *col_refs = refs
    taug[...] = old[...]
    g_ref[...] = renew_targets(lines, flips, parts, g[...], q[...], logw[...], taug)[1]
    for col_ref in col_refs:
        col_ref[...] = jnp.zeros_like(col_ref)
    least = add_sources(xaug, logws, taug, (p0, p1), col_refs)
    finish_sums(xaug, logws, taug, least, p0, col_refs, out_ref)


def map_kernel(flips, parts, n_t, feat, xaug, old, g, q, logw, *refs):
    lines, refs = refs[: len(flips)], refs[len(flips) :]
    ts = refs[:n_t]
    mapped_ref, pot_ref, taug, p_ref, plan_ref, coords = refs[n_t:]
    taug[...] = old[...]
    potential = renew_targets(lines, flips, parts, g[...], q[...], logw[...], taug)[0]
    pot_ref[...] = potential[:, :LANES] * (1.0 / LOG2E)
    place = 0
    for part in ts:
        for block in range(part.shape[0]):
            coords[:, place * LANES : (place + 1) * LANES] = part[block, :feat, :]
            place += 1
    total = taug.shape[0]
    right = xaug[:, : p_ref.shape[1]]
    s = spread_rows(taug, right, p_ref, lambda rows: None)
    weight = 1.0 / s
    for begin in range(0, total, LANES):
        rows = slice(begin, begin + LANES)
        plan_ref[rows, :] = (p_ref[rows, :] * weight).astype(jnp.bfloat16)

    @pl.when(jnp.logical_not(jnp.min(s) >= SMALL_ROW))
    def _():
        reach = min(total, 2048)
        peak = jnp.full(s.shape, FLOOR, jnp.float32)
        for begin in range(0, total, reach):
            rows = slice(begin, begin + reach)
            p_ref[rows, :] = exponents(taug[rows, :], right)
            peak = jnp.maximum(peak, jnp.max(p_ref[rows, :], axis=0, keepdims=True))
        sums = jnp.zeros(s.shape, jnp.float32)
        for begin in range(0, total, reach):
            rows = slice(begin, begin + reach)
            sums += jnp.sum(jnp.exp2(p_ref[rows, :] - peak), axis=0, keepdims=True)
        shift = peak + jnp.log2(sums)
        for begin in range(0, total, reach):
            rows = slice(begin, begin + reach)
            plan_ref[rows, :] = jnp.exp2(p_ref[rows, :] - shift).astype(jnp.bfloat16)

    mapped_ref[...] = jnp.dot(coords[...], plan_ref[...], preferred_element_type=jnp.float32)


def swap(value, count, step):
    return lax.ppermute(value, AXIS, [(source, source ^ step) for source in range(count)])


def chip_stages(count):
    high, stages = count.bit_length() - 1, []
    while high > 1:
        width = min(2, high - 1)
        stages.append((high - width, width))
        high -= width
    return stages


def gather_stage(parts, count, low, width):
    held = parts[0] if len(parts) == 1 else jnp.concatenate(parts, axis=0)
    return [held] + [swap(held, count, digit << low) for digit in range(1, 1 << width)]


def gather_chips(block, count):
    parts = [block[None]]
    for low, width in chip_stages(count):
        parts = gather_stage(parts, count, low, width)
    return parts


def gather_line(block, count):
    parts = [block[None]]
    for low, width in chip_stages(count)[:-1]:
        parts = gather_stage(parts, count, low, width)
    return jnp.concatenate(parts, axis=0)


def on_device(source_points, target_points, source_logw, target_logw, inverse_eps, count):
    feat, own_sources = source_points.shape
    own_targets = target_points.shape[1]
    extra_rows = own_sources // LANES
    pad = -(1 + extra_rows) % 16
    packed = jnp.concatenate(
        [
            target_points,
            target_logw[None, :],
            source_logw.reshape(extra_rows, LANES),
            jnp.zeros((pad, own_targets), target_points.dtype),
        ],
        axis=0,
    )
    f32, bf16 = jnp.float32, jnp.bfloat16
    total = count * own_targets
    small = total <= 4096
    width = LANES
    if small:
        width = 4 * LANES if source_points.shape[1] % (3 * LANES) == 0 else 2 * LANES
    vmem = pl.BlockSpec(memory_space=pltpu.VMEM)
    smem = pl.BlockSpec(memory_space=pltpu.SMEM)
    params = pltpu.CompilerParams(vmem_limit_bytes=(24 if small else 63) << 20)
    line = jax.ShapeDtypeStruct((1, total), f32)

    def call(kernel, operands, outs, scratch=(), scalars=1):
        return pl.pallas_call(
            kernel,
            out_shape=outs,
            in_specs=[smem] * scalars + [vmem] * (len(operands) - scalars),
            out_specs=[vmem] * len(outs),
            scratch_shapes=list(scratch),
            compiler_params=params,
        )(*operands)

    def staged_shape(parts):
        rows = sum(part.shape[0] for part in parts) * own_targets
        return jax.ShapeDtypeStruct((rows, DEPTH), bf16)

    def logw_line(parts):
        rows = [part[:, feat + 1 : feat + 1 + extra_rows] for part in parts]
        return jnp.concatenate(rows, axis=0).reshape(1, -1).astype(f32)

    packed, points = lax.optimization_barrier((packed, source_points))
    mine = gather_chips(packed, count)
    theirs = [swap(part, count, 1) for part in mine]
    parts, low = len(mine), chip_stages(count)[-1][0]
    ts = mine + theirs
    (taug_mine,) = call(
        functools.partial(part_kernel, feat),
        [inverse_eps, mine[0]],
        [staged_shape(mine[:1])],
    )
    (taug_theirs,) = call(
        functools.partial(part_kernel, feat),
        [inverse_eps, theirs[0]],
        [staged_shape(theirs[:1])],
    )
    (taug_rest,) = call(
        functools.partial(part_kernel, feat),
        [inverse_eps] + mine[1:],
        [staged_shape(mine[1:])],
    )
    xs = gather_line(points, count)
    logws = logw_line(mine[:1])
    rows = logws.shape[1]

    p_scratch = pltpu.VMEM((total, width), f32)
    scratch = [
        p_scratch,
        p_scratch if small else pltpu.VMEM((8, LANES), f32),
    ] + [pltpu.VMEM((total // 16, LANES), f32)] * 16
    xaug, taug, sums, logw, q = call(
        functools.partial(near_kernel, parts, feat),
        [inverse_eps, logws, xs, taug_mine, taug_rest, taug_theirs] + ts,
        [
            jax.ShapeDtypeStruct((DEPTH, rows), bf16),
            jax.ShapeDtypeStruct((total, DEPTH), bf16),
            line,
            line,
            line,
        ],
        scratch,
    )
    flips = [(core, digit) for digit in range(parts) for core in range(2)]

    def exchange(own):
        return [own] + [swap(own, count, core | (digit << low)) for core, digit in flips[1:]]

    g = logw
    for _ in range(ITERS - 1):
        sums, g = call(
            functools.partial(next_kernel, flips, parts),
            [logws, xaug, taug, g, q, logw] + exchange(sums),
            [line, line],
            [pltpu.VMEM((total, DEPTH), bf16)] + scratch,
            scalars=0,
        )
    mapped, potential = call(
        functools.partial(map_kernel, flips, parts, len(ts), feat),
        [xaug if small else xaug[:, :own_sources], taug, g, q, logw] + exchange(sums) + ts,
        [
            jax.ShapeDtypeStruct((feat, own_sources), f32),
            jax.ShapeDtypeStruct((1, own_targets), f32),
        ],
        [
            pltpu.VMEM((total, DEPTH), bf16),
            pltpu.VMEM((total, own_sources), f32),
            pltpu.VMEM((total, own_sources), bf16),
            pltpu.VMEM((feat, total), bf16),
        ],
        scalars=0,
    )
    return (mapped, potential.reshape(own_targets))


def solution(mesh):
    count = mesh.shape[AXIS]
    placed = (
        P(None, ("grp", "wide")),
        P(None, ("grp", "wide")),
        P(("grp", "wide")),
        P(("grp", "wide")),
        P(),
    )

    def body(*blocks):
        return on_device(*blocks, count)

    return jax.shard_map(
        body,
        mesh=mesh,
        in_specs=placed,
        out_specs=(P(None, ("grp", "wide")), P(("grp", "wide"))),
        check_vma=False,
    )
```

```python
import functools
import math

import jax
import jax.numpy as jnp
from jax import lax
from jax.experimental import pallas as pl
from jax.experimental.pallas import tpu as pltpu
from jax.sharding import PartitionSpec as P

ITERS = 2
AXIS = "wide"
LOG2E = math.log2(math.e)
LANES = 128
DEPTH = 256
SMALL_ROW = 2.0**-64
SMALL_COL = 2.0**-32
LARGE_COL = 2.0**100
FLOOR = -1e30


def three_terms(value):
    high = value.astype(jnp.bfloat16)
    rest = value - high.astype(jnp.float32)
    middle = rest.astype(jnp.bfloat16)
    low = (rest - middle.astype(jnp.float32)).astype(jnp.bfloat16)
    return high, middle, low


def pick_rows(shape, rows):
    index = lax.broadcasted_iota(jnp.int32, shape, 0)
    out = jnp.zeros(shape, jnp.float32)
    for place, row in enumerate(rows):
        out = jnp.where(index == place, row, out)
    return out


def stage_source(points, scale, xaug, at):
    feat, count = points.shape
    wide = points.astype(jnp.float32)
    shift = scale * jnp.sum(wide * wide, axis=0, keepdims=True)
    shift = shift.astype(jnp.bfloat16).astype(jnp.float32)
    xaug[0:feat, at] = pick_rows((feat, count), [1.0, 1.0, 1.0, -shift]).astype(jnp.bfloat16)
    for place, term in enumerate(three_terms(2.0 * scale * wide)):
        xaug[(place + 1) * feat : (place + 2) * feat, at] = term


def stage_sources(parts, scale, xaug, begin=0):
    for part in parts:
        count = part.shape[2]
        for block in range(part.shape[0]):
            stage_source(part[block], scale, xaug, slice(begin, begin + count))
            begin += count


def target_lines(part, block, scale, feat):
    wide = part[block, :feat, :].astype(jnp.float32)
    logw = part[block, feat : feat + 16, :].astype(jnp.float32)[0:1]
    return scale * jnp.sum(wide * wide, axis=0, keepdims=True), logw * LOG2E


def stage_targets(parts, scale, taug, begin, feat):
    for part in parts:
        for block in range(part.shape[0]):
            q, logw = target_lines(part, block, scale, feat)
            terms = [term.astype(jnp.float32) for term in three_terms(logw - q)]
            extras = pick_rows((feat, LANES), terms + [1.0])
            wide = part[block, :feat, :].astype(jnp.float32)
            turned = jnp.concatenate([extras, wide], axis=0).T
            lane = lax.broadcasted_iota(jnp.int32, turned.shape, 1)
            twice = jnp.where(lane < feat, pltpu.roll(turned, feat, 1), turned)
            taug[begin : begin + LANES, 0:LANES] = turned.astype(jnp.bfloat16)
            taug[begin : begin + LANES, LANES:DEPTH] = twice.astype(jnp.bfloat16)
            begin += LANES


def renew_targets(lines, flips, parts, g, q, logw, taug):
    total = lines[0].shape[1]
    size = total // (2 * parts)
    held = []
    for line, (core, digit) in zip(lines, flips):
        value = line[...]
        places = [(block ^ (core * parts)) ^ digit for block in range(2 * parts)]
        pieces = [value[:, place * size : (place + 1) * size] for place in places]
        held.append(jnp.concatenate(pieces, axis=1))
    peak = functools.reduce(jnp.maximum, held)
    added = functools.reduce(jnp.add, [jnp.exp2(value - peak) for value in held])
    potential = g - (peak + jnp.log2(added))
    g = potential + logw
    terms = [term.astype(jnp.float32) for term in three_terms(g - jnp.max(g) - q)]
    for begin in range(0, total, LANES):
        rows = slice(begin, begin + LANES)
        extras = pick_rows((8, LANES), [term[:, rows] for term in terms] + [1.0])
        taug[rows, 0:8] = extras.T.astype(jnp.bfloat16)
    return potential, g


def exponents(left, right):
    return jnp.dot(left, right, preferred_element_type=jnp.float32)


def spread_rows(taug, right, p_ref, beside):
    total, width = taug.shape[0], right.shape[1]
    reach = min(total, 512)
    sums = jnp.zeros((8, width), jnp.float32)
    for begin in range(0, total, reach):
        e = exponents(taug[begin : begin + reach, :], right)
        for inner in range(0, reach, LANES):
            rows = slice(begin + inner, begin + inner + LANES)
            beside(rows)
            p = jnp.exp2(e[inner : inner + LANES])
            p_ref[rows, :] = p
            sums = sums + jnp.sum(p.reshape(LANES // 8, 8, width), axis=0)
    return jnp.sum(sums, axis=0, keepdims=True)


def add_columns(p_ref, weight, col_refs, rows):
    width = weight.shape[1]
    added = p_ref[rows, 0:LANES] * weight[:, 0:LANES]
    for lane in range(LANES, width, LANES):
        added = added + p_ref[rows, lane : lane + LANES] * weight[:, lane : lane + LANES]
    col_ref, at = column_block(col_refs, rows)
    col_ref[at, :] += added


def column_block(col_refs, rows):
    size = col_refs[0].shape[0]
    place = rows.start // size
    return col_refs[place], slice(rows.start - place * size, rows.stop - place * size)


def tile_columns(tile, width):
    if isinstance(tile, int):
        return pl.ds(tile * width, width)
    return pl.ds(pl.multiple_of(tile * width, width), width)


def add_sources(xaug, logws, taug, p_refs, col_refs):
    total = taug.shape[0]
    width = p_refs[0].shape[1]
    tiles = xaug.shape[1] // width
    if p_refs[1].shape != p_refs[0].shape:
        p_refs = (p_refs[0], p_refs[0])

    def step(tile, slot, held):
        def beside(rows):
            if held is not None:
                add_columns(p_refs[1 - slot], held, col_refs, rows)

        at = tile_columns(tile, width)
        s = spread_rows(taug, xaug[:, at], p_refs[slot], beside)
        return s, jnp.exp2(logws[:, at] * LOG2E) / s

    if tiles == 3:
        least, weight = step(0, 0, None)
        for tile in range(1, tiles):
            s, weight = step(tile, tile % 2, weight)
            least = jnp.minimum(least, s)
        for begin in range(0, total, LANES):
            add_columns(p_refs[0], weight, col_refs, slice(begin, begin + LANES))
        return least

    def two_steps(pair, carry):
        least, weight = carry
        s1, weight1 = step(2 * pair + 1, 1, weight)
        s0, weight0 = step(2 * pair + 2, 0, weight1)
        return jnp.minimum(least, jnp.minimum(s0, s1)), weight0

    s, weight = step(0, 0, None)
    least, weight = lax.fori_loop(0, tiles // 2 - 1, two_steps, (s, weight))
    s, weight = step(tiles - 1, 1, weight)
    for begin in range(0, total, LANES):
        add_columns(p_refs[1], weight, col_refs, slice(begin, begin + LANES))
    return jnp.minimum(least, s)


def lane_totals(col_refs, out_ref):
    total = sum(col_ref.shape[0] for col_ref in col_refs)
    reach = min(total, 2048)
    ones = jnp.ones((16, 2 * LANES), jnp.bfloat16)
    sizes = col_refs[0].shape[0]
    for begin in range(0, total, reach):
        refs = col_refs[begin // sizes : (begin + reach) // sizes]
        high, middle, _ = three_terms(jnp.concatenate([col_ref[...] for col_ref in refs], axis=0))
        both = jnp.concatenate([high, middle], axis=1)
        added = lax.dot_general(
            ones, both, (((1,), (1,)), ((), ())), preferred_element_type=jnp.float32
        )
        out_ref[:, begin : begin + reach] = added[0:1]


def finish_sums(xaug, logws, taug, least, p_ref, col_refs, out_ref):
    total = taug.shape[0]
    lane_totals(col_refs, out_ref)
    cols = out_ref[...]
    out_ref[...] = jnp.log2(cols)
    fine = jnp.logical_and(
        jnp.min(least) >= SMALL_ROW,
        jnp.logical_and(jnp.min(cols) >= SMALL_COL, jnp.max(cols) <= LARGE_COL),
    )
    top_ref = p_ref.at[:, 0:LANES]

    @pl.when(jnp.logical_not(fine))
    def _():
        for col_ref in col_refs:
            col_ref[...] = jnp.zeros_like(col_ref)
        top_ref[...] = jnp.full_like(top_ref, FLOOR)

        def careful(tile, carry):
            at = tile_columns(tile, LANES)
            right = xaug[:, at]

            def block_rows(block):
                return pl.ds(pl.multiple_of(block * LANES, LANES), LANES)

            def highest(block, peak):
                e = exponents(taug[block_rows(block), :], right)
                return jnp.maximum(peak, jnp.max(e, axis=0, keepdims=True))

            peak = jnp.full((1, LANES), FLOOR, jnp.float32)
            peak = lax.fori_loop(0, total // LANES, highest, peak)

            def summed(block, s):
                e = exponents(taug[block_rows(block), :], right)
                return s + jnp.sum(jnp.exp2(e - peak), axis=0, keepdims=True)

            s = lax.fori_loop(0, total // LANES, summed, jnp.zeros((1, LANES), jnp.float32))
            shift = logws[:, at] * LOG2E - peak - jnp.log2(s)

            size = col_refs[0].shape[0]
            for place, col_ref in enumerate(col_refs):

                def collected(block, carry, place=place, col_ref=col_ref):
                    rows = block_rows(place * (size // LANES) + block)
                    term = exponents(taug[rows, :], right) + shift
                    old = top_ref[rows, :]
                    top = jnp.maximum(old, term)
                    here = block_rows(block)
                    col = col_ref[here, :] * jnp.exp2(old - top) + jnp.exp2(term - top)
                    col_ref[here, :] = col
                    top_ref[rows, :] = top
                    return carry

                lax.fori_loop(0, size // LANES, collected, 0)
            return carry

        lax.fori_loop(0, xaug.shape[1] // LANES, careful, 0)
        for begin in range(0, total, LANES):
            rows = slice(begin, begin + LANES)
            col_ref, at = column_block(col_refs, rows)
            tops = top_ref[rows, :].T
            top = jnp.max(tops, axis=0, keepdims=True)
            added = jnp.sum(col_ref[at, :].T * jnp.exp2(tops - top), axis=0, keepdims=True)
            out_ref[:, rows] = top + jnp.log2(added)


def part_kernel(feat, inverse, *refs):
    stage_targets(refs[:-1], inverse[0] * LOG2E, refs[-1], 0, feat)


def near_kernel(parts, feat, inverse, logws, xs, mine, rest, theirs, *refs):
    ts, refs = refs[: 2 * parts], refs[2 * parts :]
    xaug, taug, out_ref, g_ref, q_ref, p0, p1, *col_refs = refs
    scale = inverse[0] * LOG2E
    stage_sources([xs], scale, xaug)
    place = 0
    for part in ts:
        for block in range(part.shape[0]):
            at = slice(place * LANES, (place + 1) * LANES)
            q_ref[:, at], g_ref[:, at] = target_lines(part, block, scale, feat)
            place += 1
    begin = 0
    for part in (mine, rest, theirs):
        taug[begin : begin + part.shape[0], :] = part[...]
        begin += part.shape[0]
    stage_targets(ts[parts + 1 :], scale, taug, begin, feat)
    for col_ref in col_refs:
        col_ref[...] = jnp.zeros_like(col_ref)
    least = add_sources(xaug, logws, taug, (p0, p1), col_refs)
    finish_sums(xaug, logws, taug, least, p0, col_refs, out_ref)


def next_kernel(flips, parts, logws, xaug, old, g, q, logw, *refs):
    lines, refs = refs[: len(flips)], refs[len(flips) :]
    out_ref, g_ref, taug, p0, p1, *col_refs = refs
    taug[...] = old[...]
    g_ref[...] = renew_targets(lines, flips, parts, g[...], q[...], logw[...], taug)[1]
    for col_ref in col_refs:
        col_ref[...] = jnp.zeros_like(col_ref)
    least = add_sources(xaug, logws, taug, (p0, p1), col_refs)
    finish_sums(xaug, logws, taug, least, p0, col_refs, out_ref)


def map_kernel(flips, parts, n_t, feat, xaug, old, g, q, logw, *refs):
    lines, refs = refs[: len(flips)], refs[len(flips) :]
    ts = refs[:n_t]
    mapped_ref, pot_ref, taug, p_ref, plan_ref, coords = refs[n_t:]
    taug[...] = old[...]
    potential = renew_targets(lines, flips, parts, g[...], q[...], logw[...], taug)[0]
    pot_ref[...] = potential[:, :LANES] * (1.0 / LOG2E)
    place = 0
    for part in ts:
        for block in range(part.shape[0]):
            coords[:, place * LANES : (place + 1) * LANES] = part[block, :feat, :]
            place += 1
    total = taug.shape[0]
    right = xaug[:, : p_ref.shape[1]]
    s = spread_rows(taug, right, p_ref, lambda rows: None)
    weight = 1.0 / s
    for begin in range(0, total, LANES):
        rows = slice(begin, begin + LANES)
        plan_ref[rows, :] = (p_ref[rows, :] * weight).astype(jnp.bfloat16)

    @pl.when(jnp.logical_not(jnp.min(s) >= SMALL_ROW))
    def _():
        reach = min(total, 2048)
        peak = jnp.full(s.shape, FLOOR, jnp.float32)
        for begin in range(0, total, reach):
            rows = slice(begin, begin + reach)
            p_ref[rows, :] = exponents(taug[rows, :], right)
            peak = jnp.maximum(peak, jnp.max(p_ref[rows, :], axis=0, keepdims=True))
        sums = jnp.zeros(s.shape, jnp.float32)
        for begin in range(0, total, reach):
            rows = slice(begin, begin + reach)
            sums += jnp.sum(jnp.exp2(p_ref[rows, :] - peak), axis=0, keepdims=True)
        shift = peak + jnp.log2(sums)
        for begin in range(0, total, reach):
            rows = slice(begin, begin + reach)
            plan_ref[rows, :] = jnp.exp2(p_ref[rows, :] - shift).astype(jnp.bfloat16)

    mapped_ref[...] = jnp.dot(coords[...], plan_ref[...], preferred_element_type=jnp.float32)


def swap(value, count, step):
    return lax.ppermute(value, AXIS, [(source, source ^ step) for source in range(count)])


def chip_stages(count):
    high, stages = count.bit_length() - 1, []
    while high > 1:
        width = min(2, high - 1)
        stages.append((high - width, width))
        high -= width
    return stages


def gather_stage(parts, count, low, width):
    held = parts[0] if len(parts) == 1 else jnp.concatenate(parts, axis=0)
    return [held] + [swap(held, count, digit << low) for digit in range(1, 1 << width)]


def gather_chips(block, count):
    parts = [block[None]]
    for low, width in chip_stages(count):
        parts = gather_stage(parts, count, low, width)
    return parts


def gather_line(block, count):
    parts = [block[None]]
    for low, width in chip_stages(count)[:-1]:
        parts = gather_stage(parts, count, low, width)
    return jnp.concatenate(parts, axis=0)


def on_device(source_points, target_points, source_logw, target_logw, inverse_eps, count):
    feat, own_sources = source_points.shape
    own_targets = target_points.shape[1]
    extra_rows = own_sources // LANES
    pad = -(1 + extra_rows) % 16
    packed = jnp.concatenate(
        [
            target_points,
            target_logw[None, :],
            source_logw.reshape(extra_rows, LANES),
            jnp.zeros((pad, own_targets), target_points.dtype),
        ],
        axis=0,
    )
    f32, bf16 = jnp.float32, jnp.bfloat16
    total = count * own_targets
    small = total <= 4096
    width = 2 * LANES if small else LANES
    vmem = pl.BlockSpec(memory_space=pltpu.VMEM)
    smem = pl.BlockSpec(memory_space=pltpu.SMEM)
    params = pltpu.CompilerParams(vmem_limit_bytes=(24 if small else 63) << 20)
    line = jax.ShapeDtypeStruct((1, total), f32)

    def call(kernel, operands, outs, scratch=(), scalars=1):
        return pl.pallas_call(
            kernel,
            out_shape=outs,
            in_specs=[smem] * scalars + [vmem] * (len(operands) - scalars),
            out_specs=[vmem] * len(outs),
            scratch_shapes=list(scratch),
            compiler_params=params,
        )(*operands)

    def staged_shape(parts):
        rows = sum(part.shape[0] for part in parts) * own_targets
        return jax.ShapeDtypeStruct((rows, DEPTH), bf16)

    def logw_line(parts):
        rows = [part[:, feat + 1 : feat + 1 + extra_rows] for part in parts]
        return jnp.concatenate(rows, axis=0).reshape(1, -1).astype(f32)

    packed, points = lax.optimization_barrier((packed, source_points))
    mine = gather_chips(packed, count)
    theirs = [swap(part, count, 1) for part in mine]
    parts, low = len(mine), chip_stages(count)[-1][0]
    ts = mine + theirs
    (taug_mine,) = call(
        functools.partial(part_kernel, feat),
        [inverse_eps, mine[0]],
        [staged_shape(mine[:1])],
    )
    (taug_theirs,) = call(
        functools.partial(part_kernel, feat),
        [inverse_eps, theirs[0]],
        [staged_shape(theirs[:1])],
    )
    (taug_rest,) = call(
        functools.partial(part_kernel, feat),
        [inverse_eps] + mine[1:],
        [staged_shape(mine[1:])],
    )
    xs = gather_line(points, count)
    logws = logw_line(mine[:1])
    rows = logws.shape[1]

    p_scratch = pltpu.VMEM((total, width), f32)
    scratch = [
        p_scratch,
        p_scratch if small else pltpu.VMEM((8, LANES), f32),
    ] + [pltpu.VMEM((total // 16, LANES), f32)] * 16
    p_wide = pltpu.VMEM((total, 4 * LANES), f32)
    near_scratch = [p_wide, p_wide] + scratch[2:] if rows == 12 * LANES and small else scratch
    xaug, taug, sums, logw, q = call(
        functools.partial(near_kernel, parts, feat),
        [inverse_eps, logws, xs, taug_mine, taug_rest, taug_theirs] + ts,
        [
            jax.ShapeDtypeStruct((DEPTH, rows), bf16),
            jax.ShapeDtypeStruct((total, DEPTH), bf16),
            line,
            line,
            line,
        ],
        near_scratch,
    )
    flips = [(core, digit) for digit in range(parts) for core in range(2)]

    def exchange(own):
        return [own] + [swap(own, count, core | (digit << low)) for core, digit in flips[1:]]

    g = logw
    for _ in range(ITERS - 1):
        sums, g = call(
            functools.partial(next_kernel, flips, parts),
            [logws, xaug, taug, g, q, logw] + exchange(sums),
            [line, line],
            [pltpu.VMEM((total, DEPTH), bf16)] + scratch,
            scalars=0,
        )
    mapped, potential = call(
        functools.partial(map_kernel, flips, parts, len(ts), feat),
        [xaug if small else xaug[:, :own_sources], taug, g, q, logw] + exchange(sums) + ts,
        [
            jax.ShapeDtypeStruct((feat, own_sources), f32),
            jax.ShapeDtypeStruct((1, own_targets), f32),
        ],
        [
            pltpu.VMEM((total, DEPTH), bf16),
            pltpu.VMEM((total, own_sources), f32),
            pltpu.VMEM((total, own_sources), bf16),
            pltpu.VMEM((feat, total), bf16),
        ],
        scalars=0,
    )
    return (mapped, potential.reshape(own_targets))


def solution(mesh):
    count = mesh.shape[AXIS]
    placed = (
        P(None, ("grp", "wide")),
        P(None, ("grp", "wide")),
        P(("grp", "wide")),
        P(("grp", "wide")),
        P(),
    )

    def body(*blocks):
        return on_device(*blocks, count)

    return jax.shard_map(
        body,
        mesh=mesh,
        in_specs=placed,
        out_specs=(P(None, ("grp", "wide")), P(("grp", "wide"))),
        check_vma=False,
    )
```
